128 devices in a mesh: section: 4 (over z_hi, core), dp: 32 (over z_lo, y, x).
Axes of the slice: x: 4, y: 4, z: 4 (z_hi: 2, z_lo: 2; z = z_hi * 2 + z_lo), core: 2. Of those that a mesh axis runs over, the one named last changes fastest.
Arguments:
- node_states: bfloat16 [4096, 128], P('dp'), may hold values from -6 to 6
- edge_features: bfloat16 [16, 32768], P(None, 'dp'), may hold values from -6 to 6
- edge_source: int32 [32768], P('dp'), may hold values from 0 to 31, as said below
- edge_target: int32 [32768], P('dp'), may hold values from 0 to 31, as said below
- edge_live: int32 [32768], P('dp'), may hold values 0 or 1
- w_edge_in: bfloat16 [16, 128], replicated, may hold values from -1.5 to 1.5
- b_edge_in: float32 [128], replicated, may hold values from -3 to 3
- w_edge_out: bfloat16 [128, 16384], replicated, may hold values from -0.0625 to 0.0625
- b_edge_out: float32 [16384], replicated, may hold values from -0.3 to 0.3
- w_input: bfloat16 [128, 384], replicated, may hold values from -0.5 to 0.5
- w_hidden: bfloat16 [128, 384], replicated, may hold values from -0.5 to 0.5
- b_input: float32 [384], replicated, may hold values from -3 to 3
- b_hidden: float32 [384], replicated, may hold values from -3 to 3
- cotangent: float32 [4096, 128], P('dp'), may hold values from -6 to 6
Outputs:
- final_states: float32 [4096, 128], P(('dp', 'section'))
- grad_states: float32 [4096, 128], P(('dp', 'section'))
- grad_w_edge_in: float32 [16, 128], replicated
- grad_b_edge_in: float32 [128], replicated
- grad_w_edge_out: float32 [128, 16384], replicated
- grad_b_edge_out: float32 [16384], replicated
- grad_w_input: float32 [128, 384], replicated
- grad_w_hidden: float32 [128, 384], replicated
- grad_b_input: float32 [384], replicated
- grad_b_hidden: float32 [384], replicated
The draws below stay inside these ranges and needn't reach their ends.
Inputs may be any that keep to these rules, and one draw needn't show every extreme that they name: `edge_source`: an edge's source and target are two different atom slots of the same molecule, counted from the start of the edge's node block; the edge slots of a molecule are 256 consecutive slots, molecule m of a block owning atom slots m * 32 to m * 32 + 31. `edge_target`: as for edge_source.
All inputs are finite; a program needn't handle non-finite values. No bound on the sum of `edge_live` on one device may be relied on, other than what follows from the above.
Results may differ from the reference program's by a relative error of at most 0.028.
The reference program's roundings to bfloat16 on the way count: a program that leaves them out, or rounds other values in their place, can miss the bound.
Values may be sent and summed in bfloat16 or wider, within the bound.
No kernel may reach another device: no remote copies, remote signals or barrier semaphores. Data moves between devices by JAX's collectives and lax.ppermute only.
A program may use at most 128 MiB of HBM per device.

```python
import jax
import jax.numpy as jnp
from jax import lax

H = 128
EH = 128
EIN = 16
ATOMS = 32
EPM = 256
MOLS = 1
MB = 4
NODES = 4096
EDGES = 32768
N_DP = 32


def edge_pairs(key):
    first_key, second_key = jax.random.split(key)
    position = jnp.arange(EDGES, dtype=jnp.int32) % (MOLS * EPM)
    molecule = position // EPM
    atom_from = jax.random.randint(first_key, (EDGES,), 0, ATOMS, dtype=jnp.int32)
    offset = jax.random.randint(second_key, (EDGES,), 1, ATOMS, dtype=jnp.int32)
    return (molecule * ATOMS + atom_from, molecule * ATOMS + (atom_from + offset) % ATOMS)


def draw_edge_source(key, part):
    return edge_pairs(key)[0]


def draw_edge_target(key, part):
    return edge_pairs(key)[1]


def place_ends(entries, stream_key, low, top_value):
    spot = [jax.random.randint(jax.random.fold_in(stream_key, axis), (), 0, length) for axis, length in enumerate(entries.shape)]
    widest = entries.shape.index(max(entries.shape))
    beside = spot[:widest] + [(spot[widest] + 1) % entries.shape[widest]] + spot[widest + 1:]
    return entries.at[tuple(spot)].set(low).at[tuple(beside)].set(top_value)


def block_scale(stream_key, shape, pieces, low, high):
    def one(axis_at, parts):
        draws = jax.random.uniform(jax.random.fold_in(jax.random.fold_in(stream_key, 6), axis_at), (parts,), jnp.float32, low / len(pieces), high / len(pieces))
        return jnp.repeat(jnp.exp(draws), shape[axis_at] // parts).reshape((-1,) + (1,) * (len(shape) - axis_at - 1))

    level = one(*pieces[0])
    for cut in pieces[1:]:
        level = level * one(*cut)
    return level


def normal_values(rng, dims, deviation, reach, cuts=(), kind=jnp.bfloat16):
    drawn = deviation * jax.random.normal(rng, dims, jnp.float32)
    if cuts:
        drawn = drawn * block_scale(rng, dims, cuts, -0.22, 0.18)
    return jnp.clip(drawn, -reach, reach).astype(kind)


def setup_inputs(seed: int = 0) -> dict:
    streams_of = jax.random.split(jax.random.key(seed), 15)
    return {
        "node_states": normal_values(streams_of[0], (NODES, H), 1.0, 6.0, ((0, 32),)),
        "edge_features": normal_values(streams_of[1], (EIN, EDGES), 1.0, 6.0, ((1, 32),)),
        "edge_source": draw_edge_source(jax.random.fold_in(streams_of[14], 71), 0),
        "edge_target": draw_edge_target(jax.random.fold_in(streams_of[14], 71), 0),
        "edge_live": place_ends((jax.random.randint(streams_of[4], (EDGES,), 0, 4) < 3).astype(jnp.int32), jax.random.fold_in(streams_of[4], 1), 0, 1),
        "w_edge_in": normal_values(streams_of[5], (EIN, EH), EIN ** -0.5, 1.5),
        "b_edge_in": normal_values(streams_of[6], (EH,), 0.5, 3.0, (), jnp.float32),
        "w_edge_out": normal_values(streams_of[7], (EH, H * H), (EH * H // 2) ** -0.5, 0.0625),
        "b_edge_out": normal_values(streams_of[8], (H * H,), 0.05, 0.3, (), jnp.float32),
        "w_input": normal_values(streams_of[9], (H, 3 * H), H ** -0.5, 0.5),
        "w_hidden": normal_values(streams_of[10], (H, 3 * H), H ** -0.5, 0.5),
        "b_input": normal_values(streams_of[11], (3 * H,), 0.5, 3.0, (), jnp.float32),
        "b_hidden": normal_values(streams_of[12], (3 * H,), 0.5, 3.0, (), jnp.float32),
        "cotangent": normal_values(streams_of[13], (NODES, H), 1.0, 6.0, ((0, 32),), jnp.float32),
    }


@jax.custom_vjp
def low(v):
    return lax.optimization_barrier(v.astype(jnp.bfloat16)).astype(jnp.float32)

@jax.custom_vjp
def low_back(v):
    return v

def low_keep(v):
    return (low(v), None)

def low_pass(kept, grad):
    return (grad,)

def back_keep(v):
    return (v, None)

def back_low(kept, grad):
    return (low(grad),)
low.defvjp(low_keep, low_pass)
low_back.defvjp(back_keep, back_low)

def product(left, right):
    return jnp.dot(left, right, precision=lax.Precision.HIGHEST)

def messages_all(states, features, source, target, live_mask, w_edge_in, b_edge_in, w_edge_out, b_edge_out):
    hidden_size = states.shape[-1]

    def one_block(operands):
        block_feat, block_src, block_tgt, block_live, block_states = operands
        edge_pre = product(block_feat, w_edge_in) + b_edge_in
        edge_hidden = low(jax.nn.silu(edge_pre))
        edge_mats = low_back(low(product(edge_hidden, w_edge_out) + b_edge_out))
        mat_cube = edge_mats.reshape(edge_mats.shape[0], hidden_size, hidden_size)
        picked = jnp.take(block_states, block_src, axis=0)
        edge_terms = jnp.einsum('eij,ej->ei', mat_cube, picked, precision=lax.Precision.HIGHEST) * block_live[:, None]
        return jax.ops.segment_sum(edge_terms, block_tgt, num_segments=block_states.shape[0])
    summed = lax.map(jax.checkpoint(one_block), (features, source, target, live_mask, states))
    return low_back(low(summed))

def gru_step(message, states, w_input, w_hidden, b_input, b_hidden):
    hidden_size = states.shape[-1]
    from_msg = low_back(product(message, w_input) + b_input)
    from_state = low_back(product(states, w_hidden) + b_hidden)
    reset_gate = jax.nn.sigmoid(from_msg[:, :hidden_size] + from_state[:, :hidden_size])
    update_gate = jax.nn.sigmoid(from_msg[:, hidden_size:2 * hidden_size] + from_state[:, hidden_size:2 * hidden_size])
    candidate = jnp.tanh(from_msg[:, 2 * hidden_size:] + reset_gate * from_state[:, 2 * hidden_size:])
    return (1.0 - update_gate) * candidate + update_gate * states

def reference(node_states, edge_features, edge_source, edge_target, edge_live, w_edge_in, b_edge_in, w_edge_out, b_edge_out, w_input, w_hidden, b_input, b_hidden, cotangent):
    blocks = N_DP * MB
    node_rows = MOLS * ATOMS
    edge_rows = MOLS * EPM
    hidden_size = node_states.shape[1]
    features = edge_features.astype(jnp.float32).T.reshape(blocks, edge_rows, edge_features.shape[0])
    source = edge_source.reshape(blocks, edge_rows)
    target = edge_target.reshape(blocks, edge_rows)
    live_mask = edge_live.astype(jnp.float32).reshape(blocks, edge_rows)

    def forward(states, w_ein, b_ein, w_eout, b_eout, w_in, w_hid, b_in, b_hid):

        def mpnn_layer(current):
            summed = messages_all(current.reshape(blocks, node_rows, hidden_size), features, source, target, live_mask, w_ein, b_ein, w_eout, b_eout)
            return gru_step(summed.reshape(blocks * node_rows, hidden_size), current, w_in, w_hid, b_in, b_hid)
        layer_one = low(mpnn_layer(states))
        return mpnn_layer(layer_one)
    primals = (node_states.astype(jnp.float32), w_edge_in.astype(jnp.float32), b_edge_in, w_edge_out.astype(jnp.float32), b_edge_out, w_input.astype(jnp.float32), w_hidden.astype(jnp.float32), b_input, b_hidden)
    final_states, pullback = jax.vjp(forward, *primals)
    gradients = pullback(cotangent)
    return (final_states, gradients[0], gradients[1], gradients[2], gradients[3], gradients[4], gradients[5], gradients[6], gradients[7], gradients[8])
```

```python
import functools

import jax
import jax.numpy as jnp
from jax import lax
from jax.experimental import pallas as pl
from jax.experimental.pallas import tpu as pltpu
from jax.sharding import Mesh
from jax.sharding import PartitionSpec as P

H = 128
ATOMS = 32
EPM = 256
MB = 4
NODES = MB * ATOMS
PAIRS = ATOMS * ATOMS
OWN = H // MB
GAP = 129
ROWS = 144
SMALL = 8
GROUP = 32
BF = jnp.bfloat16
F32 = jnp.float32


def nn(left, right):
    return jnp.dot(left, right, preferred_element_type=F32)


def nt(left, right):
    return lax.dot_general(left, right, (((1,), (1,)), ((), ())), preferred_element_type=F32)


def tn(left, right):
    return lax.dot_general(left, right, (((0,), (0,)), ((), ())), preferred_element_type=F32)


def halves(value):
    high = value.astype(BF)
    return high, (value - high.astype(F32)).astype(BF)


def fine(dot, left, right):
    lh, ll = halves(left)
    rh, rl = halves(right)
    return dot(lh, rh) + (dot(lh, rl) + dot(ll, rh))


def fine_left(dot, left, right):
    lh, ll = halves(left)
    return dot(lh, right) + dot(ll, right)


def fine_right(dot, left, right):
    rh, rl = halves(right)
    return dot(left, rh) + dot(left, rl)


def sigmoid(value):
    return 0.5 * jnp.tanh(0.5 * value) + 0.5


def gate_forward(message, states, w_input, w_hidden, b_input, b_hidden):
    from_msg = nn(message, w_input) + b_input
    from_state = nn(states, w_hidden) + b_hidden
    reset = sigmoid(from_msg[:, :H] + from_state[:, :H])
    update = sigmoid(from_msg[:, H : 2 * H] + from_state[:, H : 2 * H])
    state_cand = from_state[:, 2 * H :]
    candidate = jnp.tanh(from_msg[:, 2 * H :] + reset * state_cand)
    renewed = (1.0 - update) * candidate + update * states.astype(F32)
    return reset, update, candidate, state_cand, renewed


def gate_backward(grad, states, parts, w_input, w_hidden):
    reset, update, candidate, state_cand = parts
    act = grad * (1.0 - update) * (1.0 - candidate * candidate)
    d_reset = act * state_cand * reset * (1.0 - reset)
    d_update = grad * (states.astype(F32) - candidate) * update * (1.0 - update)
    d_in = jnp.concatenate([d_reset, d_update, act], axis=1).astype(BF)
    d_hid = jnp.concatenate([d_reset, d_update, act * reset], axis=1).astype(BF)
    g_msg = nt(d_in, w_input).astype(BF)
    grad_states = grad * update + nt(d_hid, w_hidden)
    return d_in, d_hid, g_msg, grad_states


def edge_front(features, w_edge_in, b_edge_in):
    return tn(features, w_edge_in) + b_edge_in


def local_kernel(
    sect_ref,
    states_ref,
    feat_ref,
    ends_ref,
    w_ein_ref,
    b_ein_ref,
    w_hbm,
    b_mat_ref,
    w_in_ref,
    w_hid_ref,
    b_in_ref,
    b_hid_ref,
    cot_ref,
    send_ref,
    final_ref,
    base_ref,
    grad_t_ref,
    pairs_out_ref,
    w_ref,
    u_one,
    u_two,
    d_all,
    d_own,
    pair_h,
    rows_scr,
    small_scr,
    q_scr,
    sems,
):
    sect = sect_ref[0]
    chunk = 2048

    def w_copy(at):
        cols = pl.ds(at * chunk, chunk)
        return pltpu.make_async_copy(w_hbm.at[:, cols], w_ref.at[:, cols], sems.at[at])

    for at in range(8):
        w_copy(at).start()

    states0 = states_ref[...]
    w_ein = w_ein_ref[...]
    b_ein = b_ein_ref[...]
    b_mat = b_mat_ref[...]
    source = ends_ref[0]
    target = ends_ref[1]
    live = ends_ref[2]
    pair = jnp.where(live > 0, source * ATOMS + target, -1)

    slot = lax.broadcasted_iota(jnp.int32, (PAIRS, H), 0)
    for mol in range(MB):
        pre = edge_front(feat_ref[:, mol * EPM : (mol + 1) * EPM], w_ein, b_ein)
        hidden = (pre * sigmoid(pre)).astype(BF)
        hot = jnp.concatenate(
            [
                jnp.where(slot == pair[2 * mol + part : 2 * mol + part + 1, :], 1.0, 0.0).astype(BF)
                for part in range(2)
            ],
            axis=1,
        )
        pair_h[mol * PAIRS : (mol + 1) * PAIRS, :] = nn(hot, hidden).astype(BF)

    node = lax.broadcasted_iota(jnp.int32, (NODES, H), 0)
    hot_t, hot_s = [], []
    for row in range(8):
        shift = (row // 2) * ATOMS
        keep = live[row : row + 1, :] > 0
        t_at = jnp.where(keep, target[row : row + 1, :] + shift, -1)
        s_at = source[row : row + 1, :] + shift
        hot_t.append(jnp.where(node == t_at, 1.0, 0.0).astype(BF))
        hot_s.append(jnp.where(node == s_at, 1.0, 0.0).astype(BF))
    hot_t = jnp.concatenate(hot_t, axis=1)
    hot_s = jnp.concatenate(hot_s, axis=1)
    adj = nt(hot_t, hot_s).astype(BF)
    adj_t = nt(hot_s, hot_t).astype(BF)

    def spread(states, u_ref, wait):
        def step(at):
            base = pl.multiple_of(at * 4 * H, 4 * H)
            four = [w_ref[:, pl.ds(base + q * H, H)] for q in range(4)]
            out = nt(states, jnp.concatenate(four, axis=0))
            for q in range(4):
                u_ref[pl.ds(at * 4 + q, NODES, stride=GAP), :] = out[:, q * H : (q + 1) * H]

        if wait:
            for at in range(8):
                w_copy(at).wait()
                for inner in range(4):
                    step(at * 4 + inner)
        else:

            def body(at, carry):
                step(at)
                return carry

            lax.fori_loop(0, 32, body, 0, unroll=8)

    def u_rows(u_ref, at):
        return u_ref[pl.ds(at * GAP, H), :].astype(BF)

    def gather(states, u_ref):
        side = fine_right(nt, states, b_mat)
        extra = fine_right(nn, adj, side)
        parts = []
        for mol in range(MB):

            def body(at, total, mol=mol):
                first = mol * ATOMS + at * 4
                left = jnp.concatenate(
                    [
                        pair_h[pl.ds(pl.multiple_of((first + q) * ATOMS, ATOMS), ATOMS), :]
                        for q in range(4)
                    ],
                    axis=1,
                )
                right = jnp.concatenate([u_rows(u_ref, first + q) for q in range(4)], axis=1)
                return total + nt(left, right)

            parts.append(lax.fori_loop(0, 8, body, jnp.zeros((ATOMS, H), F32), unroll=True))
        return (jnp.concatenate(parts, axis=0) + extra).astype(BF)

    w_in = w_in_ref[...]
    w_hid = w_hid_ref[...]
    b_in = b_in_ref[...]
    b_hid = b_hid_ref[...]

    spread(states0, u_one, True)
    msg_one = gather(states0, u_one)
    *parts_one, renewed = gate_forward(msg_one, states0, w_in, w_hid, b_in, b_hid)
    states1 = renewed.astype(BF)
    spread(states1, u_two, False)
    msg_two = gather(states1, u_two)
    *parts_two, final = gate_forward(msg_two, states1, w_in, w_hid, b_in, b_hid)
    own_rows = pl.ds(pl.multiple_of(sect * ATOMS, ATOMS), ATOMS)
    rows_scr[...] = final
    final_ref[...] = rows_scr[own_rows, :]

    d_in2, d_hid2, g_two, back_one = gate_backward(cot_ref[...], states1, parts_two, w_in, w_hid)
    g_two_t = g_two.astype(F32).T.astype(BF)

    for mol in range(MB):
        left = g_two_t[:, mol * ATOMS : (mol + 1) * ATOMS]

        def body(at, carry, mol=mol, left=left):
            first = mol * ATOMS + at * 4
            right = jnp.concatenate(
                [
                    pair_h[pl.ds(pl.multiple_of((first + q) * ATOMS, ATOMS), ATOMS), :]
                    for q in range(4)
                ],
                axis=1,
            )
            out = nn(left, right)
            for q in range(4):
                d_all[pl.ds(first + q, H, stride=GAP), :] = out[:, q * H : (q + 1) * H]
            return carry

        lax.fori_loop(0, 8, body, 0, unroll=True)

    def back_body(at, total):
        base = pl.multiple_of(at * 4 * H, 4 * H)
        left = jnp.concatenate(
            [d_all[pl.ds((at * 4 + q) * GAP, NODES), :].astype(BF) for q in range(4)], axis=1
        )
        right = jnp.concatenate([w_ref[:, pl.ds(base + q * H, H)] for q in range(4)], axis=0)
        return total + nn(left, right)

    back_msg = lax.fori_loop(0, 32, back_body, jnp.zeros((NODES, H), F32), unroll=8)
    share = nn(adj_t, g_two)
    grad_one = back_one + back_msg + fine(nn, share, b_mat)

    d_in1, d_hid1, g_one, back_zero = gate_backward(grad_one, states0, parts_one, w_in, w_hid)
    rows_scr[...] = g_one.astype(F32).T
    g_one_t = rows_scr[...].astype(BF)
    g_one_own = rows_scr[own_rows, :].astype(BF)

    for mol in range(MB):
        left = g_one_own[:, mol * ATOMS : (mol + 1) * ATOMS]

        def body(at, carry, mol=mol, left=left):
            first = mol * ATOMS + at * 4
            right = jnp.concatenate(
                [
                    pair_h[pl.ds(pl.multiple_of((first + q) * ATOMS, ATOMS), ATOMS), :]
                    for q in range(4)
                ],
                axis=1,
            )
            out = nn(left, right)
            for q in range(4):
                d_own[pl.ds(first + q, OWN, stride=GAP), :] = out[:, q * H : (q + 1) * H]
            return carry

        lax.fori_loop(0, 8, body, 0, unroll=True)

    both_t = jnp.concatenate([states0.astype(F32).T, states1.astype(F32).T], axis=1).astype(BF)

    def own_body(at, carry):
        right = jnp.concatenate(
            [
                d_own[pl.ds(at * GAP, NODES), :].astype(BF),
                d_all[pl.ds((sect * OWN + at) * GAP, NODES), :].astype(BF),
            ],
            axis=0,
        )
        send_ref[at, 0:H, :] = nn(both_t, right).astype(BF)
        return carry

    lax.fori_loop(0, OWN, own_body, 0, unroll=8)

    rows_scr[...] = g_one.astype(F32)
    g1 = rows_scr[own_rows, :].astype(BF)
    rows_scr[...] = g_two.astype(F32)
    g2 = rows_scr[own_rows, :].astype(BF)
    g_both = jnp.concatenate([g1, g2], axis=1)

    def q_body(at, carry):
        first = sect * ATOMS + at * 2
        right = jnp.concatenate(
            [
                jnp.concatenate([u_rows(u_one, first + q), u_rows(u_two, first + q)], axis=0)
                for q in range(2)
            ],
            axis=1,
        )
        out = nn(g_both, right).astype(BF)
        for q in range(2):
            q_scr[pl.ds(pl.multiple_of((at * 2 + q) * ATOMS, ATOMS), ATOMS), :] = out[
                :, q * H : (q + 1) * H
            ]
        return carry

    lax.fori_loop(0, 16, q_body, 0, unroll=8)
    own_cols = pl.ds(pl.multiple_of(sect * EPM, EPM), EPM)
    feat_own = feat_ref[:, own_cols]
    pre_own = edge_front(feat_own, w_ein, b_ein)
    sig = sigmoid(pre_own)
    slope = sig * (1.0 + pre_own * (1.0 - sig))
    rows_scr[0:8, :] = pair.astype(F32)
    pair_own = rows_scr[pl.ds(sect * 2, 2), :].astype(jnp.int32)
    hot = jnp.concatenate(
        [jnp.where(slot == pair_own[part : part + 1, :], 1.0, 0.0).astype(BF) for part in range(2)],
        axis=1,
    )
    g_pre = tn(hot, q_scr[...]) * slope

    adj_f = adj.astype(F32)
    del adj_f
    g_share_t = nn(g_one_t, adj), nn(g_two_t, adj)
    grad_b_out = fine_left(nn, g_share_t[0], states0) + fine_left(nn, g_share_t[1], states1)
    rows_scr[...] = grad_b_out
    small_scr[0:32, :] = rows_scr[own_rows, :]
    both_rows = jnp.concatenate(
        [msg_one.astype(F32).T, msg_two.astype(F32).T], axis=1
    )
    d_in_both = jnp.concatenate([d_in1, d_in2], axis=0)
    d_hid_both = jnp.concatenate([d_hid1, d_hid2], axis=0)
    for at, (rows_t, d_both) in enumerate(
        ((both_rows, d_in_both), (both_t.astype(F32), d_hid_both))
    ):
        rows_scr[...] = rows_t[:, :H]
        first = rows_scr[own_rows, :]
        rows_scr[...] = rows_t[:, H:]
        left = jnp.concatenate([first, rows_scr[own_rows, :]], axis=1).astype(BF)
        out = nn(left, d_both)
        for part in range(3):
            row = 32 + at * 96 + part * 32
            small_scr[row : row + 32, :] = out[:, part * H : (part + 1) * H]
    small_scr[224:240, :] = fine_right(nn, feat_own, g_pre)
    small_scr[240:256, :] = jnp.zeros((16, H), F32)
    small_scr[240:241, :] = jnp.sum(g_pre, axis=0, keepdims=True)
    for at, pair_d in enumerate(((d_in1, d_in2), (d_hid1, d_hid2))):
        for part in range(3):
            cols = slice(part * H, (part + 1) * H)
            rows_scr[...] = pair_d[0][:, cols].astype(F32) + pair_d[1][:, cols].astype(F32)
            row = 241 + at * 3 + part
            small_scr[row : row + 1, :] = jnp.sum(rows_scr[own_rows, :], axis=0, keepdims=True)
    for at in range(GROUP):
        high, low = halves(small_scr[at * SMALL : (at + 1) * SMALL, :])
        send_ref[at, H:ROWS, :] = jnp.concatenate([high.astype(F32), low.astype(F32)], axis=0).astype(BF)

    rows_scr[...] = back_zero + fine(nn, nn(adj_t, g_one), b_mat)
    base_ref[...] = rows_scr[own_rows, :]
    grad_t_ref[...] = g_one_t
    pairs_out_ref[...] = pair_h[pl.ds(pl.multiple_of(sect * PAIRS, PAIRS), PAIRS), :]


def sum_kernel(got_ref, out_ref):
    def body(at, total):
        return total + got_ref[at].astype(F32)

    total = lax.fori_loop(1, GROUP, body, got_ref[0].astype(F32), unroll=True)
    small = total[H : H + SMALL] + total[H + SMALL : ROWS]
    high, low = halves(small)
    piece = jnp.concatenate([total[:H].T, high.astype(F32), low.astype(F32)], axis=0).astype(BF)

    def put(at, carry):
        out_ref[at] = piece
        return carry

    lax.fori_loop(0, 2 * GROUP, put, 0, unroll=8)


def states_kernel(sect_ref, base_ref, grad_t_ref, pairs_ref, w_ref, out_ref, d_all, rows_scr):
    sect = sect_ref[0]
    rows_scr[...] = grad_t_ref[...].astype(F32).T
    own = rows_scr[pl.ds(pl.multiple_of(sect * ATOMS, ATOMS), ATOMS), :]
    left = own.T.astype(BF)
    gap = ATOMS + 1

    def body(at, carry):
        right = jnp.concatenate(
            [
                pairs_ref[pl.ds(pl.multiple_of((at * 4 + q) * ATOMS, ATOMS), ATOMS), :]
                for q in range(4)
            ],
            axis=1,
        )
        out = nn(left, right)
        for q in range(4):
            d_all[pl.ds(at * 4 + q, H, stride=gap), :] = out[:, q * H : (q + 1) * H]
        return carry

    lax.fori_loop(0, 8, body, 0, unroll=True)

    def back_body(at, total):
        base = pl.multiple_of(at * 4 * H, 4 * H)
        left = jnp.concatenate(
            [d_all[pl.ds((at * 4 + q) * gap, ATOMS), :].astype(BF) for q in range(4)], axis=1
        )
        right = jnp.concatenate([w_ref[:, pl.ds(base + q * H, H)] for q in range(4)], axis=0)
        return total + nn(left, right)

    out_ref[...] = lax.fori_loop(0, 32, back_body, base_ref[...], unroll=8)


def place_kernel(count, core_ref, got_ref, out_hbm, stage, sems):
    core = core_ref[0]
    steps = [(half, row) for half in range(2) for row in range(8)]

    def copy(at):
        half, row = steps[at]
        section = half * 2 + core
        cols = pl.ds(pl.multiple_of(section * GROUP * H, GROUP * H), GROUP * H)
        return pltpu.make_async_copy(
            stage.at[at % 4], out_hbm.at[pl.ds(row * 16, 16), cols], sems.at[at % 4]
        )

    for at, (half, row) in enumerate(steps):
        if at >= 4:
            copy(at - 4).wait()
        for dev in range(GROUP):
            stage[at % 4, :, dev * H : (dev + 1) * H] = got_ref[
                half * GROUP + dev, row * 16 : (row + 1) * 16, :
            ].astype(F32)
        copy(at).start()
    for at in range(len(steps) - 4, len(steps)):
        copy(at).wait()


def first_kernel(core_ref, got_ref, out_hbm, stage, sems):
    place_kernel(2, core_ref, got_ref, out_hbm, stage, sems)


def second_kernel(
    core_ref, other_ref, mine_ref, far_ref, half_hbm, out_hbm, gb_ref, gi_ref, gh_ref, misc_ref, small, stage, sems
):
    del half_hbm
    place_kernel(2, other_ref, far_ref, out_hbm, stage, sems)
    for which, ref in ((core_ref[0], mine_ref), (other_ref[0], far_ref)):
        for half in range(2):
            base = (half * 2 + which) * (GROUP * SMALL)
            for dev in range(GROUP):
                both = ref[half * GROUP + dev, H:ROWS, :].astype(F32)
                at = pl.multiple_of(base + dev * SMALL, SMALL)
                small[pl.ds(at, SMALL), :] = both[:SMALL] + both[SMALL:]
    misc = jnp.zeros((32, H), F32)
    for sect in range(MB):
        base = sect * GROUP * SMALL
        rows = slice(sect * 32, (sect + 1) * 32)
        gb_ref[rows, :] = small[base : base + 32, :]
        for part in range(3):
            cols = slice(part * H, (part + 1) * H)
            row = base + 32 + part * 32
            gi_ref[rows, cols] = small[row : row + 32, :]
            gh_ref[rows, cols] = small[row + 96 : row + 128, :]
        misc = misc + small[base + 224 : base + 256, :]
    misc_ref[...] = misc


def local(
    node_states,
    edge_features,
    edge_source,
    edge_target,
    edge_live,
    w_edge_in,
    b_edge_in,
    w_edge_out,
    b_edge_out,
    w_input,
    w_hidden,
    b_input,
    b_hidden,
    cotangent,
):
    vmem = pl.BlockSpec(memory_space=pltpu.VMEM)
    smem = pl.BlockSpec(memory_space=pltpu.SMEM)
    hbm = pl.BlockSpec(memory_space=pl.ANY)
    shape = jax.ShapeDtypeStruct
    limit = 60 * 2**20
    core = lax.axis_index("core").astype(jnp.int32)
    sect = (lax.axis_index("zh") * 2 + core).astype(jnp.int32)
    sect = sect.reshape(1)
    mine = core.reshape(1)
    other = 1 - mine
    ends = jnp.stack([edge_source, edge_target, edge_live]).reshape(3, 8, 128)

    send, final, base, grad_t, pairs = pl.pallas_call(
        local_kernel,
        out_shape=(
            shape((GROUP, ROWS, H), BF),
            shape((ATOMS, H), F32),
            shape((ATOMS, H), F32),
            shape((H, NODES), BF),
            shape((PAIRS, H), BF),
        ),
        in_specs=[smem] + [vmem] * 5 + [hbm] + [vmem] * 6,
        out_specs=(vmem,) * 5,
        scratch_shapes=[
            pltpu.VMEM((H, H * H), BF),
            pltpu.VMEM((NODES * GAP, H), F32),
            pltpu.VMEM((NODES * GAP, H), F32),
            pltpu.VMEM((H * GAP, H), F32),
            pltpu.VMEM((OWN * GAP, H), F32),
            pltpu.VMEM((MB * PAIRS, H), BF),
            pltpu.VMEM((NODES, H), F32),
            pltpu.VMEM((GROUP * SMALL, H), F32),
            pltpu.VMEM((PAIRS, H), BF),
            pltpu.SemaphoreType.DMA((8,)),
        ],
        compiler_params=pltpu.CompilerParams(vmem_limit_bytes=limit),
        name="layers",
    )(
        sect,
        node_states,
        edge_features,
        ends,
        w_edge_in,
        b_edge_in.reshape(1, H),
        w_edge_out,
        b_edge_out.reshape(H, H),
        w_input,
        w_hidden,
        b_input.reshape(1, 3 * H),
        b_hidden.reshape(1, 3 * H),
        cotangent,
    )

    got = lax.all_to_all(send, "dp", split_axis=0, concat_axis=0)
    piece = pl.pallas_call(
        sum_kernel,
        out_shape=shape((2 * GROUP, ROWS, H), BF),
        in_specs=[vmem],
        out_specs=vmem,
        compiler_params=pltpu.CompilerParams(vmem_limit_bytes=limit),
        name="sum_parts",
    )(got)
    near = lax.all_to_all(piece, ("zh", "dp"), split_axis=0, concat_axis=0)
    far = lax.ppermute(near, "core", [(0, 1), (1, 0)])

    stage = [pltpu.VMEM((4, 16, GROUP * H), F32), pltpu.SemaphoreType.DMA((4,))]
    half = pl.pallas_call(
        first_kernel,
        out_shape=shape((H, H * H), F32),
        in_specs=[smem, vmem],
        out_specs=hbm,
        scratch_shapes=stage,
        compiler_params=pltpu.CompilerParams(vmem_limit_bytes=limit),
        name="place_near",
    )(mine, near)
    grad_states = pl.pallas_call(
        states_kernel,
        out_shape=shape((ATOMS, H), F32),
        in_specs=[smem] + [vmem] * 4,
        out_specs=vmem,
        scratch_shapes=[pltpu.VMEM((H * (ATOMS + 1), H), F32), pltpu.VMEM((NODES, H), F32)],
        compiler_params=pltpu.CompilerParams(vmem_limit_bytes=limit),
        name="states_back",
    )(sect, base, grad_t, pairs, w_edge_out)
    grad_w_out, grad_b_out, grad_w_in, grad_w_hid, misc = pl.pallas_call(
        second_kernel,
        out_shape=(
            shape((H, H * H), F32),
            shape((H, H), F32),
            shape((H, 3 * H), F32),
            shape((H, 3 * H), F32),
            shape((32, H), F32),
        ),
        in_specs=[smem, smem, vmem, vmem, hbm],
        out_specs=(hbm, vmem, vmem, vmem, vmem),
        scratch_shapes=[pltpu.VMEM((MB * GROUP * SMALL, H), F32)] + stage,
        input_output_aliases={4: 0},
        compiler_params=pltpu.CompilerParams(vmem_limit_bytes=limit),
        name="place_far",
    )(mine, other, near, far, half)
    return (
        final,
        grad_states,
        misc[:16],
        misc[16],
        grad_w_out,
        grad_b_out.reshape(H * H),
        grad_w_in,
        grad_w_hid,
        misc[17:20].reshape(3 * H),
        misc[20:23].reshape(3 * H),
    )


def solution(mesh):
    wide = Mesh(mesh.devices.reshape(2, 2, GROUP), ("zh", "core", "dp"))
    split = P(("dp", "zh", "core"), None)
    in_specs = (
        P("dp", None),
        P(None, "dp"),
        P("dp"),
        P("dp"),
        P("dp"),
        P(),
        P(),
        P(),
        P(),
        P(),
        P(),
        P(),
        P(),
        P("dp", None),
    )
    out_specs = (split, split, P(), P(), P(), P(), P(), P(), P(), P())
    return jax.shard_map(local, mesh=wide, in_specs=in_specs, out_specs=out_specs, check_vma=False)
```

```python
import functools

import jax
import jax.numpy as jnp
from jax import lax
from jax.experimental import pallas as pl
from jax.experimental.pallas import tpu as pltpu
from jax.sharding import Mesh
from jax.sharding import PartitionSpec as P

H = 128
ATOMS = 32
EPM = 256
MB = 4
NODES = MB * ATOMS
PAIRS = ATOMS * ATOMS
OWN = H // MB
GAP = 129
ROWS = 136
SMALL = 8
GROUP = 32
BF = jnp.bfloat16
F32 = jnp.float32


def nn(left, right):
    return jnp.dot(left, right, preferred_element_type=F32)


def nt(left, right):
    return lax.dot_general(left, right, (((1,), (1,)), ((), ())), preferred_element_type=F32)


def tn(left, right):
    return lax.dot_general(left, right, (((0,), (0,)), ((), ())), preferred_element_type=F32)


def halves(value):
    high = value.astype(BF)
    return high, (value - high.astype(F32)).astype(BF)


def fine(dot, left, right):
    lh, ll = halves(left)
    rh, rl = halves(right)
    return dot(lh, rh) + (dot(lh, rl) + dot(ll, rh))


def fine_left(dot, left, right):
    lh, ll = halves(left)
    return dot(lh, right) + dot(ll, right)


def fine_right(dot, left, right):
    rh, rl = halves(right)
    return dot(left, rh) + dot(left, rl)


def sigmoid(value):
    return 0.5 * jnp.tanh(0.5 * value) + 0.5


def gate_forward(message, states, w_input, w_hidden, b_input, b_hidden):
    from_msg = nn(message, w_input) + b_input
    from_state = nn(states, w_hidden) + b_hidden
    reset = sigmoid(from_msg[:, :H] + from_state[:, :H])
    update = sigmoid(from_msg[:, H : 2 * H] + from_state[:, H : 2 * H])
    state_cand = from_state[:, 2 * H :]
    candidate = jnp.tanh(from_msg[:, 2 * H :] + reset * state_cand)
    renewed = (1.0 - update) * candidate + update * states.astype(F32)
    return reset, update, candidate, state_cand, renewed


def gate_backward(grad, states, parts, w_input, w_hidden):
    reset, update, candidate, state_cand = parts
    act = grad * (1.0 - update) * (1.0 - candidate * candidate)
    d_reset = act * state_cand * reset * (1.0 - reset)
    d_update = grad * (states.astype(F32) - candidate) * update * (1.0 - update)
    d_in = jnp.concatenate([d_reset, d_update, act], axis=1).astype(BF)
    d_hid = jnp.concatenate([d_reset, d_update, act * reset], axis=1).astype(BF)
    g_msg = nt(d_in, w_input).astype(BF)
    grad_states = grad * update + nt(d_hid, w_hidden)
    return d_in, d_hid, g_msg, grad_states


def edge_front(features, w_edge_in, b_edge_in):
    return tn(features, w_edge_in) + b_edge_in


def local_kernel(sect_ref, *refs):
    ins, refs = refs[:14], refs[14:]
    (send_ref, final_ref, base_ref, grad_t_ref, pairs_out_ref), refs = refs[:5], refs[5:]
    held, refs = refs[:14], refs[14:]
    u_one, u_two, d_all, d_own, pair_h, rows_scr, small_scr, q_scr, sems, w_sems = refs
    (
        source_ref,
        target_ref,
        live_ref,
        feat_ref,
        w_ein_ref,
        b_ein_ref,
        states_ref,
        b_mat_ref,
        w_in_ref,
        w_hid_ref,
        b_in_ref,
        b_hid_ref,
        cot_ref,
        w_ref,
    ) = held
    sect = sect_ref[0]
    chunk = 2048
    copies = [
        pltpu.make_async_copy(ins[at], held[at], sems.at[at]) for at in range(13)
    ]

    def w_copy(at):
        cols = pl.ds(at * chunk, chunk)
        return pltpu.make_async_copy(ins[13].at[:, cols], w_ref.at[:, cols], w_sems.at[at])

    for copy in copies:
        copy.start()
    for at in range(8):
        w_copy(at).start()
    for copy in copies:
        copy.wait()

    states0 = states_ref[...]
    w_ein = w_ein_ref[...]
    b_ein = b_ein_ref[...]
    b_mat = b_mat_ref[...]
    source = source_ref[...]
    target = target_ref[...]
    live = live_ref[...]
    pair = jnp.where(live > 0, source * ATOMS + target, -1)

    slot = lax.broadcasted_iota(jnp.int32, (PAIRS, H), 0)
    for mol in range(MB):
        pre = edge_front(feat_ref[:, mol * EPM : (mol + 1) * EPM], w_ein, b_ein)
        hidden = (pre * sigmoid(pre)).astype(BF)
        hot = jnp.concatenate(
            [
                jnp.where(slot == pair[2 * mol + part : 2 * mol + part + 1, :], 1.0, 0.0).astype(BF)
                for part in range(2)
            ],
            axis=1,
        )
        pair_h[mol * PAIRS : (mol + 1) * PAIRS, :] = nn(hot, hidden).astype(BF)

    node = lax.broadcasted_iota(jnp.int32, (NODES, H), 0)
    hot_t, hot_s = [], []
    for row in range(8):
        shift = (row // 2) * ATOMS
        keep = live[row : row + 1, :] > 0
        t_at = jnp.where(keep, target[row : row + 1, :] + shift, -1)
        s_at = source[row : row + 1, :] + shift
        hot_t.append(jnp.where(node == t_at, 1.0, 0.0).astype(BF))
        hot_s.append(jnp.where(node == s_at, 1.0, 0.0).astype(BF))
    hot_t = jnp.concatenate(hot_t, axis=1)
    hot_s = jnp.concatenate(hot_s, axis=1)
    adj = nt(hot_t, hot_s).astype(BF)
    adj_t = nt(hot_s, hot_t).astype(BF)

    def spread(states, u_ref, wait):
        def step(at):
            base = pl.multiple_of(at * 4 * H, 4 * H)
            four = [w_ref[:, pl.ds(base + q * H, H)] for q in range(4)]
            out = nt(states, jnp.concatenate(four, axis=0))
            for q in range(4):
                u_ref[pl.ds(at * 4 + q, NODES, stride=GAP), :] = out[:, q * H : (q + 1) * H]

        if wait:
            for at in range(8):
                w_copy(at).wait()
                for inner in range(4):
                    step(at * 4 + inner)
        else:

            def body(at, carry):
                step(at)
                return carry

            lax.fori_loop(0, 32, body, 0, unroll=8)

    def u_rows(u_ref, at):
        return u_ref[pl.ds(at * GAP, H), :].astype(BF)

    def gather(states, u_ref):
        side = fine_right(nt, states, b_mat)
        extra = fine_right(nn, adj, side)
        parts = []
        for mol in range(MB):

            def body(at, total, mol=mol):
                first = mol * ATOMS + at * 4
                left = jnp.concatenate(
                    [
                        pair_h[pl.ds(pl.multiple_of((first + q) * ATOMS, ATOMS), ATOMS), :]
                        for q in range(4)
                    ],
                    axis=1,
                )
                right = jnp.concatenate([u_rows(u_ref, first + q) for q in range(4)], axis=1)
                return total + nt(left, right)

            parts.append(lax.fori_loop(0, 8, body, jnp.zeros((ATOMS, H), F32), unroll=True))
        return (jnp.concatenate(parts, axis=0) + extra).astype(BF)

    w_in = w_in_ref[...]
    w_hid = w_hid_ref[...]
    b_in = jnp.concatenate([b_in_ref[part : part + 1, :] for part in range(3)], axis=1)
    b_hid = jnp.concatenate([b_hid_ref[part : part + 1, :] for part in range(3)], axis=1)

    spread(states0, u_one, True)
    msg_one = gather(states0, u_one)
    *parts_one, renewed = gate_forward(msg_one, states0, w_in, w_hid, b_in, b_hid)
    states1 = renewed.astype(BF)
    spread(states1, u_two, False)
    msg_two = gather(states1, u_two)
    *parts_two, final = gate_forward(msg_two, states1, w_in, w_hid, b_in, b_hid)
    own_rows = pl.ds(pl.multiple_of(sect * ATOMS, ATOMS), ATOMS)
    rows_scr[...] = final
    final_ref[...] = rows_scr[own_rows, :]

    d_in2, d_hid2, g_two, back_one = gate_backward(cot_ref[...], states1, parts_two, w_in, w_hid)
    g_two_t = g_two.astype(F32).T.astype(BF)

    for mol in range(MB):
        left = g_two_t[:, mol * ATOMS : (mol + 1) * ATOMS]

        def body(at, carry, mol=mol, left=left):
            first = mol * ATOMS + at * 4
            right = jnp.concatenate(
                [
                    pair_h[pl.ds(pl.multiple_of((first + q) * ATOMS, ATOMS), ATOMS), :]
                    for q in range(4)
                ],
                axis=1,
            )
            out = nn(left, right)
            for q in range(4):
                d_all[pl.ds(first + q, H, stride=GAP), :] = out[:, q * H : (q + 1) * H]
            return carry

        lax.fori_loop(0, 8, body, 0, unroll=True)

    def back_body(at, total):
        base = pl.multiple_of(at * 4 * H, 4 * H)
        left = jnp.concatenate(
            [d_all[pl.ds((at * 4 + q) * GAP, NODES), :].astype(BF) for q in range(4)], axis=1
        )
        right = jnp.concatenate([w_ref[:, pl.ds(base + q * H, H)] for q in range(4)], axis=0)
        return total + nn(left, right)

    back_msg = lax.fori_loop(0, 32, back_body, jnp.zeros((NODES, H), F32), unroll=8)
    share = nn(adj_t, g_two)
    grad_one = back_one + back_msg + fine(nn, share, b_mat)

    d_in1, d_hid1, g_one, back_zero = gate_backward(grad_one, states0, parts_one, w_in, w_hid)
    rows_scr[...] = g_one.astype(F32).T
    g_one_t = rows_scr[...].astype(BF)
    g_one_own = rows_scr[own_rows, :].astype(BF)

    for mol in range(MB):
        left = g_one_own[:, mol * ATOMS : (mol + 1) * ATOMS]

        def body(at, carry, mol=mol, left=left):
            first = mol * ATOMS + at * 4
            right = jnp.concatenate(
                [
                    pair_h[pl.ds(pl.multiple_of((first + q) * ATOMS, ATOMS), ATOMS), :]
                    for q in range(4)
                ],
                axis=1,
            )
            out = nn(left, right)
            for q in range(4):
                d_own[pl.ds(first + q, OWN, stride=GAP), :] = out[:, q * H : (q + 1) * H]
            return carry

        lax.fori_loop(0, 8, body, 0, unroll=True)

    both_t = jnp.concatenate([states0.astype(F32).T, states1.astype(F32).T], axis=1).astype(BF)

    def own_body(at, carry):
        right = jnp.concatenate(
            [
                d_own[pl.ds(at * GAP, NODES), :].astype(BF),
                d_all[pl.ds((sect * OWN + at) * GAP, NODES), :].astype(BF),
            ],
            axis=0,
        )
        send_ref[at, 0:H, :] = nn(both_t, right).astype(BF)
        return carry

    lax.fori_loop(0, OWN, own_body, 0, unroll=8)

    rows_scr[...] = g_one.astype(F32)
    g1 = rows_scr[own_rows, :].astype(BF)
    rows_scr[...] = g_two.astype(F32)
    g2 = rows_scr[own_rows, :].astype(BF)
    g_both = jnp.concatenate([g1, g2], axis=1)

    def q_body(at, carry):
        first = sect * ATOMS + at * 2
        right = jnp.concatenate(
            [
                jnp.concatenate([u_rows(u_one, first + q), u_rows(u_two, first + q)], axis=0)
                for q in range(2)
            ],
            axis=1,
        )
        out = nn(g_both, right).astype(BF)
        for q in range(2):
            q_scr[pl.ds(pl.multiple_of((at * 2 + q) * ATOMS, ATOMS), ATOMS), :] = out[
                :, q * H : (q + 1) * H
            ]
        return carry

    lax.fori_loop(0, 16, q_body, 0, unroll=8)
    own_cols = pl.ds(pl.multiple_of(sect * EPM, EPM), EPM)
    feat_own = feat_ref[:, own_cols]
    pre_own = edge_front(feat_own, w_ein, b_ein)
    sig = sigmoid(pre_own)
    slope = sig * (1.0 + pre_own * (1.0 - sig))
    rows_scr[0:8, :] = pair.astype(F32)
    pair_own = rows_scr[pl.ds(sect * 2, 2), :].astype(jnp.int32)
    hot = jnp.concatenate(
        [jnp.where(slot == pair_own[part : part + 1, :], 1.0, 0.0).astype(BF) for part in range(2)],
        axis=1,
    )
    g_pre = tn(hot, q_scr[...]) * slope

    g_share_t = nn(g_one_t, adj), nn(g_two_t, adj)
    grad_b_out = fine_left(nn, g_share_t[0], states0) + fine_left(nn, g_share_t[1], states1)
    rows_scr[...] = grad_b_out
    small_scr[0:32, :] = rows_scr[own_rows, :]
    both_rows = jnp.concatenate(
        [msg_one.astype(F32).T, msg_two.astype(F32).T], axis=1
    )
    d_in_both = jnp.concatenate([d_in1, d_in2], axis=0)
    d_hid_both = jnp.concatenate([d_hid1, d_hid2], axis=0)
    for at, (rows_t, d_both) in enumerate(
        ((both_rows, d_in_both), (both_t.astype(F32), d_hid_both))
    ):
        rows_scr[...] = rows_t[:, :H]
        first = rows_scr[own_rows, :]
        rows_scr[...] = rows_t[:, H:]
        left = jnp.concatenate([first, rows_scr[own_rows, :]], axis=1).astype(BF)
        out = nn(left, d_both)
        for part in range(3):
            row = 32 + at * 96 + part * 32
            small_scr[row : row + 32, :] = out[:, part * H : (part + 1) * H]
    small_scr[224:240, :] = fine_right(nn, feat_own, g_pre)
    small_scr[240:256, :] = jnp.zeros((16, H), F32)
    small_scr[240:241, :] = jnp.sum(g_pre, axis=0, keepdims=True)
    for at, pair_d in enumerate(((d_in1, d_in2), (d_hid1, d_hid2))):
        for part in range(3):
            cols = slice(part * H, (part + 1) * H)
            rows_scr[...] = pair_d[0][:, cols].astype(F32) + pair_d[1][:, cols].astype(F32)
            row = 241 + at * 3 + part
            small_scr[row : row + 1, :] = jnp.sum(rows_scr[own_rows, :], axis=0, keepdims=True)
    for at in range(GROUP):
        send_ref[at, H:ROWS, :] = small_scr[at * SMALL : (at + 1) * SMALL, :].astype(BF)

    rows_scr[...] = back_zero + fine(nn, nn(adj_t, g_one), b_mat)
    base_ref[...] = rows_scr[own_rows, :]
    grad_t_ref[...] = g_one_t
    pairs_out_ref[...] = pair_h[pl.ds(pl.multiple_of(sect * PAIRS, PAIRS), PAIRS), :]


def sum_kernel(got_ref, out_ref):
    def body(at, total):
        return total + got_ref[at].astype(F32)

    total = lax.fori_loop(1, GROUP, body, got_ref[0].astype(F32), unroll=True)
    piece = jnp.concatenate([total[:H].T, total[H:]], axis=0).astype(BF)

    def put(at, carry):
        out_ref[at] = piece
        return carry

    lax.fori_loop(0, 2 * GROUP, put, 0, unroll=8)


def states_kernel(sect_ref, base_ref, grad_t_ref, pairs_ref, w_ref, out_ref, d_all, rows_scr):
    sect = sect_ref[0]
    rows_scr[...] = grad_t_ref[...].astype(F32).T
    own = rows_scr[pl.ds(pl.multiple_of(sect * ATOMS, ATOMS), ATOMS), :]
    left = own.T.astype(BF)
    gap = ATOMS + 1

    def body(at, carry):
        right = jnp.concatenate(
            [
                pairs_ref[pl.ds(pl.multiple_of((at * 4 + q) * ATOMS, ATOMS), ATOMS), :]
                for q in range(4)
            ],
            axis=1,
        )
        out = nn(left, right)
        for q in range(4):
            d_all[pl.ds(at * 4 + q, H, stride=gap), :] = out[:, q * H : (q + 1) * H]
        return carry

    lax.fori_loop(0, 8, body, 0, unroll=True)

    def back_body(at, total):
        base = pl.multiple_of(at * 4 * H, 4 * H)
        left = jnp.concatenate(
            [d_all[pl.ds((at * 4 + q) * gap, ATOMS), :].astype(BF) for q in range(4)], axis=1
        )
        right = jnp.concatenate([w_ref[:, pl.ds(base + q * H, H)] for q in range(4)], axis=0)
        return total + nn(left, right)

    out_ref[...] = lax.fori_loop(0, 32, back_body, base_ref[...], unroll=8)


def place_kernel(count, core_ref, got_ref, out_hbm, stage, sems):
    core = core_ref[0]
    steps = [(half, row) for half in range(2) for row in range(8)]

    def copy(at):
        half, row = steps[at]
        section = half * 2 + core
        cols = pl.ds(pl.multiple_of(section * GROUP * H, GROUP * H), GROUP * H)
        return pltpu.make_async_copy(
            stage.at[at % 4], out_hbm.at[pl.ds(row * 16, 16), cols], sems.at[at % 4]
        )

    for at, (half, row) in enumerate(steps):
        if at >= 4:
            copy(at - 4).wait()
        for dev in range(GROUP):
            stage[at % 4, :, dev * H : (dev + 1) * H] = got_ref[
                half * GROUP + dev, row * 16 : (row + 1) * 16, :
            ].astype(F32)
        copy(at).start()
    for at in range(len(steps) - 4, len(steps)):
        copy(at).wait()


def first_kernel(core_ref, got_ref, out_hbm, stage, sems):
    place_kernel(2, core_ref, got_ref, out_hbm, stage, sems)


def second_kernel(
    core_ref, other_ref, mine_ref, far_ref, half_hbm, out_hbm, gb_ref, gi_ref, gh_ref, ge_ref, be_ref, bi_ref, bh_ref, small, stage, sems
):
    del half_hbm
    place_kernel(2, other_ref, far_ref, out_hbm, stage, sems)
    for which, ref in ((core_ref[0], mine_ref), (other_ref[0], far_ref)):
        for half in range(2):
            base = (half * 2 + which) * (GROUP * SMALL)
            for dev in range(GROUP):
                at = pl.multiple_of(base + dev * SMALL, SMALL)
                small[pl.ds(at, SMALL), :] = ref[half * GROUP + dev, H:ROWS, :].astype(F32)
    misc = jnp.zeros((32, H), F32)
    for sect in range(MB):
        base = sect * GROUP * SMALL
        rows = slice(sect * 32, (sect + 1) * 32)
        gb_ref[rows, :] = small[base : base + 32, :]
        for part in range(3):
            cols = slice(part * H, (part + 1) * H)
            row = base + 32 + part * 32
            gi_ref[rows, cols] = small[row : row + 32, :]
            gh_ref[rows, cols] = small[row + 96 : row + 128, :]
        misc = misc + small[base + 224 : base + 256, :]
    ge_ref[...] = misc[0:16]
    be_ref[...] = misc[16:17]
    bi_ref[...] = misc[17:20]
    bh_ref[...] = misc[20:23]


VMEM_SPEC = pl.BlockSpec(memory_space=pltpu.VMEM)
SMEM_SPEC = pl.BlockSpec(memory_space=pltpu.SMEM)
ANY_SPEC = pl.BlockSpec(memory_space=pl.ANY)
BIG = 60 * 2**20
LOW = 8 * 2**20
shape = jax.ShapeDtypeStruct


def run_layers(sect, operands):
    return pl.pallas_call(
        local_kernel,
        out_shape=(
            shape((GROUP, ROWS, H), BF),
            shape((ATOMS, H), F32),
            shape((ATOMS, H), F32),
            shape((H, NODES), BF),
            shape((PAIRS, H), BF),
        ),
        in_specs=[SMEM_SPEC] + [ANY_SPEC] * 14,
        out_specs=(VMEM_SPEC,) * 5,
        scratch_shapes=[pltpu.VMEM(v.shape, v.dtype) for v in operands]
        + [
            pltpu.VMEM((NODES * GAP, H), F32),
            pltpu.VMEM((NODES * GAP, H), F32),
            pltpu.VMEM((H * GAP, H), F32),
            pltpu.VMEM((OWN * GAP, H), F32),
            pltpu.VMEM((MB * PAIRS, H), BF),
            pltpu.VMEM((NODES, H), F32),
            pltpu.VMEM((GROUP * SMALL, H), F32),
            pltpu.VMEM((PAIRS, H), BF),
            pltpu.SemaphoreType.DMA((13,)),
            pltpu.SemaphoreType.DMA((8,)),
        ],
        compiler_params=pltpu.CompilerParams(vmem_limit_bytes=BIG),
        name="layers",
    )(sect, *operands)


def local(
    node_states,
    edge_features,
    edge_source,
    edge_target,
    edge_live,
    w_edge_in,
    b_edge_in,
    w_edge_out,
    b_edge_out,
    w_input,
    w_hidden,
    b_input,
    b_hidden,
    cotangent,
):
    core = lax.axis_index("core").astype(jnp.int32)
    sect = (lax.axis_index("zh") * 2 + core).astype(jnp.int32)
    sect = sect.reshape(1)
    mine = core.reshape(1)
    other = 1 - mine
    operands = [v.reshape(8, 128) for v in (edge_source, edge_target, edge_live)] + [
        edge_features,
        w_edge_in,
        b_edge_in.reshape(1, H),
        node_states,
        b_edge_out.reshape(H, H),
        w_input,
        w_hidden,
        b_input.reshape(3, H),
        b_hidden.reshape(3, H),
        cotangent,
        w_edge_out,
    ]

    send, final, base, grad_t, pairs = run_layers(sect, operands)
    got = lax.all_to_all(send, "dp", split_axis=0, concat_axis=0)
    piece = pl.pallas_call(
        sum_kernel,
        out_shape=shape((2 * GROUP, ROWS, H), BF),
        in_specs=[VMEM_SPEC],
        out_specs=VMEM_SPEC,
        compiler_params=pltpu.CompilerParams(vmem_limit_bytes=LOW),
        name="sum_parts",
    )(got)
    grad_states = pl.pallas_call(
        states_kernel,
        out_shape=shape((ATOMS, H), F32),
        in_specs=[SMEM_SPEC] + [VMEM_SPEC] * 4,
        out_specs=VMEM_SPEC,
        scratch_shapes=[pltpu.VMEM((H * (ATOMS + 1), H), F32), pltpu.VMEM((NODES, H), F32)],
        compiler_params=pltpu.CompilerParams(vmem_limit_bytes=LOW),
        cost_estimate=pl.CostEstimate(
            flops=2 * ATOMS * H * H * H, bytes_accessed=2 * H * H * H, transcendentals=0
        ),
        name="states_back",
    )(sect, base, grad_t, pairs, w_edge_out)
    near = lax.all_to_all(piece, ("zh", "dp"), split_axis=0, concat_axis=0)
    near, grad_states = lax.optimization_barrier((near, grad_states))
    far = lax.ppermute(near, "core", [(0, 1), (1, 0)])

    stage = [pltpu.VMEM((4, 16, GROUP * H), F32), pltpu.SemaphoreType.DMA((4,))]
    half = pl.pallas_call(
        first_kernel,
        out_shape=shape((H, H * H), F32),
        in_specs=[SMEM_SPEC, VMEM_SPEC],
        out_specs=ANY_SPEC,
        scratch_shapes=stage,
        compiler_params=pltpu.CompilerParams(vmem_limit_bytes=LOW),
        name="place_near",
    )(mine, near)
    grad_w_out, grad_b_out, grad_w_in, grad_w_hid, grad_ein, grad_bein, grad_bin, grad_bhid = pl.pallas_call(
        second_kernel,
        out_shape=(
            shape((H, H * H), F32),
            shape((H, H), F32),
            shape((H, 3 * H), F32),
            shape((H, 3 * H), F32),
            shape((16, H), F32),
            shape((1, H), F32),
            shape((3, H), F32),
            shape((3, H), F32),
        ),
        in_specs=[SMEM_SPEC, SMEM_SPEC, VMEM_SPEC, VMEM_SPEC, ANY_SPEC],
        out_specs=(ANY_SPEC,) + (VMEM_SPEC,) * 7,
        scratch_shapes=[pltpu.VMEM((MB * GROUP * SMALL, H), F32)] + stage,
        input_output_aliases={4: 0},
        compiler_params=pltpu.CompilerParams(vmem_limit_bytes=LOW),
        name="place_far",
    )(mine, other, near, far, half)
    return (
        final,
        grad_states,
        grad_ein,
        grad_bein.reshape(H),
        grad_w_out,
        grad_b_out.reshape(H * H),
        grad_w_in,
        grad_w_hid,
        grad_bin.reshape(3 * H),
        grad_bhid.reshape(3 * H),
    )


def solution(mesh):
    wide = Mesh(mesh.devices.reshape(2, 2, GROUP), ("zh", "core", "dp"))
    split = P(("dp", "zh", "core"), None)
    in_specs = (
        P("dp", None),
        P(None, "dp"),
        P("dp"),
        P("dp"),
        P("dp"),
        P(),
        P(),
        P(),
        P(),
        P(),
        P(),
        P(),
        P(),
        P("dp", None),
    )
    out_specs = (split, split, P(), P(), P(), P(), P(), P(), P(), P())
    return jax.shard_map(local, mesh=wide, in_specs=in_specs, out_specs=out_specs, check_vma=False)
```

```python
import functools

import jax
import jax.numpy as jnp
from jax import lax
from jax.experimental import pallas as pl
from jax.experimental.pallas import tpu as pltpu
from jax.sharding import Mesh
from jax.sharding import PartitionSpec as P

H = 128
ATOMS = 32
EPM = 256
MB = 4
NODES = MB * ATOMS
PAIRS = ATOMS * ATOMS
OWN = H // MB
GAP = 129
ROWS = 136
SMALL = 8
GROUP = 32
HALF = H // 2
CUTS = (0, 16, 32, 48, 64)
RUNS = 4
BF = jnp.bfloat16
F32 = jnp.float32


def nn(left, right):
    return jnp.dot(left, right, preferred_element_type=F32)


def nt(left, right):
    return lax.dot_general(left, right, (((1,), (1,)), ((), ())), preferred_element_type=F32)


def tn(left, right):
    return lax.dot_general(left, right, (((0,), (0,)), ((), ())), preferred_element_type=F32)


def halves(value):
    high = value.astype(BF)
    return high, (value - high.astype(F32)).astype(BF)


def fine(dot, left, right):
    lh, ll = halves(left)
    rh, rl = halves(right)
    return dot(lh, rh) + (dot(lh, rl) + dot(ll, rh))


def fine_left(dot, left, right):
    lh, ll = halves(left)
    return dot(lh, right) + dot(ll, right)


def fine_right(dot, left, right):
    rh, rl = halves(right)
    return dot(left, rh) + dot(left, rl)


def sigmoid(value):
    return 0.5 * jnp.tanh(0.5 * value) + 0.5


def gate_forward(message, states, w_input, w_hidden, b_input, b_hidden):
    from_msg = nn(message, w_input) + b_input
    from_state = nn(states, w_hidden) + b_hidden
    reset = sigmoid(from_msg[:, :H] + from_state[:, :H])
    update = sigmoid(from_msg[:, H : 2 * H] + from_state[:, H : 2 * H])
    state_cand = from_state[:, 2 * H :]
    candidate = jnp.tanh(from_msg[:, 2 * H :] + reset * state_cand)
    renewed = (1.0 - update) * candidate + update * states.astype(F32)
    return reset, update, candidate, state_cand, renewed


def gate_backward(grad, states, parts, w_input, w_hidden):
    reset, update, candidate, state_cand = parts
    act = grad * (1.0 - update) * (1.0 - candidate * candidate)
    d_reset = act * state_cand * reset * (1.0 - reset)
    d_update = grad * (states.astype(F32) - candidate) * update * (1.0 - update)
    d_in = jnp.concatenate([d_reset, d_update, act], axis=1).astype(BF)
    d_hid = jnp.concatenate([d_reset, d_update, act * reset], axis=1).astype(BF)
    g_msg = nt(d_in, w_input).astype(BF)
    grad_states = grad * update + nt(d_hid, w_hidden)
    return d_in, d_hid, g_msg, grad_states


def edge_front(features, w_edge_in, b_edge_in):
    return tn(features, w_edge_in) + b_edge_in


def local_kernel(sect_ref, *refs):
    ins, refs = refs[:14], refs[14:]
    (send_ref, final_ref, base_ref, grad_t_ref, pairs_out_ref), refs = refs[:5], refs[5:]
    held, refs = refs[:14], refs[14:]
    u_one, u_two, d_all, d_own, pair_h, rows_scr, small_scr, q_scr, sems, w_sems = refs
    (
        source_ref,
        target_ref,
        live_ref,
        feat_ref,
        w_ein_ref,
        b_ein_ref,
        states_ref,
        b_mat_ref,
        w_in_ref,
        w_hid_ref,
        b_in_ref,
        b_hid_ref,
        cot_ref,
        w_ref,
    ) = held
    sect = sect_ref[0]
    chunk = 2048
    copies = [
        pltpu.make_async_copy(ins[at], held[at], sems.at[at]) for at in range(13)
    ]

    def w_copy(at):
        cols = pl.ds(at * chunk, chunk)
        return pltpu.make_async_copy(ins[13].at[:, cols], w_ref.at[:, cols], w_sems.at[at])

    for copy in copies:
        copy.start()
    for at in range(8):
        w_copy(at).start()
    for copy in copies:
        copy.wait()

    states0 = states_ref[...]
    w_ein = w_ein_ref[...]
    b_ein = b_ein_ref[...]
    b_mat = b_mat_ref[...]
    source = source_ref[...]
    target = target_ref[...]
    live = live_ref[...]
    pair = jnp.where(live > 0, source * ATOMS + target, -1)

    slot = lax.broadcasted_iota(jnp.int32, (PAIRS, H), 0)
    for mol in range(MB):
        pre = edge_front(feat_ref[:, mol * EPM : (mol + 1) * EPM], w_ein, b_ein)
        hidden = (pre * sigmoid(pre)).astype(BF)
        hot = jnp.concatenate(
            [
                jnp.where(slot == pair[2 * mol + part : 2 * mol + part + 1, :], 1.0, 0.0).astype(BF)
                for part in range(2)
            ],
            axis=1,
        )
        pair_h[mol * PAIRS : (mol + 1) * PAIRS, :] = nn(hot, hidden).astype(BF)

    node = lax.broadcasted_iota(jnp.int32, (NODES, H), 0)
    hot_t, hot_s = [], []
    for row in range(8):
        shift = (row // 2) * ATOMS
        keep = live[row : row + 1, :] > 0
        t_at = jnp.where(keep, target[row : row + 1, :] + shift, -1)
        s_at = source[row : row + 1, :] + shift
        hot_t.append(jnp.where(node == t_at, 1.0, 0.0).astype(BF))
        hot_s.append(jnp.where(node == s_at, 1.0, 0.0).astype(BF))
    hot_t = jnp.concatenate(hot_t, axis=1)
    hot_s = jnp.concatenate(hot_s, axis=1)
    adj = nt(hot_t, hot_s).astype(BF)
    adj_t = nt(hot_s, hot_t).astype(BF)

    def spread(states, u_ref, wait):
        def step(at):
            base = pl.multiple_of(at * 4 * H, 4 * H)
            four = [w_ref[:, pl.ds(base + q * H, H)] for q in range(4)]
            out = nt(states, jnp.concatenate(four, axis=0))
            for q in range(4):
                u_ref[pl.ds(at * 4 + q, NODES, stride=GAP), :] = out[:, q * H : (q + 1) * H]

        if wait:
            for at in range(8):
                w_copy(at).wait()
                for inner in range(4):
                    step(at * 4 + inner)
        else:

            def body(at, carry):
                step(at)
                return carry

            lax.fori_loop(0, 32, body, 0, unroll=8)

    def u_rows(u_ref, at):
        return u_ref[pl.ds(at * GAP, H), :].astype(BF)

    def gather(states, u_ref):
        side = fine_right(nt, states, b_mat)
        extra = fine_right(nn, adj, side)
        parts = []
        for mol in range(MB):

            def body(at, total, mol=mol):
                first = mol * ATOMS + at * 4
                left = jnp.concatenate(
                    [
                        pair_h[pl.ds(pl.multiple_of((first + q) * ATOMS, ATOMS), ATOMS), :]
                        for q in range(4)
                    ],
                    axis=1,
                )
                right = jnp.concatenate([u_rows(u_ref, first + q) for q in range(4)], axis=1)
                return total + nt(left, right)

            parts.append(lax.fori_loop(0, 8, body, jnp.zeros((ATOMS, H), F32), unroll=True))
        return (jnp.concatenate(parts, axis=0) + extra).astype(BF)

    w_in = w_in_ref[...]
    w_hid = w_hid_ref[...]
    b_in = jnp.concatenate([b_in_ref[part : part + 1, :] for part in range(3)], axis=1)
    b_hid = jnp.concatenate([b_hid_ref[part : part + 1, :] for part in range(3)], axis=1)

    spread(states0, u_one, True)
    msg_one = gather(states0, u_one)
    *parts_one, renewed = gate_forward(msg_one, states0, w_in, w_hid, b_in, b_hid)
    states1 = renewed.astype(BF)
    spread(states1, u_two, False)
    msg_two = gather(states1, u_two)
    *parts_two, final = gate_forward(msg_two, states1, w_in, w_hid, b_in, b_hid)
    own_rows = pl.ds(pl.multiple_of(sect * ATOMS, ATOMS), ATOMS)
    rows_scr[...] = final
    final_ref[...] = rows_scr[own_rows, :]

    d_in2, d_hid2, g_two, back_one = gate_backward(cot_ref[...], states1, parts_two, w_in, w_hid)
    g_two_t = g_two.astype(F32).T.astype(BF)

    for mol in range(MB):
        left = g_two_t[:, mol * ATOMS : (mol + 1) * ATOMS]

        def body(at, carry, mol=mol, left=left):
            first = mol * ATOMS + at * 4
            right = jnp.concatenate(
                [
                    pair_h[pl.ds(pl.multiple_of((first + q) * ATOMS, ATOMS), ATOMS), :]
                    for q in range(4)
                ],
                axis=1,
            )
            out = nn(left, right)
            for q in range(4):
                d_all[pl.ds(first + q, H, stride=GAP), :] = out[:, q * H : (q + 1) * H]
            return carry

        lax.fori_loop(0, 8, body, 0, unroll=True)

    def back_body(at, total):
        base = pl.multiple_of(at * 4 * H, 4 * H)
        left = jnp.concatenate(
            [d_all[pl.ds((at * 4 + q) * GAP, NODES), :].astype(BF) for q in range(4)], axis=1
        )
        right = jnp.concatenate([w_ref[:, pl.ds(base + q * H, H)] for q in range(4)], axis=0)
        return total + nn(left, right)

    back_msg = lax.fori_loop(0, 32, back_body, jnp.zeros((NODES, H), F32), unroll=8)
    share = nn(adj_t, g_two)
    grad_one = back_one + back_msg + fine(nn, share, b_mat)

    d_in1, d_hid1, g_one, back_zero = gate_backward(grad_one, states0, parts_one, w_in, w_hid)
    rows_scr[...] = g_one.astype(F32).T
    g_one_t = rows_scr[...].astype(BF)
    g_one_own = rows_scr[own_rows, :].astype(BF)

    for mol in range(MB):
        left = g_one_own[:, mol * ATOMS : (mol + 1) * ATOMS]

        def body(at, carry, mol=mol, left=left):
            first = mol * ATOMS + at * 4
            right = jnp.concatenate(
                [
                    pair_h[pl.ds(pl.multiple_of((first + q) * ATOMS, ATOMS), ATOMS), :]
                    for q in range(4)
                ],
                axis=1,
            )
            out = nn(left, right)
            for q in range(4):
                d_own[pl.ds(first + q, OWN, stride=GAP), :] = out[:, q * H : (q + 1) * H]
            return carry

        lax.fori_loop(0, 8, body, 0, unroll=True)

    both_t = jnp.concatenate([states0.astype(F32).T, states1.astype(F32).T], axis=1).astype(BF)

    def own_body(at, carry):
        right = jnp.concatenate(
            [
                d_own[pl.ds(at * GAP, NODES), :].astype(BF),
                d_all[pl.ds((sect * OWN + at) * GAP, NODES), :].astype(BF),
            ],
            axis=0,
        )
        send_ref[at, 0:H, :] = nn(both_t, right).astype(BF)
        return carry

    lax.fori_loop(0, OWN, own_body, 0, unroll=8)

    rows_scr[...] = g_one.astype(F32)
    g1 = rows_scr[own_rows, :].astype(BF)
    rows_scr[...] = g_two.astype(F32)
    g2 = rows_scr[own_rows, :].astype(BF)
    g_both = jnp.concatenate([g1, g2], axis=1)

    def q_body(at, carry):
        first = sect * ATOMS + at * 2
        right = jnp.concatenate(
            [
                jnp.concatenate([u_rows(u_one, first + q), u_rows(u_two, first + q)], axis=0)
                for q in range(2)
            ],
            axis=1,
        )
        out = nn(g_both, right).astype(BF)
        for q in range(2):
            q_scr[pl.ds(pl.multiple_of((at * 2 + q) * ATOMS, ATOMS), ATOMS), :] = out[
                :, q * H : (q + 1) * H
            ]
        return carry

    lax.fori_loop(0, 16, q_body, 0, unroll=8)
    own_cols = pl.ds(pl.multiple_of(sect * EPM, EPM), EPM)
    feat_own = feat_ref[:, own_cols]
    pre_own = edge_front(feat_own, w_ein, b_ein)
    sig = sigmoid(pre_own)
    slope = sig * (1.0 + pre_own * (1.0 - sig))
    rows_scr[0:8, :] = pair.astype(F32)
    pair_own = rows_scr[pl.ds(sect * 2, 2), :].astype(jnp.int32)
    hot = jnp.concatenate(
        [jnp.where(slot == pair_own[part : part + 1, :], 1.0, 0.0).astype(BF) for part in range(2)],
        axis=1,
    )
    g_pre = tn(hot, q_scr[...]) * slope

    g_share_t = nn(g_one_t, adj), nn(g_two_t, adj)
    grad_b_out = fine_left(nn, g_share_t[0], states0) + fine_left(nn, g_share_t[1], states1)
    rows_scr[...] = grad_b_out
    small_scr[0:32, :] = rows_scr[own_rows, :]
    both_rows = jnp.concatenate(
        [msg_one.astype(F32).T, msg_two.astype(F32).T], axis=1
    )
    d_in_both = jnp.concatenate([d_in1, d_in2], axis=0)
    d_hid_both = jnp.concatenate([d_hid1, d_hid2], axis=0)
    for at, (rows_t, d_both) in enumerate(
        ((both_rows, d_in_both), (both_t.astype(F32), d_hid_both))
    ):
        rows_scr[...] = rows_t[:, :H]
        first = rows_scr[own_rows, :]
        rows_scr[...] = rows_t[:, H:]
        left = jnp.concatenate([first, rows_scr[own_rows, :]], axis=1).astype(BF)
        out = nn(left, d_both)
        for part in range(3):
            row = 32 + at * 96 + part * 32
            small_scr[row : row + 32, :] = out[:, part * H : (part + 1) * H]
    small_scr[224:240, :] = fine_right(nn, feat_own, g_pre)
    small_scr[240:256, :] = jnp.zeros((16, H), F32)
    small_scr[240:241, :] = jnp.sum(g_pre, axis=0, keepdims=True)
    for at, pair_d in enumerate(((d_in1, d_in2), (d_hid1, d_hid2))):
        for part in range(3):
            cols = slice(part * H, (part + 1) * H)
            rows_scr[...] = pair_d[0][:, cols].astype(F32) + pair_d[1][:, cols].astype(F32)
            row = 241 + at * 3 + part
            small_scr[row : row + 1, :] = jnp.sum(rows_scr[own_rows, :], axis=0, keepdims=True)
    for at in range(GROUP):
        send_ref[at, H:ROWS, :] = small_scr[at * SMALL : (at + 1) * SMALL, :].astype(BF)

    rows_scr[...] = back_zero + fine(nn, nn(adj_t, g_one), b_mat)
    base_ref[...] = rows_scr[own_rows, :]
    grad_t_ref[...] = g_one_t
    pairs_out_ref[...] = pair_h[pl.ds(pl.multiple_of(sect * PAIRS, PAIRS), PAIRS), :]


def sum_kernel(place_ref, got_ref, out_ref, two):
    shift = place_ref[2]

    def body(at, total):
        return total + got_ref[at].astype(F32)

    total = lax.fori_loop(1, GROUP, body, got_ref[0].astype(F32), unroll=True)
    rows = total[:H].T
    for part in range(2):
        half_rows = rows[part * HALF : (part + 1) * HALF]
        two[part] = jnp.concatenate([half_rows, total[H:]], axis=0).astype(BF)

    def put(at, carry):
        out_ref[at] = two[jnp.bitwise_and(jnp.right_shift(at, shift), 1)]
        return carry

    lax.fori_loop(0, 2 * GROUP, put, 0, unroll=8)


def states_kernel(sect_ref, base_ref, grad_t_ref, pairs_ref, w_ref, out_ref, d_all, rows_scr):
    sect = sect_ref[0]
    rows_scr[...] = grad_t_ref[...].astype(F32).T
    own = rows_scr[pl.ds(pl.multiple_of(sect * ATOMS, ATOMS), ATOMS), :]
    left = own.T.astype(BF)
    gap = ATOMS + 1

    def body(at, carry):
        right = jnp.concatenate(
            [
                pairs_ref[pl.ds(pl.multiple_of((at * 4 + q) * ATOMS, ATOMS), ATOMS), :]
                for q in range(4)
            ],
            axis=1,
        )
        out = nn(left, right)
        for q in range(4):
            d_all[pl.ds(at * 4 + q, H, stride=gap), :] = out[:, q * H : (q + 1) * H]
        return carry

    lax.fori_loop(0, 8, body, 0, unroll=True)

    def back_body(at, total):
        base = pl.multiple_of(at * 4 * H, 4 * H)
        left = jnp.concatenate(
            [d_all[pl.ds((at * 4 + q) * gap, ATOMS), :].astype(BF) for q in range(4)], axis=1
        )
        right = jnp.concatenate([w_ref[:, pl.ds(base + q * H, H)] for q in range(4)], axis=0)
        return total + nn(left, right)

    out_ref[...] = lax.fori_loop(0, 32, back_body, base_ref[...], unroll=8)


def place_rows(place_ref, other_core, other_half, parts, out_hbm, stage, sem):
    core = jnp.bitwise_xor(place_ref[3], 1) if other_core else place_ref[3]
    copies = []
    for run, (ref, first) in enumerate(parts):
        bit = place_ref[run // 2]
        if other_half:
            bit = jnp.bitwise_xor(bit, 1)
        low, high = CUTS[run], CUTS[run + 1]
        half = low // GROUP
        at_col = (half * 2 + core) * (GROUP * H) + (low - half * GROUP) * H
        width = (high - low) * H
        for part in range(2):
            for dev in range(low, high):
                for row in range(part * 32, part * 32 + 32, 16):
                    stage[row : row + 16, dev * H : (dev + 1) * H] = ref[
                        dev - first, row : row + 16, :
                    ].astype(F32)
            copies.append(
                pltpu.make_async_copy(
                    stage.at[pl.ds(part * 32, 32), pl.ds(low * H, width)],
                    out_hbm.at[
                        pl.ds(pl.multiple_of(bit * HALF + part * 32, 32), 32),
                        pl.ds(pl.multiple_of(at_col, H), width),
                    ],
                    sem.at[len(copies)],
                )
            )
            copies[-1].start()
    for copy in copies:
        copy.wait()


def place_own(place_ref, near_ref, out_hbm, stage, sems):
    place_rows(place_ref, False, False, [(near_ref, 0)] * RUNS, out_hbm, stage, sems)


def place_core(
    place_ref,
    near_ref,
    far_ref,
    part_hbm,
    out_hbm,
    gb_ref,
    gi_ref,
    gh_ref,
    ge_ref,
    be_ref,
    bi_ref,
    bh_ref,
    small,
    stage,
    sems,
):
    del part_hbm
    place_rows(place_ref, True, False, [(far_ref, 0)] * RUNS, out_hbm, stage, sems)
    core = place_ref[3]
    for which, ref in ((core, near_ref), (1 - core, far_ref)):
        for half in range(2):
            base = (half * 2 + which) * (GROUP * SMALL)
            for dev in range(GROUP):
                at = pl.multiple_of(base + dev * SMALL, SMALL)
                small[pl.ds(at, SMALL), :] = ref[half * GROUP + dev, HALF:, :].astype(F32)
    misc = jnp.zeros((32, H), F32)
    for sect in range(MB):
        base = sect * GROUP * SMALL
        rows = slice(sect * 32, (sect + 1) * 32)
        gb_ref[rows, :] = small[base : base + 32, :]
        for part in range(3):
            cols = slice(part * H, (part + 1) * H)
            row = base + 32 + part * 32
            gi_ref[rows, cols] = small[row : row + 32, :]
            gh_ref[rows, cols] = small[row + 96 : row + 128, :]
        misc = misc + small[base + 224 : base + 256, :]
    ge_ref[...] = misc[0:16]
    be_ref[...] = misc[16:17]
    bi_ref[...] = misc[17:20]
    bh_ref[...] = misc[20:23]


def place_rest(other_core, place_ref, *refs):
    out_hbm, stage, sems = refs[RUNS + 1 :]
    parts = list(zip(refs[:RUNS], CUTS))
    place_rows(place_ref, other_core, True, parts, out_hbm, stage, sems)


VMEM_SPEC = pl.BlockSpec(memory_space=pltpu.VMEM)
SMEM_SPEC = pl.BlockSpec(memory_space=pltpu.SMEM)
ANY_SPEC = pl.BlockSpec(memory_space=pl.ANY)
BIG = 60 * 2**20
LOW = 8 * 2**20
shape = jax.ShapeDtypeStruct


def run_layers(sect, operands):
    return pl.pallas_call(
        local_kernel,
        out_shape=(
            shape((GROUP, ROWS, H), BF),
            shape((ATOMS, H), F32),
            shape((ATOMS, H), F32),
            shape((H, NODES), BF),
            shape((PAIRS, H), BF),
        ),
        in_specs=[SMEM_SPEC] + [ANY_SPEC] * 14,
        out_specs=(VMEM_SPEC,) * 5,
        scratch_shapes=[pltpu.VMEM(v.shape, v.dtype) for v in operands]
        + [
            pltpu.VMEM((NODES * GAP, H), F32),
            pltpu.VMEM((NODES * GAP, H), F32),
            pltpu.VMEM((H * GAP, H), F32),
            pltpu.VMEM((OWN * GAP, H), F32),
            pltpu.VMEM((MB * PAIRS, H), BF),
            pltpu.VMEM((NODES, H), F32),
            pltpu.VMEM((GROUP * SMALL, H), F32),
            pltpu.VMEM((PAIRS, H), BF),
            pltpu.SemaphoreType.DMA((13,)),
            pltpu.SemaphoreType.DMA((8,)),
        ],
        compiler_params=pltpu.CompilerParams(vmem_limit_bytes=BIG),
        name="layers",
    )(sect, *operands)


def neighbours(axis, side):
    pairs = []
    for index in range(2 * GROUP):
        spot = [index % 4, index // 4 % 4, index // 16]
        step = 1 if spot[axis] % 2 == side else -1
        spot[axis] = (spot[axis] + step) % 4
        pairs.append((index, spot[2] * 16 + spot[1] * 4 + spot[0]))
    return pairs


def local(
    node_states,
    edge_features,
    edge_source,
    edge_target,
    edge_live,
    w_edge_in,
    b_edge_in,
    w_edge_out,
    b_edge_out,
    w_input,
    w_hidden,
    b_input,
    b_hidden,
    cotangent,
):
    core = lax.axis_index("core").astype(jnp.int32)
    sect = (lax.axis_index("zh") * 2 + core).astype(jnp.int32)
    sect = sect.reshape(1)
    dp = lax.axis_index("dp").astype(jnp.int32)
    zh = lax.axis_index("zh").astype(jnp.int32)
    place = jnp.stack([dp & 1, (dp >> 2) & 1, zh * 2, core])
    operands = [v.reshape(8, 128) for v in (edge_source, edge_target, edge_live)] + [
        edge_features,
        w_edge_in,
        b_edge_in.reshape(1, H),
        node_states,
        b_edge_out.reshape(H, H),
        w_input,
        w_hidden,
        b_input.reshape(3, H),
        b_hidden.reshape(3, H),
        cotangent,
        w_edge_out,
    ]

    send, final, base, grad_t, pairs = run_layers(sect, operands)
    grad_states = pl.pallas_call(
        states_kernel,
        out_shape=shape((ATOMS, H), F32),
        in_specs=[SMEM_SPEC] + [VMEM_SPEC] * 4,
        out_specs=VMEM_SPEC,
        scratch_shapes=[pltpu.VMEM((H * (ATOMS + 1), H), F32), pltpu.VMEM((NODES, H), F32)],
        compiler_params=pltpu.CompilerParams(vmem_limit_bytes=LOW),
        cost_estimate=pl.CostEstimate(
            flops=2 * ATOMS * H * H * H, bytes_accessed=2 * H * H * H, transcendentals=0
        ),
        name="states_back",
    )(sect, base, grad_t, pairs, w_edge_out)
    got = lax.all_to_all(send, "dp", split_axis=0, concat_axis=0)
    got, grad_states = lax.optimization_barrier((got, grad_states))
    piece = pl.pallas_call(
        sum_kernel,
        out_shape=shape((2 * GROUP, HALF + SMALL, H), BF),
        in_specs=[SMEM_SPEC, VMEM_SPEC],
        out_specs=VMEM_SPEC,
        scratch_shapes=[pltpu.VMEM((2, HALF + SMALL, H), BF)],
        compiler_params=pltpu.CompilerParams(vmem_limit_bytes=LOW),
        name="sum_parts",
    )(place, got)
    near = lax.all_to_all(piece, ("zh", "dp"), split_axis=0, concat_axis=0)
    far = lax.ppermute(near, "core", [(0, 1), (1, 0)])
    rest = [
        lax.ppermute(
            near[CUTS[run] : CUTS[run + 1], :HALF], ("zh", "dp"), neighbours(run // 2, run % 2)
        )
        for run in range(RUNS)
    ]
    stage = [pltpu.VMEM((HALF, 2 * GROUP * H), F32), pltpu.SemaphoreType.DMA((2 * RUNS,))]
    params = pltpu.CompilerParams(vmem_limit_bytes=LOW)
    cost = pl.CostEstimate(flops=0, bytes_accessed=6 * 2**20, transcendentals=0)
    whole = shape((H, H * H), F32)
    out = pl.pallas_call(
        place_own,
        out_shape=whole,
        in_specs=[SMEM_SPEC, VMEM_SPEC],
        out_specs=ANY_SPEC,
        scratch_shapes=stage,
        compiler_params=params,
        cost_estimate=cost,
        name="place_own",
    )(place, near)
    out, grad_b_out, grad_w_in, grad_w_hid, grad_ein, grad_bein, grad_bin, grad_bhid = (
        pl.pallas_call(
            place_core,
            out_shape=(
                whole,
                shape((H, H), F32),
                shape((H, 3 * H), F32),
                shape((H, 3 * H), F32),
                shape((16, H), F32),
                shape((1, H), F32),
                shape((3, H), F32),
                shape((3, H), F32),
            ),
            in_specs=[SMEM_SPEC, VMEM_SPEC, VMEM_SPEC, ANY_SPEC],
            out_specs=(ANY_SPEC,) + (VMEM_SPEC,) * 7,
            scratch_shapes=[pltpu.VMEM((MB * GROUP * SMALL, H), F32)] + stage,
            input_output_aliases={3: 0},
            compiler_params=params,
            cost_estimate=cost,
            name="place_core",
        )(place, near, far, out)
    )
    rest, out = lax.optimization_barrier((rest, out))
    far_rest = [lax.ppermute(part, "core", [(0, 1), (1, 0)]) for part in rest]
    for other_core, parts in ((False, rest), (True, far_rest)):
        out = pl.pallas_call(
            functools.partial(place_rest, other_core),
            out_shape=whole,
            in_specs=[SMEM_SPEC] + [VMEM_SPEC] * RUNS + [ANY_SPEC],
            out_specs=ANY_SPEC,
            scratch_shapes=stage,
            input_output_aliases={RUNS + 1: 0},
            compiler_params=params,
            cost_estimate=cost,
            name="place_rest",
        )(place, *parts, out)
    grad_w_out = out
    return (
        final,
        grad_states,
        grad_ein,
        grad_bein.reshape(H),
        grad_w_out,
        grad_b_out.reshape(H * H),
        grad_w_in,
        grad_w_hid,
        grad_bin.reshape(3 * H),
        grad_bhid.reshape(3 * H),
    )


def solution(mesh):
    wide = Mesh(mesh.devices.reshape(2, 2, GROUP), ("zh", "core", "dp"))
    split = P(("dp", "zh", "core"), None)
    in_specs = (
        P("dp", None),
        P(None, "dp"),
        P("dp"),
        P("dp"),
        P("dp"),
        P(),
        P(),
        P(),
        P(),
        P(),
        P(),
        P(),
        P(),
        P("dp", None),
    )
    out_specs = (split, split, P(), P(), P(), P(), P(), P(), P(), P())
    return jax.shard_map(local, mesh=wide, in_specs=in_specs, out_specs=out_specs, check_vma=False)
```

```python
import functools

import jax
import jax.numpy as jnp
from jax import lax
from jax.experimental import pallas as pl
from jax.experimental.pallas import tpu as pltpu
from jax.sharding import Mesh
from jax.sharding import PartitionSpec as P

H = 128
ATOMS = 32
EPM = 256
MB = 4
NODES = MB * ATOMS
PAIRS = ATOMS * ATOMS
OWN = H // MB
GAP = 129
ROWS = 136
SMALL = 8
GROUP = 32
HALF = H // 2
CUTS = (0, 16, 32, 48, 64)
RUNS = 4
W_PARTS = 1
BF = jnp.bfloat16
F32 = jnp.float32


def nn(left, right):
    return jnp.dot(left, right, preferred_element_type=F32)


def nt(left, right):
    return lax.dot_general(left, right, (((1,), (1,)), ((), ())), preferred_element_type=F32)


def tn(left, right):
    return lax.dot_general(left, right, (((0,), (0,)), ((), ())), preferred_element_type=F32)


def halves(value):
    high = value.astype(BF)
    return high, (value - high.astype(F32)).astype(BF)


def fine(dot, left, right):
    lh, ll = halves(left)
    rh, rl = halves(right)
    return dot(lh, rh) + (dot(lh, rl) + dot(ll, rh))


def fine_left(dot, left, right):
    lh, ll = halves(left)
    return dot(lh, right) + dot(ll, right)


def fine_right(dot, left, right):
    rh, rl = halves(right)
    return dot(left, rh) + dot(left, rl)


def sigmoid(value):
    return 0.5 * jnp.tanh(0.5 * value) + 0.5


def gate_forward(message, states, w_input, w_hidden, b_input, b_hidden):
    from_msg = nn(message, w_input) + b_input
    from_state = nn(states, w_hidden) + b_hidden
    reset = sigmoid(from_msg[:, :H] + from_state[:, :H])
    update = sigmoid(from_msg[:, H : 2 * H] + from_state[:, H : 2 * H])
    state_cand = from_state[:, 2 * H :]
    candidate = jnp.tanh(from_msg[:, 2 * H :] + reset * state_cand)
    renewed = (1.0 - update) * candidate + update * states.astype(F32)
    return reset, update, candidate, state_cand, renewed


def gate_backward(grad, states, parts, w_input, w_hidden):
    reset, update, candidate, state_cand = parts
    act = grad * (1.0 - update) * (1.0 - candidate * candidate)
    d_reset = act * state_cand * reset * (1.0 - reset)
    d_update = grad * (states.astype(F32) - candidate) * update * (1.0 - update)
    d_in = jnp.concatenate([d_reset, d_update, act], axis=1).astype(BF)
    d_hid = jnp.concatenate([d_reset, d_update, act * reset], axis=1).astype(BF)
    g_msg = nt(d_in, w_input).astype(BF)
    grad_states = grad * update + nt(d_hid, w_hidden)
    return d_in, d_hid, g_msg, grad_states


def edge_front(features, w_edge_in, b_edge_in):
    return tn(features, w_edge_in) + b_edge_in


def local_kernel(sect_ref, *refs):
    ins, refs = refs[:14], refs[14:]
    (send_ref, final_ref, base_ref, grad_t_ref, pairs_out_ref), refs = refs[:5], refs[5:]
    held, refs = refs[:14], refs[14:]
    u_one, u_two, d_all, d_own, pair_h, rows_scr, small_scr, q_scr, sems, w_sems = refs
    (
        source_ref,
        target_ref,
        live_ref,
        feat_ref,
        w_ein_ref,
        b_ein_ref,
        states_ref,
        b_mat_ref,
        w_in_ref,
        w_hid_ref,
        b_in_ref,
        b_hid_ref,
        cot_ref,
        w_ref,
    ) = held
    sect = sect_ref[0]
    chunk = H * H // W_PARTS
    copies = [
        pltpu.make_async_copy(ins[at], held[at], sems.at[at]) for at in range(13)
    ]

    def w_copy(at):
        cols = pl.ds(at * chunk, chunk)
        return pltpu.make_async_copy(ins[13].at[:, cols], w_ref.at[:, cols], w_sems.at[at])

    for copy in copies:
        copy.start()
    for at in range(W_PARTS):
        w_copy(at).start()
    for copy in copies:
        copy.wait()

    states0 = states_ref[...]
    w_ein = w_ein_ref[...]
    b_ein = b_ein_ref[...]
    b_mat = b_mat_ref[...]
    source = source_ref[...]
    target = target_ref[...]
    live = live_ref[...]
    pair = jnp.where(live > 0, source * ATOMS + target, -1)

    slot = lax.broadcasted_iota(jnp.int32, (PAIRS, H), 0)

    def hot_pairs(first, second):
        return jnp.concatenate(
            [jnp.where(slot == row, 1.0, 0.0).astype(BF) for row in (first, second)], axis=1
        )

    def pair_rows(mol):
        pre = edge_front(feat_ref[:, mol * EPM : (mol + 1) * EPM], w_ein, b_ein)
        hidden = (pre * sigmoid(pre)).astype(BF)
        hot = hot_pairs(pair[2 * mol : 2 * mol + 1, :], pair[2 * mol + 1 : 2 * mol + 2, :])
        pair_h[mol * PAIRS : (mol + 1) * PAIRS, :] = nn(hot, hidden).astype(BF)

    for mol in range(MB):
        pair_rows(mol)

    node = lax.broadcasted_iota(jnp.int32, (NODES, H), 0)
    hot_t, hot_s = [], []
    for row in range(8):
        shift = (row // 2) * ATOMS
        keep = live[row : row + 1, :] > 0
        t_at = jnp.where(keep, target[row : row + 1, :] + shift, -1)
        s_at = source[row : row + 1, :] + shift
        hot_t.append(jnp.where(node == t_at, 1.0, 0.0).astype(BF))
        hot_s.append(jnp.where(node == s_at, 1.0, 0.0).astype(BF))
    hot_t = jnp.concatenate(hot_t, axis=1)
    hot_s = jnp.concatenate(hot_s, axis=1)
    adj = nt(hot_t, hot_s).astype(BF)
    adj_t = nt(hot_s, hot_t).astype(BF)

    def spread(states, u_ref, wait):
        def step(at):
            base = pl.multiple_of(at * 4 * H, 4 * H)
            four = [w_ref[:, pl.ds(base + q * H, H)] for q in range(4)]
            out = nt(states, jnp.concatenate(four, axis=0))
            for q in range(4):
                u_ref[pl.ds(at * 4 + q, NODES, stride=GAP), :] = out[:, q * H : (q + 1) * H]

        if wait:
            for at in range(W_PARTS):
                w_copy(at).wait()
            for at in range(32):
                step(at)
        else:

            def body(at, carry):
                step(at)
                return carry

            lax.fori_loop(0, 32, body, 0, unroll=True)

    def u_rows(u_ref, at):
        return u_ref[pl.ds(at * GAP, H), :].astype(BF)

    def gather(states, u_ref):
        side = fine_right(nt, states, b_mat)
        extra = fine_right(nn, adj, side)
        parts = []
        for mol in range(MB):

            def body(at, total, mol=mol):
                first = mol * ATOMS + at * 4
                left = jnp.concatenate(
                    [
                        pair_h[pl.ds(pl.multiple_of((first + q) * ATOMS, ATOMS), ATOMS), :]
                        for q in range(4)
                    ],
                    axis=1,
                )
                right = jnp.concatenate([u_rows(u_ref, first + q) for q in range(4)], axis=1)
                return total + nt(left, right)

            parts.append(lax.fori_loop(0, 8, body, jnp.zeros((ATOMS, H), F32), unroll=True))
        return (jnp.concatenate(parts, axis=0) + extra).astype(BF)

    w_in = w_in_ref[...]
    w_hid = w_hid_ref[...]
    b_in = jnp.concatenate([b_in_ref[part : part + 1, :] for part in range(3)], axis=1)
    b_hid = jnp.concatenate([b_hid_ref[part : part + 1, :] for part in range(3)], axis=1)

    spread(states0, u_one, True)
    msg_one = gather(states0, u_one)
    *parts_one, renewed = gate_forward(msg_one, states0, w_in, w_hid, b_in, b_hid)
    states1 = renewed.astype(BF)
    spread(states1, u_two, False)
    msg_two = gather(states1, u_two)
    *parts_two, final = gate_forward(msg_two, states1, w_in, w_hid, b_in, b_hid)
    own_rows = pl.ds(pl.multiple_of(sect * ATOMS, ATOMS), ATOMS)
    rows_scr[...] = final
    final_ref[...] = rows_scr[own_rows, :]

    d_in2, d_hid2, g_two, back_one = gate_backward(cot_ref[...], states1, parts_two, w_in, w_hid)
    g_two_t = g_two.astype(F32).T.astype(BF)

    for mol in range(MB):
        left = g_two_t[:, mol * ATOMS : (mol + 1) * ATOMS]

        def body(at, carry, mol=mol, left=left):
            first = mol * ATOMS + at * 4
            right = jnp.concatenate(
                [
                    pair_h[pl.ds(pl.multiple_of((first + q) * ATOMS, ATOMS), ATOMS), :]
                    for q in range(4)
                ],
                axis=1,
            )
            out = nn(left, right)
            for q in range(4):
                d_all[pl.ds(first + q, H, stride=GAP), :] = out[:, q * H : (q + 1) * H]
            return carry

        lax.fori_loop(0, 8, body, 0, unroll=True)

    def back_body(at, total):
        base = pl.multiple_of(at * 4 * H, 4 * H)
        left = jnp.concatenate(
            [d_all[pl.ds((at * 4 + q) * GAP, NODES), :].astype(BF) for q in range(4)], axis=1
        )
        right = jnp.concatenate([w_ref[:, pl.ds(base + q * H, H)] for q in range(4)], axis=0)
        return total + nn(left, right)

    back_msg = lax.fori_loop(0, 32, back_body, jnp.zeros((NODES, H), F32), unroll=True)
    share = nn(adj_t, g_two)
    grad_one = back_one + back_msg + fine(nn, share, b_mat)

    d_in1, d_hid1, g_one, back_zero = gate_backward(grad_one, states0, parts_one, w_in, w_hid)
    rows_scr[...] = g_one.astype(F32).T
    g_one_t = rows_scr[...].astype(BF)
    g_one_own = rows_scr[own_rows, :].astype(BF)

    for mol in range(MB):
        left = g_one_own[:, mol * ATOMS : (mol + 1) * ATOMS]

        def body(at, carry, mol=mol, left=left):
            first = mol * ATOMS + at * 4
            right = jnp.concatenate(
                [
                    pair_h[pl.ds(pl.multiple_of((first + q) * ATOMS, ATOMS), ATOMS), :]
                    for q in range(4)
                ],
                axis=1,
            )
            out = nn(left, right)
            for q in range(4):
                d_own[pl.ds(first + q, OWN, stride=GAP), :] = out[:, q * H : (q + 1) * H]
            return carry

        lax.fori_loop(0, 8, body, 0, unroll=True)

    both_t = jnp.concatenate([states0.astype(F32).T, states1.astype(F32).T], axis=1).astype(BF)

    def own_body(at, carry):
        right = jnp.concatenate(
            [
                jnp.concatenate(
                    [
                        d_own[pl.ds((at * 2 + q) * GAP, NODES), :].astype(BF),
                        d_all[pl.ds((sect * OWN + at * 2 + q) * GAP, NODES), :].astype(BF),
                    ],
                    axis=0,
                )
                for q in range(2)
            ],
            axis=1,
        )
        out = nn(both_t, right).astype(BF)
        for q in range(2):
            send_ref[at * 2 + q, 0:H, :] = out[:, q * H : (q + 1) * H]
        return carry

    lax.fori_loop(0, OWN // 2, own_body, 0, unroll=True)

    rows_scr[...] = g_one.astype(F32)
    g1 = rows_scr[own_rows, :].astype(BF)
    rows_scr[...] = g_two.astype(F32)
    g2 = rows_scr[own_rows, :].astype(BF)
    g_both = jnp.concatenate([g1, g2], axis=1)

    def q_body(at, carry):
        first = sect * ATOMS + at * 2
        right = jnp.concatenate(
            [
                jnp.concatenate([u_rows(u_one, first + q), u_rows(u_two, first + q)], axis=0)
                for q in range(2)
            ],
            axis=1,
        )
        out = nn(g_both, right).astype(BF)
        for q in range(2):
            q_scr[pl.ds(pl.multiple_of((at * 2 + q) * ATOMS, ATOMS), ATOMS), :] = out[
                :, q * H : (q + 1) * H
            ]
        return carry

    lax.fori_loop(0, 16, q_body, 0, unroll=True)
    own_cols = pl.ds(pl.multiple_of(sect * EPM, EPM), EPM)
    feat_own = feat_ref[:, own_cols]
    pre_own = edge_front(feat_own, w_ein, b_ein)
    sig = sigmoid(pre_own)
    slope = sig * (1.0 + pre_own * (1.0 - sig))
    rows_scr[0:8, :] = pair.astype(F32)
    pair_own = rows_scr[pl.ds(sect * 2, 2), :].astype(jnp.int32)
    hot = hot_pairs(pair_own[0:1, :], pair_own[1:2, :])
    g_pre = tn(hot, q_scr[...]) * slope

    g_share_t = nn(g_one_t, adj), nn(g_two_t, adj)
    grad_b_out = fine_left(nn, g_share_t[0], states0) + fine_left(nn, g_share_t[1], states1)
    rows_scr[...] = grad_b_out
    small_scr[0:32, :] = rows_scr[own_rows, :]
    both_rows = jnp.concatenate(
        [msg_one.astype(F32).T, msg_two.astype(F32).T], axis=1
    )
    d_in_both = jnp.concatenate([d_in1, d_in2], axis=0)
    d_hid_both = jnp.concatenate([d_hid1, d_hid2], axis=0)
    for at, (rows_t, d_both) in enumerate(
        ((both_rows, d_in_both), (both_t.astype(F32), d_hid_both))
    ):
        rows_scr[...] = rows_t[:, :H]
        first = rows_scr[own_rows, :]
        rows_scr[...] = rows_t[:, H:]
        left = jnp.concatenate([first, rows_scr[own_rows, :]], axis=1).astype(BF)
        out = nn(left, d_both)
        for part in range(3):
            row = 32 + at * 96 + part * 32
            small_scr[row : row + 32, :] = out[:, part * H : (part + 1) * H]
    small_scr[224:240, :] = fine_right(nn, feat_own, g_pre)
    small_scr[240:256, :] = jnp.zeros((16, H), F32)
    small_scr[240:241, :] = jnp.sum(g_pre, axis=0, keepdims=True)
    for at, pair_d in enumerate(((d_in1, d_in2), (d_hid1, d_hid2))):
        for part in range(3):
            cols = slice(part * H, (part + 1) * H)
            rows_scr[...] = pair_d[0][:, cols].astype(F32) + pair_d[1][:, cols].astype(F32)
            row = 241 + at * 3 + part
            small_scr[row : row + 1, :] = jnp.sum(rows_scr[own_rows, :], axis=0, keepdims=True)
    for at in range(GROUP):
        send_ref[at, H:ROWS, :] = small_scr[at * SMALL : (at + 1) * SMALL, :].astype(BF)

    rows_scr[...] = back_zero + fine(nn, nn(adj_t, g_one), b_mat)
    base_ref[...] = rows_scr[own_rows, :]
    grad_t_ref[...] = g_one_t
    pairs_out_ref[...] = pair_h[pl.ds(pl.multiple_of(sect * PAIRS, PAIRS), PAIRS), :]


def sum_kernel(place_ref, got_ref, out_ref, two):
    shift = place_ref[2]

    def body(at, total):
        return total + got_ref[at].astype(F32)

    total = lax.fori_loop(1, GROUP, body, got_ref[0].astype(F32), unroll=True)
    rows = total[:H].T
    for part in range(2):
        half_rows = rows[part * HALF : (part + 1) * HALF]
        two[part] = jnp.concatenate([half_rows, total[H:]], axis=0).astype(BF)

    def put(at, carry):
        out_ref[at] = two[jnp.bitwise_and(jnp.right_shift(at, shift), 1)]
        return carry

    lax.fori_loop(0, 2 * GROUP, put, 0, unroll=8)


def states_kernel(sect_ref, base_ref, grad_t_ref, pairs_ref, w_ref, out_ref, d_all, rows_scr):
    sect = sect_ref[0]
    rows_scr[...] = grad_t_ref[...].astype(F32).T
    own = rows_scr[pl.ds(pl.multiple_of(sect * ATOMS, ATOMS), ATOMS), :]
    left = own.T.astype(BF)
    gap = ATOMS + 1

    def body(at, carry):
        right = jnp.concatenate(
            [
                pairs_ref[pl.ds(pl.multiple_of((at * 4 + q) * ATOMS, ATOMS), ATOMS), :]
                for q in range(4)
            ],
            axis=1,
        )
        out = nn(left, right)
        for q in range(4):
            d_all[pl.ds(at * 4 + q, H, stride=gap), :] = out[:, q * H : (q + 1) * H]
        return carry

    lax.fori_loop(0, 8, body, 0, unroll=True)

    def back_body(at, total):
        base = pl.multiple_of(at * 4 * H, 4 * H)
        left = jnp.concatenate(
            [d_all[pl.ds((at * 4 + q) * gap, ATOMS), :].astype(BF) for q in range(4)], axis=1
        )
        right = jnp.concatenate([w_ref[:, pl.ds(base + q * H, H)] for q in range(4)], axis=0)
        return total + nn(left, right)

    out_ref[...] = lax.fori_loop(0, 32, back_body, base_ref[...], unroll=True)


def place_rows(place_ref, other_core, other_half, parts, out_hbm, stage, sem):
    core = jnp.bitwise_xor(place_ref[3], 1) if other_core else place_ref[3]
    copies = []
    for run, (ref, first) in enumerate(parts):
        bit = place_ref[run // 2]
        if other_half:
            bit = jnp.bitwise_xor(bit, 1)
        low, high = CUTS[run], CUTS[run + 1]
        half = low // GROUP
        at_col = (half * 2 + core) * (GROUP * H) + (low - half * GROUP) * H
        width = (high - low) * H
        for part in range(2):
            for dev in range(low, high):
                for row in range(part * 32, part * 32 + 32, 16):
                    stage[row : row + 16, dev * H : (dev + 1) * H] = ref[
                        dev - first, row : row + 16, :
                    ].astype(F32)
            copies.append(
                pltpu.make_async_copy(
                    stage.at[pl.ds(part * 32, 32), pl.ds(low * H, width)],
                    out_hbm.at[
                        pl.ds(pl.multiple_of(bit * HALF + part * 32, 32), 32),
                        pl.ds(pl.multiple_of(at_col, H), width),
                    ],
                    sem.at[len(copies)],
                )
            )
            copies[-1].start()
    for copy in copies:
        copy.wait()


def place_own(place_ref, near_ref, out_hbm, stage, sems):
    place_rows(place_ref, False, False, [(near_ref, 0)] * RUNS, out_hbm, stage, sems)


def place_core(
    place_ref,
    near_ref,
    far_ref,
    part_hbm,
    out_hbm,
    gb_ref,
    gi_ref,
    gh_ref,
    ge_ref,
    be_ref,
    bi_ref,
    bh_ref,
    small,
    stage,
    sems,
):
    del part_hbm
    place_rows(place_ref, True, False, [(far_ref, 0)] * RUNS, out_hbm, stage, sems)
    core = place_ref[3]
    for which, ref in ((core, near_ref), (1 - core, far_ref)):
        for half in range(2):
            base = (half * 2 + which) * (GROUP * SMALL)
            for dev in range(GROUP):
                at = pl.multiple_of(base + dev * SMALL, SMALL)
                small[pl.ds(at, SMALL), :] = ref[half * GROUP + dev, HALF:, :].astype(F32)
    misc = jnp.zeros((32, H), F32)
    for sect in range(MB):
        base = sect * GROUP * SMALL
        rows = slice(sect * 32, (sect + 1) * 32)
        gb_ref[rows, :] = small[base : base + 32, :]
        for part in range(3):
            cols = slice(part * H, (part + 1) * H)
            row = base + 32 + part * 32
            gi_ref[rows, cols] = small[row : row + 32, :]
            gh_ref[rows, cols] = small[row + 96 : row + 128, :]
        misc = misc + small[base + 224 : base + 256, :]
    ge_ref[...] = misc[0:16]
    be_ref[...] = misc[16:17]
    bi_ref[...] = misc[17:20]
    bh_ref[...] = misc[20:23]


def place_rest(other_core, place_ref, *refs):
    out_hbm, stage, sems = refs[RUNS + 1 :]
    parts = list(zip(refs[:RUNS], CUTS))
    place_rows(place_ref, other_core, True, parts, out_hbm, stage, sems)


VMEM_SPEC = pl.BlockSpec(memory_space=pltpu.VMEM)
SMEM_SPEC = pl.BlockSpec(memory_space=pltpu.SMEM)
ANY_SPEC = pl.BlockSpec(memory_space=pl.ANY)
BIG = 60 * 2**20
LOW = 8 * 2**20
shape = jax.ShapeDtypeStruct


def run_layers(sect, operands):
    return pl.pallas_call(
        local_kernel,
        out_shape=(
            shape((GROUP, ROWS, H), BF),
            shape((ATOMS, H), F32),
            shape((ATOMS, H), F32),
            shape((H, NODES), BF),
            shape((PAIRS, H), BF),
        ),
        in_specs=[SMEM_SPEC] + [ANY_SPEC] * 14,
        out_specs=(VMEM_SPEC,) * 5,
        scratch_shapes=[pltpu.VMEM(v.shape, v.dtype) for v in operands]
        + [
            pltpu.VMEM((NODES * GAP, H), F32),
            pltpu.VMEM((NODES * GAP, H), F32),
            pltpu.VMEM((H * GAP, H), F32),
            pltpu.VMEM((OWN * GAP, H), F32),
            pltpu.VMEM((MB * PAIRS, H), BF),
            pltpu.VMEM((NODES, H), F32),
            pltpu.VMEM((GROUP * SMALL, H), F32),
            pltpu.VMEM((PAIRS, H), BF),
            pltpu.SemaphoreType.DMA((13,)),
            pltpu.SemaphoreType.DMA((W_PARTS,)),
        ],
        compiler_params=pltpu.CompilerParams(vmem_limit_bytes=BIG),
        name="layers",
    )(sect, *operands)


def neighbours(axis, side):
    pairs = []
    for index in range(2 * GROUP):
        spot = [index % 4, index // 4 % 4, index // 16]
        step = 1 if spot[axis] % 2 == side else -1
        spot[axis] = (spot[axis] + step) % 4
        pairs.append((index, spot[2] * 16 + spot[1] * 4 + spot[0]))
    return pairs


def local(
    node_states,
    edge_features,
    edge_source,
    edge_target,
    edge_live,
    w_edge_in,
    b_edge_in,
    w_edge_out,
    b_edge_out,
    w_input,
    w_hidden,
    b_input,
    b_hidden,
    cotangent,
):
    core = lax.axis_index("core").astype(jnp.int32)
    sect = (lax.axis_index("zh") * 2 + core).astype(jnp.int32)
    sect = sect.reshape(1)
    dp = lax.axis_index("dp").astype(jnp.int32)
    zh = lax.axis_index("zh").astype(jnp.int32)
    place = jnp.stack([dp & 1, (dp >> 2) & 1, zh * 2, core])
    operands = [v.reshape(8, 128) for v in (edge_source, edge_target, edge_live)] + [
        edge_features,
        w_edge_in,
        b_edge_in.reshape(1, H),
        node_states,
        b_edge_out.reshape(H, H),
        w_input,
        w_hidden,
        b_input.reshape(3, H),
        b_hidden.reshape(3, H),
        cotangent,
        w_edge_out,
    ]

    send, final, base, grad_t, pairs = run_layers(sect, operands)
    grad_states = pl.pallas_call(
        states_kernel,
        out_shape=shape((ATOMS, H), F32),
        in_specs=[SMEM_SPEC] + [VMEM_SPEC] * 4,
        out_specs=VMEM_SPEC,
        scratch_shapes=[pltpu.VMEM((H * (ATOMS + 1), H), F32), pltpu.VMEM((NODES, H), F32)],
        compiler_params=pltpu.CompilerParams(vmem_limit_bytes=LOW),
        cost_estimate=pl.CostEstimate(
            flops=2 * ATOMS * H * H * H, bytes_accessed=2 * H * H * H, transcendentals=0
        ),
        name="states_back",
    )(sect, base, grad_t, pairs, w_edge_out)
    got = lax.all_to_all(send, "dp", split_axis=0, concat_axis=0)
    got, grad_states = lax.optimization_barrier((got, grad_states))
    piece = pl.pallas_call(
        sum_kernel,
        out_shape=shape((2 * GROUP, HALF + SMALL, H), BF),
        in_specs=[SMEM_SPEC, VMEM_SPEC],
        out_specs=VMEM_SPEC,
        scratch_shapes=[pltpu.VMEM((2, HALF + SMALL, H), BF)],
        compiler_params=pltpu.CompilerParams(vmem_limit_bytes=LOW),
        name="sum_parts",
    )(place, got)
    near = lax.all_to_all(piece, ("zh", "dp"), split_axis=0, concat_axis=0)
    far = lax.ppermute(near, "core", [(0, 1), (1, 0)])
    rest = [
        lax.ppermute(
            near[CUTS[run] : CUTS[run + 1], :HALF], ("zh", "dp"), neighbours(run // 2, run % 2)
        )
        for run in range(RUNS)
    ]
    stage = [pltpu.VMEM((HALF, 2 * GROUP * H), F32), pltpu.SemaphoreType.DMA((2 * RUNS,))]
    params = pltpu.CompilerParams(vmem_limit_bytes=LOW)
    cost = pl.CostEstimate(flops=0, bytes_accessed=6 * 2**20, transcendentals=0)
    whole = shape((H, H * H), F32)
    out = pl.pallas_call(
        place_own,
        out_shape=whole,
        in_specs=[SMEM_SPEC, VMEM_SPEC],
        out_specs=ANY_SPEC,
        scratch_shapes=stage,
        compiler_params=params,
        cost_estimate=cost,
        name="place_own",
    )(place, near)
    out, grad_b_out, grad_w_in, grad_w_hid, grad_ein, grad_bein, grad_bin, grad_bhid = (
        pl.pallas_call(
            place_core,
            out_shape=(
                whole,
                shape((H, H), F32),
                shape((H, 3 * H), F32),
                shape((H, 3 * H), F32),
                shape((16, H), F32),
                shape((1, H), F32),
                shape((3, H), F32),
                shape((3, H), F32),
            ),
            in_specs=[SMEM_SPEC, VMEM_SPEC, VMEM_SPEC, ANY_SPEC],
            out_specs=(ANY_SPEC,) + (VMEM_SPEC,) * 7,
            scratch_shapes=[pltpu.VMEM((MB * GROUP * SMALL, H), F32)] + stage,
            input_output_aliases={3: 0},
            compiler_params=params,
            cost_estimate=cost,
            name="place_core",
        )(place, near, far, out)
    )
    rest, out = lax.optimization_barrier((rest, out))
    far_rest = [lax.ppermute(part, "core", [(0, 1), (1, 0)]) for part in rest]
    for other_core, parts in ((False, rest), (True, far_rest)):
        out = pl.pallas_call(
            functools.partial(place_rest, other_core),
            out_shape=whole,
            in_specs=[SMEM_SPEC] + [VMEM_SPEC] * RUNS + [ANY_SPEC],
            out_specs=ANY_SPEC,
            scratch_shapes=stage,
            input_output_aliases={RUNS + 1: 0},
            compiler_params=params,
            cost_estimate=cost,
            name="place_rest",
        )(place, *parts, out)
    grad_w_out = out
    return (
        final,
        grad_states,
        grad_ein,
        grad_bein.reshape(H),
        grad_w_out,
        grad_b_out.reshape(H * H),
        grad_w_in,
        grad_w_hid,
        grad_bin.reshape(3 * H),
        grad_bhid.reshape(3 * H),
    )


def solution(mesh):
    wide = Mesh(mesh.devices.reshape(2, 2, GROUP), ("zh", "core", "dp"))
    split = P(("dp", "zh", "core"), None)
    in_specs = (
        P("dp", None),
        P(None, "dp"),
        P("dp"),
        P("dp"),
        P("dp"),
        P(),
        P(),
        P(),
        P(),
        P(),
        P(),
        P(),
        P(),
        P("dp", None),
    )
    out_specs = (split, split, P(), P(), P(), P(), P(), P(), P(), P())
    return jax.shard_map(local, mesh=wide, in_specs=in_specs, out_specs=out_specs, check_vma=False)
```

```python
import functools

import jax
import jax.numpy as jnp
from jax import lax
from jax.experimental import pallas as pl
from jax.experimental.pallas import tpu as pltpu
from jax.sharding import Mesh
from jax.sharding import PartitionSpec as P

H = 128
ATOMS = 32
EPM = 256
MB = 4
NODES = MB * ATOMS
PAIRS = ATOMS * ATOMS
OWN = H // MB
GAP = 129
ROWS = 136
SMALL = 8
GROUP = 32
CLASS = 8
AXES = 3
W_PARTS = 1
BF = jnp.bfloat16
F32 = jnp.float32


def spot_of(dp):
    return dp % 4, dp // 4 % 4, dp // 16


def slot_of(dp):
    x, y, z = spot_of(dp)
    return ((x + z) % 2 * 2 + (y + z) % 2) * CLASS + z * 4 + y // 2 * 2 + x // 2


DP_AT = sorted(range(GROUP), key=slot_of)


def nn(left, right):
    return jnp.dot(left, right, preferred_element_type=F32)


def nt(left, right):
    return lax.dot_general(left, right, (((1,), (1,)), ((), ())), preferred_element_type=F32)


def tn(left, right):
    return lax.dot_general(left, right, (((0,), (0,)), ((), ())), preferred_element_type=F32)


def halves(value):
    high = value.astype(BF)
    return high, (value - high.astype(F32)).astype(BF)


def fine(dot, left, right):
    lh, ll = halves(left)
    rh, rl = halves(right)
    return dot(lh, rh) + (dot(lh, rl) + dot(ll, rh))


def fine_left(dot, left, right):
    lh, ll = halves(left)
    return dot(lh, right) + dot(ll, right)


def fine_right(dot, left, right):
    rh, rl = halves(right)
    return dot(left, rh) + dot(left, rl)


def sigmoid(value):
    return 0.5 * jnp.tanh(0.5 * value) + 0.5


def gate_forward(message, states, w_input, w_hidden, b_input, b_hidden):
    from_msg = nn(message, w_input) + b_input
    from_state = nn(states, w_hidden) + b_hidden
    reset = sigmoid(from_msg[:, :H] + from_state[:, :H])
    update = sigmoid(from_msg[:, H : 2 * H] + from_state[:, H : 2 * H])
    state_cand = from_state[:, 2 * H :]
    candidate = jnp.tanh(from_msg[:, 2 * H :] + reset * state_cand)
    renewed = (1.0 - update) * candidate + update * states.astype(F32)
    return reset, update, candidate, state_cand, renewed


def gate_backward(grad, states, parts, w_input, w_hidden):
    reset, update, candidate, state_cand = parts
    act = grad * (1.0 - update) * (1.0 - candidate * candidate)
    d_reset = act * state_cand * reset * (1.0 - reset)
    d_update = grad * (states.astype(F32) - candidate) * update * (1.0 - update)
    d_in = jnp.concatenate([d_reset, d_update, act], axis=1).astype(BF)
    d_hid = jnp.concatenate([d_reset, d_update, act * reset], axis=1).astype(BF)
    g_msg = nt(d_in, w_input).astype(BF)
    grad_states = grad * update + nt(d_hid, w_hidden)
    return d_in, d_hid, g_msg, grad_states


def edge_front(features, w_edge_in, b_edge_in):
    return tn(features, w_edge_in) + b_edge_in


def local_kernel(sect_ref, *refs):
    ins, refs = refs[:14], refs[14:]
    (send_ref, final_ref, base_ref, grad_t_ref, pairs_out_ref), refs = refs[:5], refs[5:]
    held, refs = refs[:14], refs[14:]
    u_one, u_two, d_all, d_own, pair_h, rows_scr, small_scr, q_scr, sems, w_sems = refs
    (
        source_ref,
        target_ref,
        live_ref,
        feat_ref,
        w_ein_ref,
        b_ein_ref,
        states_ref,
        b_mat_ref,
        w_in_ref,
        w_hid_ref,
        b_in_ref,
        b_hid_ref,
        cot_ref,
        w_ref,
    ) = held
    sect = sect_ref[0]
    chunk = H * H // W_PARTS
    copies = [
        pltpu.make_async_copy(ins[at], held[at], sems.at[at]) for at in range(13)
    ]

    def w_copy(at):
        cols = pl.ds(at * chunk, chunk)
        return pltpu.make_async_copy(ins[13].at[:, cols], w_ref.at[:, cols], w_sems.at[at])

    for copy in copies:
        copy.start()
    for at in range(W_PARTS):
        w_copy(at).start()
    for copy in copies:
        copy.wait()

    states0 = states_ref[...]
    w_ein = w_ein_ref[...]
    b_ein = b_ein_ref[...]
    b_mat = b_mat_ref[...]
    source = source_ref[...]
    target = target_ref[...]
    live = live_ref[...]
    pair = jnp.where(live > 0, source * ATOMS + target, -1)

    slot = lax.broadcasted_iota(jnp.int32, (PAIRS, H), 0)

    def hot_pairs(first, second):
        return jnp.concatenate(
            [jnp.where(slot == row, 1.0, 0.0).astype(BF) for row in (first, second)], axis=1
        )

    def pair_rows(mol):
        pre = edge_front(feat_ref[:, mol * EPM : (mol + 1) * EPM], w_ein, b_ein)
        hidden = (pre * sigmoid(pre)).astype(BF)
        hot = hot_pairs(pair[2 * mol : 2 * mol + 1, :], pair[2 * mol + 1 : 2 * mol + 2, :])
        pair_h[mol * PAIRS : (mol + 1) * PAIRS, :] = nn(hot, hidden).astype(BF)

    for mol in range(MB):
        pair_rows(mol)

    node = lax.broadcasted_iota(jnp.int32, (NODES, H), 0)
    hot_t, hot_s = [], []
    for row in range(8):
        shift = (row // 2) * ATOMS
        keep = live[row : row + 1, :] > 0
        t_at = jnp.where(keep, target[row : row + 1, :] + shift, -1)
        s_at = source[row : row + 1, :] + shift
        hot_t.append(jnp.where(node == t_at, 1.0, 0.0).astype(BF))
        hot_s.append(jnp.where(node == s_at, 1.0, 0.0).astype(BF))
    hot_t = jnp.concatenate(hot_t, axis=1)
    hot_s = jnp.concatenate(hot_s, axis=1)
    adj = nt(hot_t, hot_s).astype(BF)
    adj_t = nt(hot_s, hot_t).astype(BF)

    def spread(states, u_ref, wait):
        def step(at):
            base = pl.multiple_of(at * 4 * H, 4 * H)
            four = [w_ref[:, pl.ds(base + q * H, H)] for q in range(4)]
            out = nt(states, jnp.concatenate(four, axis=0))
            for q in range(4):
                u_ref[pl.ds(at * 4 + q, NODES, stride=GAP), :] = out[:, q * H : (q + 1) * H]

        if wait:
            for at in range(W_PARTS):
                w_copy(at).wait()
            for at in range(32):
                step(at)
        else:

            def body(at, carry):
                step(at)
                return carry

            lax.fori_loop(0, 32, body, 0, unroll=True)

    def u_rows(u_ref, at):
        return u_ref[pl.ds(at * GAP, H), :].astype(BF)

    def gather(states, u_ref):
        side = fine_right(nt, states, b_mat)
        extra = fine_right(nn, adj, side)
        parts = []
        for mol in range(MB):

            def body(at, total, mol=mol):
                first = mol * ATOMS + at * 4
                left = jnp.concatenate(
                    [
                        pair_h[pl.ds(pl.multiple_of((first + q) * ATOMS, ATOMS), ATOMS), :]
                        for q in range(4)
                    ],
                    axis=1,
                )
                right = jnp.concatenate([u_rows(u_ref, first + q) for q in range(4)], axis=1)
                return total + nt(left, right)

            parts.append(lax.fori_loop(0, 8, body, jnp.zeros((ATOMS, H), F32), unroll=True))
        return (jnp.concatenate(parts, axis=0) + extra).astype(BF)

    w_in = w_in_ref[...]
    w_hid = w_hid_ref[...]
    b_in = jnp.concatenate([b_in_ref[part : part + 1, :] for part in range(3)], axis=1)
    b_hid = jnp.concatenate([b_hid_ref[part : part + 1, :] for part in range(3)], axis=1)

    spread(states0, u_one, True)
    msg_one = gather(states0, u_one)
    *parts_one, renewed = gate_forward(msg_one, states0, w_in, w_hid, b_in, b_hid)
    states1 = renewed.astype(BF)
    spread(states1, u_two, False)
    msg_two = gather(states1, u_two)
    *parts_two, final = gate_forward(msg_two, states1, w_in, w_hid, b_in, b_hid)
    own_rows = pl.ds(pl.multiple_of(sect * ATOMS, ATOMS), ATOMS)
    rows_scr[...] = final
    final_ref[...] = rows_scr[own_rows, :]

    d_in2, d_hid2, g_two, back_one = gate_backward(cot_ref[...], states1, parts_two, w_in, w_hid)
    g_two_t = g_two.astype(F32).T.astype(BF)

    for mol in range(MB):
        left = g_two_t[:, mol * ATOMS : (mol + 1) * ATOMS]

        def body(at, carry, mol=mol, left=left):
            first = mol * ATOMS + at * 4
            right = jnp.concatenate(
                [
                    pair_h[pl.ds(pl.multiple_of((first + q) * ATOMS, ATOMS), ATOMS), :]
                    for q in range(4)
                ],
                axis=1,
            )
            out = nn(left, right)
            for q in range(4):
                d_all[pl.ds(first + q, H, stride=GAP), :] = out[:, q * H : (q + 1) * H]
            return carry

        lax.fori_loop(0, 8, body, 0, unroll=True)

    def back_body(at, total):
        base = pl.multiple_of(at * 4 * H, 4 * H)
        left = jnp.concatenate(
            [d_all[pl.ds((at * 4 + q) * GAP, NODES), :].astype(BF) for q in range(4)], axis=1
        )
        right = jnp.concatenate([w_ref[:, pl.ds(base + q * H, H)] for q in range(4)], axis=0)
        return total + nn(left, right)

    back_msg = lax.fori_loop(0, 32, back_body, jnp.zeros((NODES, H), F32), unroll=True)
    share = nn(adj_t, g_two)
    grad_one = back_one + back_msg + fine(nn, share, b_mat)

    d_in1, d_hid1, g_one, back_zero = gate_backward(grad_one, states0, parts_one, w_in, w_hid)
    rows_scr[...] = g_one.astype(F32).T
    g_one_t = rows_scr[...].astype(BF)
    g_one_own = rows_scr[own_rows, :].astype(BF)

    for mol in range(MB):
        left = g_one_own[:, mol * ATOMS : (mol + 1) * ATOMS]

        def body(at, carry, mol=mol, left=left):
            first = mol * ATOMS + at * 4
            right = jnp.concatenate(
                [
                    pair_h[pl.ds(pl.multiple_of((first + q) * ATOMS, ATOMS), ATOMS), :]
                    for q in range(4)
                ],
                axis=1,
            )
            out = nn(left, right)
            for q in range(4):
                d_own[pl.ds(first + q, OWN, stride=GAP), :] = out[:, q * H : (q + 1) * H]
            return carry

        lax.fori_loop(0, 8, body, 0, unroll=True)

    both_t = jnp.concatenate([states0.astype(F32).T, states1.astype(F32).T], axis=1).astype(BF)

    for at in range(OWN // 2):
        right = jnp.concatenate(
            [
                jnp.concatenate(
                    [
                        d_own[pl.ds((at * 2 + q) * GAP, NODES), :].astype(BF),
                        d_all[pl.ds((sect * OWN + at * 2 + q) * GAP, NODES), :].astype(BF),
                    ],
                    axis=0,
                )
                for q in range(2)
            ],
            axis=1,
        )
        out = nn(both_t, right).astype(BF)
        for q in range(2):
            send_ref[DP_AT[at * 2 + q], 0:H, :] = out[:, q * H : (q + 1) * H]

    rows_scr[...] = g_one.astype(F32)
    g1 = rows_scr[own_rows, :].astype(BF)
    rows_scr[...] = g_two.astype(F32)
    g2 = rows_scr[own_rows, :].astype(BF)
    g_both = jnp.concatenate([g1, g2], axis=1)

    def q_body(at, carry):
        first = sect * ATOMS + at * 2
        right = jnp.concatenate(
            [
                jnp.concatenate([u_rows(u_one, first + q), u_rows(u_two, first + q)], axis=0)
                for q in range(2)
            ],
            axis=1,
        )
        out = nn(g_both, right).astype(BF)
        for q in range(2):
            q_scr[pl.ds(pl.multiple_of((at * 2 + q) * ATOMS, ATOMS), ATOMS), :] = out[
                :, q * H : (q + 1) * H
            ]
        return carry

    lax.fori_loop(0, 16, q_body, 0, unroll=True)
    own_cols = pl.ds(pl.multiple_of(sect * EPM, EPM), EPM)
    feat_own = feat_ref[:, own_cols]
    pre_own = edge_front(feat_own, w_ein, b_ein)
    sig = sigmoid(pre_own)
    slope = sig * (1.0 + pre_own * (1.0 - sig))
    rows_scr[0:8, :] = pair.astype(F32)
    pair_own = rows_scr[pl.ds(sect * 2, 2), :].astype(jnp.int32)
    hot = hot_pairs(pair_own[0:1, :], pair_own[1:2, :])
    g_pre = tn(hot, q_scr[...]) * slope

    g_share_t = nn(g_one_t, adj), nn(g_two_t, adj)
    grad_b_out = fine_left(nn, g_share_t[0], states0) + fine_left(nn, g_share_t[1], states1)
    rows_scr[...] = grad_b_out
    small_scr[0:32, :] = rows_scr[own_rows, :]
    both_rows = jnp.concatenate(
        [msg_one.astype(F32).T, msg_two.astype(F32).T], axis=1
    )
    d_in_both = jnp.concatenate([d_in1, d_in2], axis=0)
    d_hid_both = jnp.concatenate([d_hid1, d_hid2], axis=0)
    for at, (rows_t, d_both) in enumerate(
        ((both_rows, d_in_both), (both_t.astype(F32), d_hid_both))
    ):
        rows_scr[...] = rows_t[:, :H]
        first = rows_scr[own_rows, :]
        rows_scr[...] = rows_t[:, H:]
        left = jnp.concatenate([first, rows_scr[own_rows, :]], axis=1).astype(BF)
        out = nn(left, d_both)
        for part in range(3):
            row = 32 + at * 96 + part * 32
            small_scr[row : row + 32, :] = out[:, part * H : (part + 1) * H]
    small_scr[224:240, :] = fine_right(nn, feat_own, g_pre)
    small_scr[240:256, :] = jnp.zeros((16, H), F32)
    small_scr[240:241, :] = jnp.sum(g_pre, axis=0, keepdims=True)
    for at, pair_d in enumerate(((d_in1, d_in2), (d_hid1, d_hid2))):
        for part in range(3):
            cols = slice(part * H, (part + 1) * H)
            rows_scr[...] = pair_d[0][:, cols].astype(F32) + pair_d[1][:, cols].astype(F32)
            row = 241 + at * 3 + part
            small_scr[row : row + 1, :] = jnp.sum(rows_scr[own_rows, :], axis=0, keepdims=True)
    for at in range(GROUP):
        send_ref[DP_AT[at], H:ROWS, :] = small_scr[at * SMALL : (at + 1) * SMALL, :].astype(BF)

    rows_scr[...] = back_zero + fine(nn, nn(adj_t, g_one), b_mat)
    base_ref[...] = rows_scr[own_rows, :]
    grad_t_ref[...] = g_one_t
    pairs_out_ref[...] = pair_h[pl.ds(pl.multiple_of(sect * PAIRS, PAIRS), PAIRS), :]


def sum_kernel(got_ref, out_ref):
    def body(at, total):
        return total + got_ref[at].astype(F32)

    total = lax.fori_loop(1, GROUP, body, got_ref[0].astype(F32), unroll=True)
    piece = jnp.concatenate([total[:H].T, total[H:]], axis=0).astype(BF)

    for at in range(2 * CLASS):
        out_ref[at] = piece


def states_kernel(sect_ref, base_ref, grad_t_ref, pairs_ref, w_ref, out_ref, d_all, rows_scr):
    sect = sect_ref[0]
    rows_scr[...] = grad_t_ref[...].astype(F32).T
    own = rows_scr[pl.ds(pl.multiple_of(sect * ATOMS, ATOMS), ATOMS), :]
    left = own.T.astype(BF)
    gap = ATOMS + 1

    def body(at, carry):
        right = jnp.concatenate(
            [
                pairs_ref[pl.ds(pl.multiple_of((at * 4 + q) * ATOMS, ATOMS), ATOMS), :]
                for q in range(4)
            ],
            axis=1,
        )
        out = nn(left, right)
        for q in range(4):
            d_all[pl.ds(at * 4 + q, H, stride=gap), :] = out[:, q * H : (q + 1) * H]
        return carry

    lax.fori_loop(0, 8, body, 0, unroll=True)

    def back_body(at, total):
        base = pl.multiple_of(at * 4 * H, 4 * H)
        left = jnp.concatenate(
            [d_all[pl.ds((at * 4 + q) * gap, ATOMS), :].astype(BF) for q in range(4)], axis=1
        )
        right = jnp.concatenate([w_ref[:, pl.ds(base + q * H, H)] for q in range(4)], axis=0)
        return total + nn(left, right)

    out_ref[...] = lax.fori_loop(0, 32, back_body, base_ref[...], unroll=True)


def place_rows(place_ref, parts, out_hbm, stage, sem):
    copies = []
    for part, (ref, other_core, change) in enumerate(parts):
        core, kind = place_of(place_ref, other_core, change)
        for half in range(2):
            at_col = ((half * 2 + core) * GROUP + kind * CLASS) * H
            low = (part * 2 + half) * CLASS * H
            cols = pl.ds(low, CLASS * H)
            for dev in range(CLASS):
                for row in range(0, H, 16):
                    stage[row : row + 16, low + dev * H : low + (dev + 1) * H] = ref[
                        half * CLASS + dev, row : row + 16, :
                    ].astype(F32)
            copies.append(
                pltpu.make_async_copy(
                    stage.at[:, cols],
                    out_hbm.at[:, pl.ds(pl.multiple_of(at_col, CLASS * H), CLASS * H)],
                    sem.at[len(copies)],
                )
            )
            copies[-1].start()
    return copies


def place_of(place_ref, other_core, change):
    core, kind = place_ref[0], place_ref[1]
    return (1 - core if other_core else core), jnp.bitwise_xor(kind, change)


CHANGES = (2, 1, 3)


def place_own(place_ref, near_ref, far_ref, out_hbm, stage, sems):
    parts = [(near_ref, False, 0), (far_ref, True, 0)]
    for copy in place_rows(place_ref, parts, out_hbm, stage, sems):
        copy.wait()


def place_rest(place_ref, *refs):
    out_hbm, stage, sems = refs[AXES + 1 :]
    parts = [(ref, False, change) for ref, change in zip(refs, CHANGES)]
    for copy in place_rows(place_ref, parts, out_hbm, stage, sems):
        copy.wait()


def place_last(place_ref, near_ref, far_ref, *refs):
    rest, far_rest, refs = refs[:AXES], refs[AXES : 2 * AXES], refs[2 * AXES + 1 :]
    out_hbm, *ends = refs[:8]
    stage, sems, small, gb, gi, gh, ge, be, bi, bh, end_sems = refs[8:]
    own = [(near_ref, False, 0), (far_ref, True, 0)]
    own += [(ref, False, change) for ref, change in zip(rest, CHANGES)]
    last = [(ref, True, change) for ref, change in zip(far_rest, CHANGES)]
    copies = place_rows(place_ref, last, out_hbm, stage, sems)
    for ref, other_core, change in own + last:
        core, kind = place_of(place_ref, other_core, change)
        for at in range(2 * CLASS):
            block = ((at // CLASS) * 2 + core) * GROUP + kind * CLASS + at % CLASS
            row = pl.multiple_of(block * SMALL, SMALL)
            small[pl.ds(row, SMALL), :] = ref[at, H:ROWS, :].astype(F32)
    misc = jnp.zeros((32, H), F32)
    for sect in range(MB):
        base = sect * GROUP * SMALL
        rows = slice(sect * 32, (sect + 1) * 32)
        gb[rows, :] = small[base : base + 32, :]
        for part in range(3):
            cols = slice(part * H, (part + 1) * H)
            row = base + 32 + part * 32
            gi[rows, cols] = small[row : row + 32, :]
            gh[rows, cols] = small[row + 96 : row + 128, :]
        misc = misc + small[base + 224 : base + 256, :]
    ge[...] = misc[0:16]
    be[...] = misc[16:17]
    bi[...] = misc[17:20]
    bh[...] = misc[20:23]
    end_copies = [
        pltpu.make_async_copy(here, there, end_sems.at[at])
        for at, (here, there) in enumerate(zip((gb, gi, gh, ge, be, bi, bh), ends))
    ]
    for copy in end_copies:
        copy.start()
    for copy in copies + end_copies:
        copy.wait()


VMEM_SPEC = pl.BlockSpec(memory_space=pltpu.VMEM)
SMEM_SPEC = pl.BlockSpec(memory_space=pltpu.SMEM)
ANY_SPEC = pl.BlockSpec(memory_space=pl.ANY)
BIG = 60 * 2**20
LOW = 8 * 2**20
shape = jax.ShapeDtypeStruct


def run_layers(sect, operands):
    return pl.pallas_call(
        local_kernel,
        out_shape=(
            shape((GROUP, ROWS, H), BF),
            shape((ATOMS, H), F32),
            shape((ATOMS, H), F32),
            shape((H, NODES), BF),
            shape((PAIRS, H), BF),
        ),
        in_specs=[SMEM_SPEC] + [ANY_SPEC] * 14,
        out_specs=(VMEM_SPEC,) * 5,
        scratch_shapes=[pltpu.VMEM(v.shape, v.dtype) for v in operands]
        + [
            pltpu.VMEM(((NODES + 1) * GAP, H), F32),
            pltpu.VMEM(((NODES + 1) * GAP, H), F32),
            pltpu.VMEM(((H + 1) * GAP, H), F32),
            pltpu.VMEM(((OWN + 1) * GAP, H), F32),
            pltpu.VMEM((MB * PAIRS, H), BF),
            pltpu.VMEM((NODES, H), F32),
            pltpu.VMEM((GROUP * SMALL, H), F32),
            pltpu.VMEM((PAIRS, H), BF),
            pltpu.SemaphoreType.DMA((13,)),
            pltpu.SemaphoreType.DMA((W_PARTS,)),
        ],
        compiler_params=pltpu.CompilerParams(vmem_limit_bytes=BIG),
        name="layers",
    )(sect, *operands)


def neighbours(axis):
    pairs = []
    for zh in range(2):
        for core in range(2):
            for dp in range(GROUP):
                x, y, z = spot_of(dp)
                spot = [x, y, zh * 2 + z]
                spot[axis] = (spot[axis] + (-1 if core else 1)) % 4
                x, y, z = spot
                pairs.append(
                    (
                        z // 2 * 64 + core * GROUP + z % 2 * 16 + y * 4 + x,
                        zh * 64 + core * GROUP + dp,
                    )
                )
    return pairs


def local(
    node_states,
    edge_features,
    edge_source,
    edge_target,
    edge_live,
    w_edge_in,
    b_edge_in,
    w_edge_out,
    b_edge_out,
    w_input,
    w_hidden,
    b_input,
    b_hidden,
    cotangent,
):
    core = lax.axis_index("core").astype(jnp.int32)
    sect = (lax.axis_index("zh") * 2 + core).astype(jnp.int32)
    sect = sect.reshape(1)
    dp = lax.axis_index("dp").astype(jnp.int32)
    z = dp >> 4
    place = jnp.stack([core, ((dp + z) & 1) * 2 + (((dp >> 2) + z) & 1)])
    operands = [v.reshape(8, 128) for v in (edge_source, edge_target, edge_live)] + [
        edge_features,
        w_edge_in,
        b_edge_in.reshape(1, H),
        node_states,
        b_edge_out.reshape(H, H),
        w_input,
        w_hidden,
        b_input.reshape(3, H),
        b_hidden.reshape(3, H),
        cotangent,
        w_edge_out,
    ]

    send, final, base, grad_t, pairs = run_layers(sect, operands)
    grad_states = pl.pallas_call(
        states_kernel,
        out_shape=shape((ATOMS, H), F32),
        in_specs=[SMEM_SPEC] + [VMEM_SPEC] * 4,
        out_specs=VMEM_SPEC,
        scratch_shapes=[pltpu.VMEM(((H + 1) * (ATOMS + 1), H), F32), pltpu.VMEM((NODES, H), F32)],
        compiler_params=pltpu.CompilerParams(vmem_limit_bytes=LOW),
        cost_estimate=pl.CostEstimate(
            flops=2 * ATOMS * H * H * H, bytes_accessed=2 * H * H * H, transcendentals=0
        ),
        name="states_back",
    )(sect, base, grad_t, pairs, w_edge_out)
    got = lax.all_to_all(send, "dp", split_axis=0, concat_axis=0)
    got, grad_states = lax.optimization_barrier((got, grad_states))
    piece = pl.pallas_call(
        sum_kernel,
        out_shape=shape((2 * CLASS, ROWS, H), BF),
        in_specs=[VMEM_SPEC],
        out_specs=VMEM_SPEC,
        compiler_params=pltpu.CompilerParams(vmem_limit_bytes=LOW),
        name="sum_parts",
    )(got)
    classes = [
        [zh * 64 + c * GROUP + DP_AT[kind * CLASS + at] for zh in range(2) for at in range(CLASS)]
        for c in range(2)
        for kind in range(4)
    ]
    near = lax.all_to_all(
        piece, ("zh", "core", "dp"), split_axis=0, concat_axis=0, axis_index_groups=classes
    )
    swap = [(0, 1), (1, 0)]
    far = lax.ppermute(near, "core", swap)
    rest = [lax.ppermute(near, ("zh", "core", "dp"), neighbours(axis)) for axis in range(AXES)]

    params = pltpu.CompilerParams(vmem_limit_bytes=LOW)
    cost = pl.CostEstimate(flops=0, bytes_accessed=6 * 2**20, transcendentals=0)

    def stage(parts):
        return [pltpu.VMEM((H, parts * 2 * CLASS * H), F32), pltpu.SemaphoreType.DMA((2 * parts,))]

    whole = shape((H, H * H), F32)
    out = pl.pallas_call(
        place_own,
        out_shape=whole,
        in_specs=[SMEM_SPEC, VMEM_SPEC, VMEM_SPEC],
        out_specs=ANY_SPEC,
        scratch_shapes=stage(2),
        compiler_params=params,
        cost_estimate=cost,
        name="place_own",
    )(place, near, far)
    rest, out = lax.optimization_barrier((rest, out))
    far_rest = [lax.ppermute(part, "core", swap) for part in rest]
    out = pl.pallas_call(
        place_rest,
        out_shape=whole,
        in_specs=[SMEM_SPEC] + [VMEM_SPEC] * AXES + [ANY_SPEC],
        out_specs=ANY_SPEC,
        scratch_shapes=stage(AXES),
        input_output_aliases={AXES + 1: 0},
        compiler_params=params,
        cost_estimate=cost,
        name="place_rest",
    )(place, *rest, out)
    ends = [
        shape((H, H), F32),
        shape((H, 3 * H), F32),
        shape((H, 3 * H), F32),
        shape((16, H), F32),
        shape((1, H), F32),
        shape((3, H), F32),
        shape((3, H), F32),
    ]
    grad_w_out, grad_b_out, grad_w_in, grad_w_hid, grad_ein, grad_bein, grad_bin, grad_bhid = (
        pl.pallas_call(
            place_last,
            out_shape=[whole] + ends,
            in_specs=[SMEM_SPEC] + [VMEM_SPEC] * (2 * AXES + 2) + [ANY_SPEC],
            out_specs=[ANY_SPEC] * 8,
            scratch_shapes=stage(AXES)
            + [pltpu.VMEM((MB * GROUP * SMALL, H), F32)]
            + [pltpu.VMEM(v.shape, v.dtype) for v in ends]
            + [pltpu.SemaphoreType.DMA((7,))],
            input_output_aliases={2 * AXES + 3: 0},
            compiler_params=params,
            cost_estimate=cost,
            name="place_last",
        )(place, near, far, *rest, *far_rest, out)
    )
    return (
        final,
        grad_states,
        grad_ein,
        grad_bein.reshape(H),
        grad_w_out,
        grad_b_out.reshape(H * H),
        grad_w_in,
        grad_w_hid,
        grad_bin.reshape(3 * H),
        grad_bhid.reshape(3 * H),
    )


def solution(mesh):
    wide = Mesh(mesh.devices.reshape(2, 2, GROUP), ("zh", "core", "dp"))
    split = P(("dp", "zh", "core"), None)
    in_specs = (
        P("dp", None),
        P(None, "dp"),
        P("dp"),
        P("dp"),
        P("dp"),
        P(),
        P(),
        P(),
        P(),
        P(),
        P(),
        P(),
        P(),
        P("dp", None),
    )
    out_specs = (split, split, P(), P(), P(), P(), P(), P(), P(), P())
    return jax.shard_map(local, mesh=wide, in_specs=in_specs, out_specs=out_specs, check_vma=False)
```

```python
import functools

import jax
import jax.numpy as jnp
from jax import lax
from jax.experimental import pallas as pl
from jax.experimental.pallas import tpu as pltpu
from jax.sharding import Mesh
from jax.sharding import PartitionSpec as P

H = 128
ATOMS = 32
EPM = 256
MB = 4
NODES = MB * ATOMS
PAIRS = ATOMS * ATOMS
OWN = H // MB
GAP = 129
ROWS = 136
SMALL = 8
GROUP = 32
CLASS = 8
AXES = 3
W_PARTS = 1
BF = jnp.bfloat16
F32 = jnp.float32


def spot_of(dp):
    return dp % 4, dp // 4 % 4, dp // 16


def slot_of(dp):
    x, y, z = spot_of(dp)
    return ((x + z) % 2 * 2 + (y + z) % 2) * CLASS + z * 4 + y // 2 * 2 + x // 2


DP_AT = sorted(range(GROUP), key=slot_of)


def nn(left, right):
    return jnp.dot(left, right, preferred_element_type=F32)


def nt(left, right):
    return lax.dot_general(left, right, (((1,), (1,)), ((), ())), preferred_element_type=F32)


def tn(left, right):
    return lax.dot_general(left, right, (((0,), (0,)), ((), ())), preferred_element_type=F32)


def halves(value):
    high = value.astype(BF)
    return high, (value - high.astype(F32)).astype(BF)


def fine(dot, left, right):
    lh, ll = halves(left)
    rh, rl = halves(right)
    return dot(lh, rh) + (dot(lh, rl) + dot(ll, rh))


def fine_left(dot, left, right):
    lh, ll = halves(left)
    return dot(lh, right) + dot(ll, right)


def fine_right(dot, left, right):
    rh, rl = halves(right)
    return dot(left, rh) + dot(left, rl)


def sigmoid(value):
    return 0.5 * jnp.tanh(0.5 * value) + 0.5


def gate_forward(message, states, w_input, w_hidden, b_input, b_hidden):
    from_msg = nn(message, w_input) + b_input
    from_state = nn(states, w_hidden) + b_hidden
    reset = sigmoid(from_msg[:, :H] + from_state[:, :H])
    update = sigmoid(from_msg[:, H : 2 * H] + from_state[:, H : 2 * H])
    state_cand = from_state[:, 2 * H :]
    candidate = jnp.tanh(from_msg[:, 2 * H :] + reset * state_cand)
    renewed = (1.0 - update) * candidate + update * states.astype(F32)
    return reset, update, candidate, state_cand, renewed


def gate_backward(grad, states, parts, w_input, w_hidden):
    reset, update, candidate, state_cand = parts
    act = grad * (1.0 - update) * (1.0 - candidate * candidate)
    d_reset = act * state_cand * reset * (1.0 - reset)
    d_update = grad * (states.astype(F32) - candidate) * update * (1.0 - update)
    d_in = jnp.concatenate([d_reset, d_update, act], axis=1).astype(BF)
    d_hid = jnp.concatenate([d_reset, d_update, act * reset], axis=1).astype(BF)
    g_msg = nt(d_in, w_input).astype(BF)
    grad_states = grad * update + nt(d_hid, w_hidden)
    return d_in, d_hid, g_msg, grad_states


def edge_front(features, w_edge_in, b_edge_in):
    return tn(features, w_edge_in) + b_edge_in


def local_kernel(*refs):
    ins, refs = refs[:14], refs[14:]
    (send_ref, final_ref, base_ref, grad_t_ref, pairs_out_ref), refs = refs[:5], refs[5:]
    held, refs = refs[:14], refs[14:]
    u_one, u_two, d_all, d_own, pair_h, rows_scr, small_scr, q_scr, sems, w_sems = refs
    (
        source_ref,
        target_ref,
        live_ref,
        feat_ref,
        w_ein_ref,
        b_ein_ref,
        states_ref,
        b_mat_ref,
        w_in_ref,
        w_hid_ref,
        b_in_ref,
        b_hid_ref,
        cot_ref,
        w_ref,
    ) = held
    sect = section()
    chunk = H * H // W_PARTS
    copies = [
        pltpu.make_async_copy(ins[at], held[at], sems.at[at]) for at in range(13)
    ]

    def w_copy(at):
        cols = pl.ds(at * chunk, chunk)
        return pltpu.make_async_copy(ins[13].at[:, cols], w_ref.at[:, cols], w_sems.at[at])

    for copy in copies:
        copy.start()
    for at in range(W_PARTS):
        w_copy(at).start()
    for copy in copies:
        copy.wait()

    states0 = states_ref[...]
    w_ein = w_ein_ref[...]
    b_ein = b_ein_ref[...]
    b_mat = b_mat_ref[...]
    source = source_ref[...]
    target = target_ref[...]
    live = live_ref[...]
    pair = jnp.where(live > 0, source * ATOMS + target, -1)

    slot = lax.broadcasted_iota(jnp.int32, (PAIRS, H), 0)

    def hot_pairs(first, second):
        return jnp.concatenate(
            [jnp.where(slot == row, 1.0, 0.0).astype(BF) for row in (first, second)], axis=1
        )

    def pair_rows(mol):
        pre = edge_front(feat_ref[:, mol * EPM : (mol + 1) * EPM], w_ein, b_ein)
        hidden = (pre * sigmoid(pre)).astype(BF)
        hot = hot_pairs(pair[2 * mol : 2 * mol + 1, :], pair[2 * mol + 1 : 2 * mol + 2, :])
        pair_h[mol * PAIRS : (mol + 1) * PAIRS, :] = nn(hot, hidden).astype(BF)

    for mol in range(MB):
        pair_rows(mol)

    node = lax.broadcasted_iota(jnp.int32, (NODES, H), 0)
    hot_t, hot_s = [], []
    for row in range(8):
        shift = (row // 2) * ATOMS
        keep = live[row : row + 1, :] > 0
        t_at = jnp.where(keep, target[row : row + 1, :] + shift, -1)
        s_at = source[row : row + 1, :] + shift
        hot_t.append(jnp.where(node == t_at, 1.0, 0.0).astype(BF))
        hot_s.append(jnp.where(node == s_at, 1.0, 0.0).astype(BF))
    hot_t = jnp.concatenate(hot_t, axis=1)
    hot_s = jnp.concatenate(hot_s, axis=1)
    adj = nt(hot_t, hot_s).astype(BF)
    adj_t = nt(hot_s, hot_t).astype(BF)

    def spread(states, u_ref, wait):
        def step(at):
            base = pl.multiple_of(at * 4 * H, 4 * H)
            four = [w_ref[:, pl.ds(base + q * H, H)] for q in range(4)]
            out = nt(states, jnp.concatenate(four, axis=0))
            for q in range(4):
                u_ref[pl.ds(at * 4 + q, NODES, stride=GAP), :] = out[:, q * H : (q + 1) * H]

        if wait:
            for at in range(W_PARTS):
                w_copy(at).wait()
            for at in range(32):
                step(at)
        else:

            def body(at, carry):
                step(at)
                return carry

            lax.fori_loop(0, 32, body, 0, unroll=True)

    def u_rows(u_ref, at):
        return u_ref[pl.ds(at * GAP, H), :].astype(BF)

    def gather(states, u_ref):
        side = fine_right(nt, states, b_mat)
        extra = fine_right(nn, adj, side)
        parts = []
        for mol in range(MB):

            def body(at, total, mol=mol):
                first = mol * ATOMS + at * 4
                left = jnp.concatenate(
                    [
                        pair_h[pl.ds(pl.multiple_of((first + q) * ATOMS, ATOMS), ATOMS), :]
                        for q in range(4)
                    ],
                    axis=1,
                )
                right = jnp.concatenate([u_rows(u_ref, first + q) for q in range(4)], axis=1)
                return total + nt(left, right)

            parts.append(lax.fori_loop(0, 8, body, jnp.zeros((ATOMS, H), F32), unroll=True))
        return (jnp.concatenate(parts, axis=0) + extra).astype(BF)

    w_in = w_in_ref[...]
    w_hid = w_hid_ref[...]
    b_in = jnp.concatenate([b_in_ref[part : part + 1, :] for part in range(3)], axis=1)
    b_hid = jnp.concatenate([b_hid_ref[part : part + 1, :] for part in range(3)], axis=1)

    spread(states0, u_one, True)
    msg_one = gather(states0, u_one)
    *parts_one, renewed = gate_forward(msg_one, states0, w_in, w_hid, b_in, b_hid)
    states1 = renewed.astype(BF)
    spread(states1, u_two, False)
    msg_two = gather(states1, u_two)
    *parts_two, final = gate_forward(msg_two, states1, w_in, w_hid, b_in, b_hid)
    own_rows = pl.ds(pl.multiple_of(sect * ATOMS, ATOMS), ATOMS)
    rows_scr[...] = final
    final_ref[...] = rows_scr[own_rows, :]

    d_in2, d_hid2, g_two, back_one = gate_backward(cot_ref[...], states1, parts_two, w_in, w_hid)
    g_two_t = g_two.astype(F32).T.astype(BF)

    for mol in range(MB):
        left = g_two_t[:, mol * ATOMS : (mol + 1) * ATOMS]

        def body(at, carry, mol=mol, left=left):
            first = mol * ATOMS + at * 4
            right = jnp.concatenate(
                [
                    pair_h[pl.ds(pl.multiple_of((first + q) * ATOMS, ATOMS), ATOMS), :]
                    for q in range(4)
                ],
                axis=1,
            )
            out = nn(left, right)
            for q in range(4):
                d_all[pl.ds(first + q, H, stride=GAP), :] = out[:, q * H : (q + 1) * H]
            return carry

        lax.fori_loop(0, 8, body, 0, unroll=True)

    def back_body(at, total):
        base = pl.multiple_of(at * 4 * H, 4 * H)
        left = jnp.concatenate(
            [d_all[pl.ds((at * 4 + q) * GAP, NODES), :].astype(BF) for q in range(4)], axis=1
        )
        right = jnp.concatenate([w_ref[:, pl.ds(base + q * H, H)] for q in range(4)], axis=0)
        return total + nn(left, right)

    back_msg = lax.fori_loop(0, 32, back_body, jnp.zeros((NODES, H), F32), unroll=True)
    share = nn(adj_t, g_two)
    grad_one = back_one + back_msg + fine(nn, share, b_mat)

    d_in1, d_hid1, g_one, back_zero = gate_backward(grad_one, states0, parts_one, w_in, w_hid)
    rows_scr[...] = g_one.astype(F32).T
    g_one_t = rows_scr[...].astype(BF)
    g_one_own = rows_scr[own_rows, :].astype(BF)

    for mol in range(MB):
        left = g_one_own[:, mol * ATOMS : (mol + 1) * ATOMS]

        def body(at, carry, mol=mol, left=left):
            first = mol * ATOMS + at * 4
            right = jnp.concatenate(
                [
                    pair_h[pl.ds(pl.multiple_of((first + q) * ATOMS, ATOMS), ATOMS), :]
                    for q in range(4)
                ],
                axis=1,
            )
            out = nn(left, right)
            for q in range(4):
                d_own[pl.ds(first + q, OWN, stride=GAP), :] = out[:, q * H : (q + 1) * H]
            return carry

        lax.fori_loop(0, 8, body, 0, unroll=True)

    both_t = jnp.concatenate([states0.astype(F32).T, states1.astype(F32).T], axis=1).astype(BF)

    for at in range(OWN // 2):
        right = jnp.concatenate(
            [
                jnp.concatenate(
                    [
                        d_own[pl.ds((at * 2 + q) * GAP, NODES), :].astype(BF),
                        d_all[pl.ds((sect * OWN + at * 2 + q) * GAP, NODES), :].astype(BF),
                    ],
                    axis=0,
                )
                for q in range(2)
            ],
            axis=1,
        )
        out = nn(both_t, right).astype(BF)
        for q in range(2):
            send_ref[DP_AT[at * 2 + q], 0:H, :] = out[:, q * H : (q + 1) * H]

    rows_scr[...] = g_one.astype(F32)
    g1 = rows_scr[own_rows, :].astype(BF)
    rows_scr[...] = g_two.astype(F32)
    g2 = rows_scr[own_rows, :].astype(BF)
    g_both = jnp.concatenate([g1, g2], axis=1)

    def q_body(at, carry):
        first = sect * ATOMS + at * 2
        right = jnp.concatenate(
            [
                jnp.concatenate([u_rows(u_one, first + q), u_rows(u_two, first + q)], axis=0)
                for q in range(2)
            ],
            axis=1,
        )
        out = nn(g_both, right).astype(BF)
        for q in range(2):
            q_scr[pl.ds(pl.multiple_of((at * 2 + q) * ATOMS, ATOMS), ATOMS), :] = out[
                :, q * H : (q + 1) * H
            ]
        return carry

    lax.fori_loop(0, 16, q_body, 0, unroll=True)
    own_cols = pl.ds(pl.multiple_of(sect * EPM, EPM), EPM)
    feat_own = feat_ref[:, own_cols]
    pre_own = edge_front(feat_own, w_ein, b_ein)
    sig = sigmoid(pre_own)
    slope = sig * (1.0 + pre_own * (1.0 - sig))
    rows_scr[0:8, :] = pair.astype(F32)
    pair_own = rows_scr[pl.ds(sect * 2, 2), :].astype(jnp.int32)
    hot = hot_pairs(pair_own[0:1, :], pair_own[1:2, :])
    g_pre = tn(hot, q_scr[...]) * slope

    g_share_t = nn(g_one_t, adj), nn(g_two_t, adj)
    grad_b_out = fine_left(nn, g_share_t[0], states0) + fine_left(nn, g_share_t[1], states1)
    rows_scr[...] = grad_b_out
    small_scr[0:32, :] = rows_scr[own_rows, :]
    both_rows = jnp.concatenate(
        [msg_one.astype(F32).T, msg_two.astype(F32).T], axis=1
    )
    d_in_both = jnp.concatenate([d_in1, d_in2], axis=0)
    d_hid_both = jnp.concatenate([d_hid1, d_hid2], axis=0)
    for at, (rows_t, d_both) in enumerate(
        ((both_rows, d_in_both), (both_t.astype(F32), d_hid_both))
    ):
        rows_scr[...] = rows_t[:, :H]
        first = rows_scr[own_rows, :]
        rows_scr[...] = rows_t[:, H:]
        left = jnp.concatenate([first, rows_scr[own_rows, :]], axis=1).astype(BF)
        out = nn(left, d_both)
        for part in range(3):
            row = 32 + at * 96 + part * 32
            small_scr[row : row + 32, :] = out[:, part * H : (part + 1) * H]
    small_scr[224:240, :] = fine_right(nn, feat_own, g_pre)
    small_scr[240:256, :] = jnp.zeros((16, H), F32)
    small_scr[240:241, :] = jnp.sum(g_pre, axis=0, keepdims=True)
    for at, pair_d in enumerate(((d_in1, d_in2), (d_hid1, d_hid2))):
        for part in range(3):
            cols = slice(part * H, (part + 1) * H)
            rows_scr[...] = pair_d[0][:, cols].astype(F32) + pair_d[1][:, cols].astype(F32)
            row = 241 + at * 3 + part
            small_scr[row : row + 1, :] = jnp.sum(rows_scr[own_rows, :], axis=0, keepdims=True)
    for at in range(GROUP):
        send_ref[DP_AT[at], H:ROWS, :] = small_scr[at * SMALL : (at + 1) * SMALL, :].astype(BF)

    rows_scr[...] = back_zero + fine(nn, nn(adj_t, g_one), b_mat)
    base_ref[...] = rows_scr[own_rows, :]
    grad_t_ref[...] = g_one_t
    pairs_out_ref[...] = pair_h[pl.ds(pl.multiple_of(sect * PAIRS, PAIRS), PAIRS), :]


def sum_kernel(got_ref, out_ref):
    def body(at, total):
        return total + got_ref[at].astype(F32)

    total = lax.fori_loop(1, GROUP, body, got_ref[0].astype(F32), unroll=True)
    piece = jnp.concatenate([total[:H].T, total[H:]], axis=0).astype(BF)

    for at in range(2 * CLASS):
        out_ref[at] = piece


def states_kernel(base_ref, grad_t_ref, pairs_ref, w_ref, out_ref, d_all, rows_scr):
    sect = section()
    rows_scr[...] = grad_t_ref[...].astype(F32).T
    own = rows_scr[pl.ds(pl.multiple_of(sect * ATOMS, ATOMS), ATOMS), :]
    left = own.T.astype(BF)
    gap = ATOMS + 1

    def body(at, carry):
        right = jnp.concatenate(
            [
                pairs_ref[pl.ds(pl.multiple_of((at * 4 + q) * ATOMS, ATOMS), ATOMS), :]
                for q in range(4)
            ],
            axis=1,
        )
        out = nn(left, right)
        for q in range(4):
            d_all[pl.ds(at * 4 + q, H, stride=gap), :] = out[:, q * H : (q + 1) * H]
        return carry

    lax.fori_loop(0, 8, body, 0, unroll=True)

    def back_body(at, total):
        base = pl.multiple_of(at * 4 * H, 4 * H)
        left = jnp.concatenate(
            [d_all[pl.ds((at * 4 + q) * gap, ATOMS), :].astype(BF) for q in range(4)], axis=1
        )
        right = jnp.concatenate([w_ref[:, pl.ds(base + q * H, H)] for q in range(4)], axis=0)
        return total + nn(left, right)

    out_ref[...] = lax.fori_loop(0, 32, back_body, base_ref[...], unroll=True)


def place_rows(parts, out_hbm, stage, sem):
    copies = []
    for part, (ref, other_core, change) in enumerate(parts):
        core, kind = place_of(other_core, change)
        for half in range(2):
            at_col = ((half * 2 + core) * GROUP + kind * CLASS) * H
            low = (part * 2 + half) * CLASS * H
            cols = pl.ds(low, CLASS * H)
            for dev in range(CLASS):
                for row in range(0, H, 16):
                    stage[row : row + 16, low + dev * H : low + (dev + 1) * H] = ref[
                        half * CLASS + dev, row : row + 16, :
                    ].astype(F32)
            copies.append(
                pltpu.make_async_copy(
                    stage.at[:, cols],
                    out_hbm.at[:, pl.ds(pl.multiple_of(at_col, CLASS * H), CLASS * H)],
                    sem.at[len(copies)],
                )
            )
            copies[-1].start()
    return copies


def place_of(other_core, change):
    core, dp = lax.axis_index("core"), lax.axis_index("dp")
    z = jnp.right_shift(dp, 4)
    kind = jnp.bitwise_and(dp + z, 1) * 2 + jnp.bitwise_and(jnp.right_shift(dp, 2) + z, 1)
    return (1 - core if other_core else core), jnp.bitwise_xor(kind, change)


def section():
    return lax.axis_index("zh") * 2 + lax.axis_index("core")


CHANGES = (2, 1, 3)


OWN_PARTS = ((False, 0), (True, 0))
REST = tuple((False, change) for change in CHANGES)
FAR_REST = tuple((True, change) for change in CHANGES)


def place_some(kinds, first, *refs):
    count = len(kinds)
    out_hbm, stage, sems = refs[count + (0 if first else 1) :]
    parts = [(ref,) + kind for ref, kind in zip(refs, kinds)]
    for copy in place_rows(parts, out_hbm, stage, sems):
        copy.wait()


def place_last(*refs):
    blocks, refs = refs[:8], refs[9:]
    out_hbm, *ends = refs[:8]
    stage, sems, small, gb, gi, gh, ge, be, bi, bh, end_sems = refs[8:]
    blocks = [(ref,) + kind for ref, kind in zip(blocks, OWN_PARTS + REST + FAR_REST)]
    copies = place_rows(blocks[6:], out_hbm, stage, sems)
    for ref, other_core, change in blocks:
        core, kind = place_of(other_core, change)
        for at in range(2 * CLASS):
            block = ((at // CLASS) * 2 + core) * GROUP + kind * CLASS + at % CLASS
            row = pl.multiple_of(block * SMALL, SMALL)
            small[pl.ds(row, SMALL), :] = ref[at, H:ROWS, :].astype(F32)
    misc = jnp.zeros((32, H), F32)
    for sect in range(MB):
        base = sect * GROUP * SMALL
        rows = slice(sect * 32, (sect + 1) * 32)
        gb[rows, :] = small[base : base + 32, :]
        for part in range(3):
            cols = slice(part * H, (part + 1) * H)
            row = base + 32 + part * 32
            gi[rows, cols] = small[row : row + 32, :]
            gh[rows, cols] = small[row + 96 : row + 128, :]
        misc = misc + small[base + 224 : base + 256, :]
    ge[...] = misc[0:16]
    be[...] = misc[16:17]
    bi[...] = misc[17:20]
    bh[...] = misc[20:23]
    end_copies = [
        pltpu.make_async_copy(here, there, end_sems.at[at])
        for at, (here, there) in enumerate(zip((gb, gi, gh, ge, be, bi, bh), ends))
    ]
    for copy in end_copies:
        copy.start()
    for copy in copies + end_copies:
        copy.wait()


VMEM_SPEC = pl.BlockSpec(memory_space=pltpu.VMEM)
ANY_SPEC = pl.BlockSpec(memory_space=pl.ANY)
BIG = 60 * 2**20
LOW = 8 * 2**20
shape = jax.ShapeDtypeStruct


def run_layers(operands):
    return pl.pallas_call(
        local_kernel,
        out_shape=(
            shape((GROUP, ROWS, H), BF),
            shape((ATOMS, H), F32),
            shape((ATOMS, H), F32),
            shape((H, NODES), BF),
            shape((PAIRS, H), BF),
        ),
        in_specs=[ANY_SPEC] * 14,
        out_specs=(VMEM_SPEC,) * 5,
        scratch_shapes=[pltpu.VMEM(v.shape, v.dtype) for v in operands]
        + [
            pltpu.VMEM(((NODES + 1) * GAP, H), F32),
            pltpu.VMEM(((NODES + 1) * GAP, H), F32),
            pltpu.VMEM(((H + 1) * GAP, H), F32),
            pltpu.VMEM(((OWN + 1) * GAP, H), F32),
            pltpu.VMEM((MB * PAIRS, H), BF),
            pltpu.VMEM((NODES, H), F32),
            pltpu.VMEM((GROUP * SMALL, H), F32),
            pltpu.VMEM((PAIRS, H), BF),
            pltpu.SemaphoreType.DMA((13,)),
            pltpu.SemaphoreType.DMA((W_PARTS,)),
        ],
        compiler_params=pltpu.CompilerParams(vmem_limit_bytes=BIG),
        name="layers",
    )(*operands)


def neighbours(axis):
    pairs = []
    for zh in range(2):
        for core in range(2):
            for dp in range(GROUP):
                x, y, z = spot_of(dp)
                spot = [x, y, zh * 2 + z]
                spot[axis] = (spot[axis] + (-1 if core else 1)) % 4
                x, y, z = spot
                pairs.append(
                    (
                        z // 2 * 64 + core * GROUP + z % 2 * 16 + y * 4 + x,
                        zh * 64 + core * GROUP + dp,
                    )
                )
    return pairs


def local(
    node_states,
    edge_features,
    edge_source,
    edge_target,
    edge_live,
    w_edge_in,
    b_edge_in,
    w_edge_out,
    b_edge_out,
    w_input,
    w_hidden,
    b_input,
    b_hidden,
    cotangent,
):
    operands = [v.reshape(8, 128) for v in (edge_source, edge_target, edge_live)] + [
        edge_features,
        w_edge_in,
        b_edge_in.reshape(1, H),
        node_states,
        b_edge_out.reshape(H, H),
        w_input,
        w_hidden,
        b_input.reshape(3, H),
        b_hidden.reshape(3, H),
        cotangent,
        w_edge_out,
    ]

    send, final, base, grad_t, pairs = run_layers(operands)
    grad_states = pl.pallas_call(
        states_kernel,
        out_shape=shape((ATOMS, H), F32),
        in_specs=[VMEM_SPEC] * 4,
        out_specs=VMEM_SPEC,
        scratch_shapes=[pltpu.VMEM(((H + 1) * (ATOMS + 1), H), F32), pltpu.VMEM((NODES, H), F32)],
        compiler_params=pltpu.CompilerParams(vmem_limit_bytes=LOW),
        cost_estimate=pl.CostEstimate(
            flops=2 * ATOMS * H * H * H, bytes_accessed=2 * H * H * H, transcendentals=0
        ),
        name="states_back",
    )(base, grad_t, pairs, w_edge_out)
    got = lax.all_to_all(send, "dp", split_axis=0, concat_axis=0)
    got, grad_states = lax.optimization_barrier((got, grad_states))
    piece = pl.pallas_call(
        sum_kernel,
        out_shape=shape((2 * CLASS, ROWS, H), BF),
        in_specs=[VMEM_SPEC],
        out_specs=VMEM_SPEC,
        compiler_params=pltpu.CompilerParams(vmem_limit_bytes=LOW),
        name="sum_parts",
    )(got)
    classes = [
        [zh * 64 + c * GROUP + DP_AT[kind * CLASS + at] for zh in range(2) for at in range(CLASS)]
        for c in range(2)
        for kind in range(4)
    ]
    near = lax.all_to_all(
        piece, ("zh", "core", "dp"), split_axis=0, concat_axis=0, axis_index_groups=classes
    )
    swap = [(0, 1), (1, 0)]
    far = lax.ppermute(near, "core", swap)
    rest = [lax.ppermute(near, ("zh", "core", "dp"), neighbours(axis)) for axis in range(AXES)]

    params = pltpu.CompilerParams(vmem_limit_bytes=LOW)
    cost = pl.CostEstimate(flops=0, bytes_accessed=6 * 2**20, transcendentals=0)

    def stage(parts):
        return [pltpu.VMEM((H, parts * 2 * CLASS * H), F32), pltpu.SemaphoreType.DMA((2 * parts,))]

    whole = shape((H, H * H), F32)

    def place_blocks(kinds, blocks, out, name):
        count = len(kinds)
        first = out is None
        return pl.pallas_call(
            functools.partial(place_some, kinds, first),
            out_shape=whole,
            in_specs=[VMEM_SPEC] * count + ([] if first else [ANY_SPEC]),
            out_specs=ANY_SPEC,
            scratch_shapes=stage(count),
            input_output_aliases={} if first else {count: 0},
            compiler_params=params,
            cost_estimate=cost,
            name=name,
        )(*blocks, *([] if first else [out]))

    out = place_blocks(OWN_PARTS, (near, far), None, "place_own")
    rest[0], out = lax.optimization_barrier((rest[0], out))
    far_rest = [lax.ppermute(rest[0], "core", swap)]
    out = place_blocks(REST[:1], rest[:1], out, "place_x")
    for axis in (1, 2):
        rest[axis], out = lax.optimization_barrier((rest[axis], out))
        far_rest.append(lax.ppermute(rest[axis], "core", swap))
    out = place_blocks(
        REST[1:] + FAR_REST[:1], (rest[1], rest[2], far_rest[0]), out, "place_y_z_far_x"
    )
    ends = [
        shape((H, H), F32),
        shape((H, 3 * H), F32),
        shape((H, 3 * H), F32),
        shape((16, H), F32),
        shape((1, H), F32),
        shape((3, H), F32),
        shape((3, H), F32),
    ]
    grad_w_out, grad_b_out, grad_w_in, grad_w_hid, grad_ein, grad_bein, grad_bin, grad_bhid = (
        pl.pallas_call(
            place_last,
            out_shape=[whole] + ends,
            in_specs=[VMEM_SPEC] * (2 * AXES + 2) + [ANY_SPEC],
            out_specs=[ANY_SPEC] * 8,
            scratch_shapes=stage(2)
            + [pltpu.VMEM((MB * GROUP * SMALL, H), F32)]
            + [pltpu.VMEM(v.shape, v.dtype) for v in ends]
            + [pltpu.SemaphoreType.DMA((7,))],
            input_output_aliases={2 * AXES + 2: 0},
            compiler_params=params,
            cost_estimate=cost,
            name="place_last",
        )(near, far, *rest, *far_rest, out)
    )
    return (
        final,
        grad_states,
        grad_ein,
        grad_bein.reshape(H),
        grad_w_out,
        grad_b_out.reshape(H * H),
        grad_w_in,
        grad_w_hid,
        grad_bin.reshape(3 * H),
        grad_bhid.reshape(3 * H),
    )


def solution(mesh):
    wide = Mesh(mesh.devices.reshape(2, 2, GROUP), ("zh", "core", "dp"))
    split = P(("dp", "zh", "core"), None)
    in_specs = (
        P("dp", None),
        P(None, "dp"),
        P("dp"),
        P("dp"),
        P("dp"),
        P(),
        P(),
        P(),
        P(),
        P(),
        P(),
        P(),
        P(),
        P("dp", None),
    )
    out_specs = (split, split, P(), P(), P(), P(), P(), P(), P(), P())
    return jax.shard_map(local, mesh=wide, in_specs=in_specs, out_specs=out_specs, check_vma=False)
```

```python
import functools

import jax
import jax.numpy as jnp
from jax import lax
from jax.experimental import pallas as pl
from jax.experimental.pallas import tpu as pltpu
from jax.sharding import Mesh
from jax.sharding import PartitionSpec as P

H = 128
ATOMS = 32
EPM = 256
MB = 4
NODES = MB * ATOMS
PAIRS = ATOMS * ATOMS
OWN = H // MB
GAP = 129
ROWS = 144
SMALL = 8
GROUP = 32
CLASS = 8
AXES = 3
W_PARTS = 1
BF = jnp.bfloat16
F32 = jnp.float32


def spot_of(dp):
    return dp % 4, dp // 4 % 4, dp // 16


def slot_of(dp):
    x, y, z = spot_of(dp)
    return ((x + z) % 2 * 2 + (y + z) % 2) * CLASS + z * 4 + y // 2 * 2 + x // 2


DP_AT = sorted(range(GROUP), key=slot_of)


def nn(left, right):
    return jnp.dot(left, right, preferred_element_type=F32)


def nt(left, right):
    return lax.dot_general(left, right, (((1,), (1,)), ((), ())), preferred_element_type=F32)


def tn(left, right):
    return lax.dot_general(left, right, (((0,), (0,)), ((), ())), preferred_element_type=F32)


def halves(value):
    high = value.astype(BF)
    return high, (value - high.astype(F32)).astype(BF)


def fine(dot, left, right):
    lh, ll = halves(left)
    rh, rl = halves(right)
    return dot(lh, rh) + (dot(lh, rl) + dot(ll, rh))


def fine_left(dot, left, right):
    lh, ll = halves(left)
    return dot(lh, right) + dot(ll, right)


def fine_right(dot, left, right):
    rh, rl = halves(right)
    return dot(left, rh) + dot(left, rl)


def sigmoid(value):
    return 0.5 * jnp.tanh(0.5 * value) + 0.5


def gate_forward(message, states, w_input, w_hidden, b_input, b_hidden):
    from_msg = nn(message, w_input) + b_input
    from_state = nn(states, w_hidden) + b_hidden
    reset = sigmoid(from_msg[:, :H] + from_state[:, :H])
    update = sigmoid(from_msg[:, H : 2 * H] + from_state[:, H : 2 * H])
    state_cand = from_state[:, 2 * H :]
    candidate = jnp.tanh(from_msg[:, 2 * H :] + reset * state_cand)
    renewed = (1.0 - update) * candidate + update * states.astype(F32)
    return reset, update, candidate, state_cand, renewed


def gate_backward(grad, states, parts, w_input, w_hidden):
    reset, update, candidate, state_cand = parts
    act = grad * (1.0 - update) * (1.0 - candidate * candidate)
    d_reset = act * state_cand * reset * (1.0 - reset)
    d_update = grad * (states.astype(F32) - candidate) * update * (1.0 - update)
    d_in = jnp.concatenate([d_reset, d_update, act], axis=1).astype(BF)
    d_hid = jnp.concatenate([d_reset, d_update, act * reset], axis=1).astype(BF)
    g_msg = nt(d_in, w_input).astype(BF)
    grad_states = grad * update + nt(d_hid, w_hidden)
    return d_in, d_hid, g_msg, grad_states


def edge_front(features, w_edge_in, b_edge_in):
    return tn(features, w_edge_in) + b_edge_in


def local_kernel(*refs):
    ins, refs = refs[:14], refs[14:]
    (send_ref, final_ref, base_ref, grad_t_ref, pairs_out_ref), refs = refs[:5], refs[5:]
    held, refs = refs[:14], refs[14:]
    u_one, u_two, d_all, d_own, pair_h, rows_scr, small_scr, q_scr, sems, w_sems = refs
    (
        source_ref,
        target_ref,
        live_ref,
        feat_ref,
        w_ein_ref,
        b_ein_ref,
        states_ref,
        b_mat_ref,
        w_in_ref,
        w_hid_ref,
        b_in_ref,
        b_hid_ref,
        cot_ref,
        w_ref,
    ) = held
    sect = section()
    chunk = H * H // W_PARTS
    copies = [
        pltpu.make_async_copy(ins[at], held[at], sems.at[at]) for at in range(13)
    ]

    def w_copy(at):
        cols = pl.ds(at * chunk, chunk)
        return pltpu.make_async_copy(ins[13].at[:, cols], w_ref.at[:, cols], w_sems.at[at])

    for copy in copies:
        copy.start()
    for at in range(W_PARTS):
        w_copy(at).start()
    for copy in copies:
        copy.wait()

    states0 = states_ref[...]
    w_ein = w_ein_ref[...]
    b_ein = b_ein_ref[...]
    b_mat = b_mat_ref[...]
    source = source_ref[...]
    target = target_ref[...]
    live = live_ref[...]
    pair = jnp.where(live > 0, source * ATOMS + target, -1)

    slot = lax.broadcasted_iota(jnp.int32, (PAIRS, H), 0)

    def hot_pairs(first, second):
        return jnp.concatenate(
            [jnp.where(slot == row, 1.0, 0.0).astype(BF) for row in (first, second)], axis=1
        )

    def pair_rows(mol):
        pre = edge_front(feat_ref[:, mol * EPM : (mol + 1) * EPM], w_ein, b_ein)
        hidden = (pre * sigmoid(pre)).astype(BF)
        hot = hot_pairs(pair[2 * mol : 2 * mol + 1, :], pair[2 * mol + 1 : 2 * mol + 2, :])
        pair_h[mol * PAIRS : (mol + 1) * PAIRS, :] = nn(hot, hidden).astype(BF)

    for mol in range(MB):
        pair_rows(mol)

    node = lax.broadcasted_iota(jnp.int32, (NODES, H), 0)
    hot_t, hot_s = [], []
    for row in range(8):
        shift = (row // 2) * ATOMS
        keep = live[row : row + 1, :] > 0
        t_at = jnp.where(keep, target[row : row + 1, :] + shift, -1)
        s_at = source[row : row + 1, :] + shift
        hot_t.append(jnp.where(node == t_at, 1.0, 0.0).astype(BF))
        hot_s.append(jnp.where(node == s_at, 1.0, 0.0).astype(BF))
    hot_t = jnp.concatenate(hot_t, axis=1)
    hot_s = jnp.concatenate(hot_s, axis=1)
    adj = nt(hot_t, hot_s).astype(BF)
    adj_t = nt(hot_s, hot_t).astype(BF)

    def spread(states, u_ref, wait):
        def step(at):
            base = pl.multiple_of(at * 4 * H, 4 * H)
            four = [w_ref[:, pl.ds(base + q * H, H)] for q in range(4)]
            out = nt(states, jnp.concatenate(four, axis=0))
            for q in range(4):
                u_ref[pl.ds(at * 4 + q, NODES, stride=GAP), :] = out[:, q * H : (q + 1) * H]

        if wait:
            for at in range(W_PARTS):
                w_copy(at).wait()
            for at in range(32):
                step(at)
        else:

            def body(at, carry):
                step(at)
                return carry

            lax.fori_loop(0, 32, body, 0, unroll=True)

    def u_rows(u_ref, at):
        return u_ref[pl.ds(at * GAP, H), :].astype(BF)

    def gather(states, u_ref):
        side = fine_right(nt, states, b_mat)
        extra = fine_right(nn, adj, side)
        parts = []
        for mol in range(MB):

            def body(at, total, mol=mol):
                first = mol * ATOMS + at * 4
                left = jnp.concatenate(
                    [
                        pair_h[pl.ds(pl.multiple_of((first + q) * ATOMS, ATOMS), ATOMS), :]
                        for q in range(4)
                    ],
                    axis=1,
                )
                right = jnp.concatenate([u_rows(u_ref, first + q) for q in range(4)], axis=1)
                return total + nt(left, right)

            parts.append(lax.fori_loop(0, 8, body, jnp.zeros((ATOMS, H), F32), unroll=True))
        return (jnp.concatenate(parts, axis=0) + extra).astype(BF)

    w_in = w_in_ref[...]
    w_hid = w_hid_ref[...]
    b_in = jnp.concatenate([b_in_ref[part : part + 1, :] for part in range(3)], axis=1)
    b_hid = jnp.concatenate([b_hid_ref[part : part + 1, :] for part in range(3)], axis=1)

    spread(states0, u_one, True)
    msg_one = gather(states0, u_one)
    *parts_one, renewed = gate_forward(msg_one, states0, w_in, w_hid, b_in, b_hid)
    states1 = renewed.astype(BF)
    spread(states1, u_two, False)
    msg_two = gather(states1, u_two)
    *parts_two, final = gate_forward(msg_two, states1, w_in, w_hid, b_in, b_hid)
    own_rows = pl.ds(pl.multiple_of(sect * ATOMS, ATOMS), ATOMS)
    rows_scr[...] = final
    final_ref[...] = rows_scr[own_rows, :]

    d_in2, d_hid2, g_two, back_one = gate_backward(cot_ref[...], states1, parts_two, w_in, w_hid)
    g_two_t = g_two.astype(F32).T.astype(BF)

    for mol in range(MB):
        left = g_two_t[:, mol * ATOMS : (mol + 1) * ATOMS]

        def body(at, carry, mol=mol, left=left):
            first = mol * ATOMS + at * 4
            right = jnp.concatenate(
                [
                    pair_h[pl.ds(pl.multiple_of((first + q) * ATOMS, ATOMS), ATOMS), :]
                    for q in range(4)
                ],
                axis=1,
            )
            out = nn(left, right)
            for q in range(4):
                d_all[pl.ds(first + q, H, stride=GAP), :] = out[:, q * H : (q + 1) * H]
            return carry

        lax.fori_loop(0, 8, body, 0, unroll=True)

    def back_body(at, total):
        base = pl.multiple_of(at * 4 * H, 4 * H)
        left = jnp.concatenate(
            [d_all[pl.ds((at * 4 + q) * GAP, NODES), :].astype(BF) for q in range(4)], axis=1
        )
        right = jnp.concatenate([w_ref[:, pl.ds(base + q * H, H)] for q in range(4)], axis=0)
        return total + nn(left, right)

    back_msg = lax.fori_loop(0, 32, back_body, jnp.zeros((NODES, H), F32), unroll=True)
    share = nn(adj_t, g_two)
    grad_one = back_one + back_msg + fine(nn, share, b_mat)

    d_in1, d_hid1, g_one, back_zero = gate_backward(grad_one, states0, parts_one, w_in, w_hid)
    rows_scr[...] = g_one.astype(F32).T
    g_one_t = rows_scr[...].astype(BF)
    g_one_own = rows_scr[own_rows, :].astype(BF)

    for mol in range(MB):
        left = g_one_own[:, mol * ATOMS : (mol + 1) * ATOMS]

        def body(at, carry, mol=mol, left=left):
            first = mol * ATOMS + at * 4
            right = jnp.concatenate(
                [
                    pair_h[pl.ds(pl.multiple_of((first + q) * ATOMS, ATOMS), ATOMS), :]
                    for q in range(4)
                ],
                axis=1,
            )
            out = nn(left, right)
            for q in range(4):
                d_own[pl.ds(first + q, OWN, stride=GAP), :] = out[:, q * H : (q + 1) * H]
            return carry

        lax.fori_loop(0, 8, body, 0, unroll=True)

    both_t = jnp.concatenate([states0.astype(F32).T, states1.astype(F32).T], axis=1).astype(BF)

    for at in range(OWN // 2):
        right = jnp.concatenate(
            [
                jnp.concatenate(
                    [
                        d_own[pl.ds((at * 2 + q) * GAP, NODES), :].astype(BF),
                        d_all[pl.ds((sect * OWN + at * 2 + q) * GAP, NODES), :].astype(BF),
                    ],
                    axis=0,
                )
                for q in range(2)
            ],
            axis=1,
        )
        out = nn(both_t, right).astype(BF)
        for q in range(2):
            send_ref[DP_AT[at * 2 + q], 0:H, :] = out[:, q * H : (q + 1) * H]

    rows_scr[...] = g_one.astype(F32)
    g1 = rows_scr[own_rows, :].astype(BF)
    rows_scr[...] = g_two.astype(F32)
    g2 = rows_scr[own_rows, :].astype(BF)
    g_both = jnp.concatenate([g1, g2], axis=1)

    def q_body(at, carry):
        first = sect * ATOMS + at * 2
        right = jnp.concatenate(
            [
                jnp.concatenate([u_rows(u_one, first + q), u_rows(u_two, first + q)], axis=0)
                for q in range(2)
            ],
            axis=1,
        )
        out = nn(g_both, right).astype(BF)
        for q in range(2):
            q_scr[pl.ds(pl.multiple_of((at * 2 + q) * ATOMS, ATOMS), ATOMS), :] = out[
                :, q * H : (q + 1) * H
            ]
        return carry

    lax.fori_loop(0, 16, q_body, 0, unroll=True)
    own_cols = pl.ds(pl.multiple_of(sect * EPM, EPM), EPM)
    feat_own = feat_ref[:, own_cols]
    pre_own = edge_front(feat_own, w_ein, b_ein)
    sig = sigmoid(pre_own)
    slope = sig * (1.0 + pre_own * (1.0 - sig))
    rows_scr[0:8, :] = pair.astype(F32)
    pair_own = rows_scr[pl.ds(sect * 2, 2), :].astype(jnp.int32)
    hot = hot_pairs(pair_own[0:1, :], pair_own[1:2, :])
    g_pre = tn(hot, q_scr[...]) * slope

    g_share_t = nn(g_one_t, adj), nn(g_two_t, adj)
    grad_b_out = fine_left(nn, g_share_t[0], states0) + fine_left(nn, g_share_t[1], states1)
    rows_scr[...] = grad_b_out
    small_scr[0:32, :] = rows_scr[own_rows, :]
    both_rows = jnp.concatenate(
        [msg_one.astype(F32).T, msg_two.astype(F32).T], axis=1
    )
    d_in_both = jnp.concatenate([d_in1, d_in2], axis=0)
    d_hid_both = jnp.concatenate([d_hid1, d_hid2], axis=0)
    for at, (rows_t, d_both) in enumerate(
        ((both_rows, d_in_both), (both_t.astype(F32), d_hid_both))
    ):
        rows_scr[...] = rows_t[:, :H]
        first = rows_scr[own_rows, :]
        rows_scr[...] = rows_t[:, H:]
        left = jnp.concatenate([first, rows_scr[own_rows, :]], axis=1).astype(BF)
        out = nn(left, d_both)
        for part in range(3):
            row = 32 + at * 96 + part * 32
            small_scr[row : row + 32, :] = out[:, part * H : (part + 1) * H]
    small_scr[224:240, :] = fine_right(nn, feat_own, g_pre)
    small_scr[240:256, :] = jnp.zeros((16, H), F32)
    small_scr[240:241, :] = jnp.sum(g_pre, axis=0, keepdims=True)
    for at, pair_d in enumerate(((d_in1, d_in2), (d_hid1, d_hid2))):
        for part in range(3):
            cols = slice(part * H, (part + 1) * H)
            rows_scr[...] = pair_d[0][:, cols].astype(F32) + pair_d[1][:, cols].astype(F32)
            row = 241 + at * 3 + part
            small_scr[row : row + 1, :] = jnp.sum(rows_scr[own_rows, :], axis=0, keepdims=True)
    for at in range(GROUP):
        high, low = halves(small_scr[at * SMALL : (at + 1) * SMALL, :])
        both = jnp.concatenate([high.astype(F32), low.astype(F32)], axis=0)
        send_ref[DP_AT[at], H:ROWS, :] = both.astype(BF)

    rows_scr[...] = back_zero + fine(nn, nn(adj_t, g_one), b_mat)
    base_ref[...] = rows_scr[own_rows, :]
    grad_t_ref[...] = g_one_t
    pairs_out_ref[...] = pair_h[pl.ds(pl.multiple_of(sect * PAIRS, PAIRS), PAIRS), :]


def sum_kernel(got_ref, out_ref):
    def body(at, total):
        return total + got_ref[at].astype(F32)

    total = lax.fori_loop(1, GROUP, body, got_ref[0].astype(F32), unroll=True)
    high, low = halves(total[H : H + SMALL] + total[H + SMALL :])
    piece = jnp.concatenate([total[:H].T, high.astype(F32), low.astype(F32)], axis=0).astype(BF)

    for at in range(2 * CLASS):
        out_ref[at] = piece


def states_kernel(base_ref, grad_t_ref, pairs_ref, w_ref, out_ref, d_all, rows_scr):
    sect = section()
    rows_scr[...] = grad_t_ref[...].astype(F32).T
    own = rows_scr[pl.ds(pl.multiple_of(sect * ATOMS, ATOMS), ATOMS), :]
    left = own.T.astype(BF)
    gap = ATOMS + 1

    def body(at, carry):
        right = jnp.concatenate(
            [
                pairs_ref[pl.ds(pl.multiple_of((at * 4 + q) * ATOMS, ATOMS), ATOMS), :]
                for q in range(4)
            ],
            axis=1,
        )
        out = nn(left, right)
        for q in range(4):
            d_all[pl.ds(at * 4 + q, H, stride=gap), :] = out[:, q * H : (q + 1) * H]
        return carry

    lax.fori_loop(0, 8, body, 0, unroll=True)

    def back_body(at, total):
        base = pl.multiple_of(at * 4 * H, 4 * H)
        left = jnp.concatenate(
            [d_all[pl.ds((at * 4 + q) * gap, ATOMS), :].astype(BF) for q in range(4)], axis=1
        )
        right = jnp.concatenate([w_ref[:, pl.ds(base + q * H, H)] for q in range(4)], axis=0)
        return total + nn(left, right)

    out_ref[...] = lax.fori_loop(0, 32, back_body, base_ref[...], unroll=True)


def place_rows(parts, out_hbm, stage, sem):
    copies = []
    for part, (ref, other_core, change) in enumerate(parts):
        core, kind = place_of(other_core, change)
        for half in range(2):
            at_col = ((half * 2 + core) * GROUP + kind * CLASS) * H
            low = (part * 2 + half) * CLASS * H
            cols = pl.ds(low, CLASS * H)
            for dev in range(CLASS):
                for row in range(0, H, 16):
                    stage[row : row + 16, low + dev * H : low + (dev + 1) * H] = ref[
                        half * CLASS + dev, row : row + 16, :
                    ].astype(F32)
            copies.append(
                pltpu.make_async_copy(
                    stage.at[:, cols],
                    out_hbm.at[:, pl.ds(pl.multiple_of(at_col, CLASS * H), CLASS * H)],
                    sem.at[len(copies)],
                )
            )
            copies[-1].start()
    return copies


def place_of(other_core, change):
    core, dp = lax.axis_index("core"), lax.axis_index("dp")
    z = jnp.right_shift(dp, 4)
    kind = jnp.bitwise_and(dp + z, 1) * 2 + jnp.bitwise_and(jnp.right_shift(dp, 2) + z, 1)
    return (1 - core if other_core else core), jnp.bitwise_xor(kind, change)


def section():
    return lax.axis_index("zh") * 2 + lax.axis_index("core")


CHANGES = (2, 1, 3)


OWN_PARTS = ((False, 0), (True, 0))
REST = tuple((False, change) for change in CHANGES)
FAR_REST = tuple((True, change) for change in CHANGES)


def place_some(kinds, first, *refs):
    count = len(kinds)
    out_hbm, stage, sems = refs[count + (0 if first else 1) :]
    parts = [(ref,) + kind for ref, kind in zip(refs, kinds)]
    for copy in place_rows(parts, out_hbm, stage, sems):
        copy.wait()


def place_last(*refs):
    blocks, refs = refs[:8], refs[9:]
    out_hbm, *ends = refs[:8]
    stage, sems, small, gb, gi, gh, ge, be, bi, bh, end_sems = refs[8:]
    blocks = [(ref,) + kind for ref, kind in zip(blocks, OWN_PARTS + REST + FAR_REST)]
    copies = place_rows(blocks[6:], out_hbm, stage, sems)
    for ref, other_core, change in blocks:
        core, kind = place_of(other_core, change)
        for at in range(2 * CLASS):
            block = ((at // CLASS) * 2 + core) * GROUP + kind * CLASS + at % CLASS
            row = pl.multiple_of(block * SMALL, SMALL)
            both = ref[at, H:ROWS, :].astype(F32)
            small[pl.ds(row, SMALL), :] = both[:SMALL] + both[SMALL:]
    misc = jnp.zeros((32, H), F32)
    for sect in range(MB):
        base = sect * GROUP * SMALL
        rows = slice(sect * 32, (sect + 1) * 32)
        gb[rows, :] = small[base : base + 32, :]
        for part in range(3):
            cols = slice(part * H, (part + 1) * H)
            row = base + 32 + part * 32
            gi[rows, cols] = small[row : row + 32, :]
            gh[rows, cols] = small[row + 96 : row + 128, :]
        misc = misc + small[base + 224 : base + 256, :]
    ge[...] = misc[0:16]
    be[...] = misc[16:17]
    bi[...] = misc[17:20]
    bh[...] = misc[20:23]
    end_copies = [
        pltpu.make_async_copy(here, there, end_sems.at[at])
        for at, (here, there) in enumerate(zip((gb, gi, gh, ge, be, bi, bh), ends))
    ]
    for copy in end_copies:
        copy.start()
    for copy in copies + end_copies:
        copy.wait()


VMEM_SPEC = pl.BlockSpec(memory_space=pltpu.VMEM)
ANY_SPEC = pl.BlockSpec(memory_space=pl.ANY)
BIG = 60 * 2**20
LOW = 8 * 2**20
shape = jax.ShapeDtypeStruct


def run_layers(operands):
    return pl.pallas_call(
        local_kernel,
        out_shape=(
            shape((GROUP, ROWS, H), BF),
            shape((ATOMS, H), F32),
            shape((ATOMS, H), F32),
            shape((H, NODES), BF),
            shape((PAIRS, H), BF),
        ),
        in_specs=[ANY_SPEC] * 14,
        out_specs=(VMEM_SPEC,) * 5,
        scratch_shapes=[pltpu.VMEM(v.shape, v.dtype) for v in operands]
        + [
            pltpu.VMEM(((NODES + 1) * GAP, H), F32),
            pltpu.VMEM(((NODES + 1) * GAP, H), F32),
            pltpu.VMEM(((H + 1) * GAP, H), F32),
            pltpu.VMEM(((OWN + 1) * GAP, H), F32),
            pltpu.VMEM((MB * PAIRS, H), BF),
            pltpu.VMEM((NODES, H), F32),
            pltpu.VMEM((GROUP * SMALL, H), F32),
            pltpu.VMEM((PAIRS, H), BF),
            pltpu.SemaphoreType.DMA((13,)),
            pltpu.SemaphoreType.DMA((W_PARTS,)),
        ],
        compiler_params=pltpu.CompilerParams(vmem_limit_bytes=BIG),
        name="layers",
    )(*operands)


def neighbours(axis):
    pairs = []
    for zh in range(2):
        for core in range(2):
            for dp in range(GROUP):
                x, y, z = spot_of(dp)
                spot = [x, y, zh * 2 + z]
                spot[axis] = (spot[axis] + (-1 if core else 1)) % 4
                x, y, z = spot
                pairs.append(
                    (
                        z // 2 * 64 + core * GROUP + z % 2 * 16 + y * 4 + x,
                        zh * 64 + core * GROUP + dp,
                    )
                )
    return pairs


def local(
    node_states,
    edge_features,
    edge_source,
    edge_target,
    edge_live,
    w_edge_in,
    b_edge_in,
    w_edge_out,
    b_edge_out,
    w_input,
    w_hidden,
    b_input,
    b_hidden,
    cotangent,
):
    operands = [v.reshape(8, 128) for v in (edge_source, edge_target, edge_live)] + [
        edge_features,
        w_edge_in,
        b_edge_in.reshape(1, H),
        node_states,
        b_edge_out.reshape(H, H),
        w_input,
        w_hidden,
        b_input.reshape(3, H),
        b_hidden.reshape(3, H),
        cotangent,
        w_edge_out,
    ]

    send, final, base, grad_t, pairs = run_layers(operands)
    grad_states = pl.pallas_call(
        states_kernel,
        out_shape=shape((ATOMS, H), F32),
        in_specs=[VMEM_SPEC] * 4,
        out_specs=VMEM_SPEC,
        scratch_shapes=[pltpu.VMEM(((H + 1) * (ATOMS + 1), H), F32), pltpu.VMEM((NODES, H), F32)],
        compiler_params=pltpu.CompilerParams(vmem_limit_bytes=LOW),
        cost_estimate=pl.CostEstimate(
            flops=2 * ATOMS * H * H * H, bytes_accessed=2 * H * H * H, transcendentals=0
        ),
        name="states_back",
    )(base, grad_t, pairs, w_edge_out)
    got = lax.all_to_all(send, "dp", split_axis=0, concat_axis=0)
    got, grad_states = lax.optimization_barrier((got, grad_states))
    piece = pl.pallas_call(
        sum_kernel,
        out_shape=shape((2 * CLASS, ROWS, H), BF),
        in_specs=[VMEM_SPEC],
        out_specs=VMEM_SPEC,
        compiler_params=pltpu.CompilerParams(vmem_limit_bytes=LOW),
        name="sum_parts",
    )(got)
    classes = [
        [zh * 64 + c * GROUP + DP_AT[kind * CLASS + at] for zh in range(2) for at in range(CLASS)]
        for c in range(2)
        for kind in range(4)
    ]
    near = lax.all_to_all(
        piece, ("zh", "core", "dp"), split_axis=0, concat_axis=0, axis_index_groups=classes
    )
    swap = [(0, 1), (1, 0)]
    far = lax.ppermute(near, "core", swap)
    rest = [lax.ppermute(near, ("zh", "core", "dp"), neighbours(axis)) for axis in range(AXES)]

    params = pltpu.CompilerParams(vmem_limit_bytes=LOW)
    cost = pl.CostEstimate(flops=0, bytes_accessed=6 * 2**20, transcendentals=0)

    def stage(parts):
        return [pltpu.VMEM((H, parts * 2 * CLASS * H), F32), pltpu.SemaphoreType.DMA((2 * parts,))]

    whole = shape((H, H * H), F32)

    def place_blocks(kinds, blocks, out, name):
        count = len(kinds)
        first = out is None
        return pl.pallas_call(
            functools.partial(place_some, kinds, first),
            out_shape=whole,
            in_specs=[VMEM_SPEC] * count + ([] if first else [ANY_SPEC]),
            out_specs=ANY_SPEC,
            scratch_shapes=stage(count),
            input_output_aliases={} if first else {count: 0},
            compiler_params=params,
            cost_estimate=cost,
            name=name,
        )(*blocks, *([] if first else [out]))

    out = place_blocks(OWN_PARTS, (near, far), None, "place_own")
    rest[0], out = lax.optimization_barrier((rest[0], out))
    far_rest = [lax.ppermute(rest[0], "core", swap)]
    out = place_blocks(REST[:1], rest[:1], out, "place_x")
    for axis in (1, 2):
        rest[axis], out = lax.optimization_barrier((rest[axis], out))
        far_rest.append(lax.ppermute(rest[axis], "core", swap))
    out = place_blocks(
        REST[1:] + FAR_REST[:1], (rest[1], rest[2], far_rest[0]), out, "place_y_z_far_x"
    )
    ends = [
        shape((H, H), F32),
        shape((H, 3 * H), F32),
        shape((H, 3 * H), F32),
        shape((16, H), F32),
        shape((1, H), F32),
        shape((3, H), F32),
        shape((3, H), F32),
    ]
    grad_w_out, grad_b_out, grad_w_in, grad_w_hid, grad_ein, grad_bein, grad_bin, grad_bhid = (
        pl.pallas_call(
            place_last,
            out_shape=[whole] + ends,
            in_specs=[VMEM_SPEC] * (2 * AXES + 2) + [ANY_SPEC],
            out_specs=[ANY_SPEC] * 8,
            scratch_shapes=stage(2)
            + [pltpu.VMEM((MB * GROUP * SMALL, H), F32)]
            + [pltpu.VMEM(v.shape, v.dtype) for v in ends]
            + [pltpu.SemaphoreType.DMA((7,))],
            input_output_aliases={2 * AXES + 2: 0},
            compiler_params=params,
            cost_estimate=cost,
            name="place_last",
        )(near, far, *rest, *far_rest, out)
    )
    return (
        final,
        grad_states,
        grad_ein,
        grad_bein.reshape(H),
        grad_w_out,
        grad_b_out.reshape(H * H),
        grad_w_in,
        grad_w_hid,
        grad_bin.reshape(3 * H),
        grad_bhid.reshape(3 * H),
    )


def solution(mesh):
    wide = Mesh(mesh.devices.reshape(2, 2, GROUP), ("zh", "core", "dp"))
    split = P(("dp", "zh", "core"), None)
    in_specs = (
        P("dp", None),
        P(None, "dp"),
        P("dp"),
        P("dp"),
        P("dp"),
        P(),
        P(),
        P(),
        P(),
        P(),
        P(),
        P(),
        P(),
        P("dp", None),
    )
    out_specs = (split, split, P(), P(), P(), P(), P(), P(), P(), P())
    return jax.shard_map(local, mesh=wide, in_specs=in_specs, out_specs=out_specs, check_vma=False)
```

```python
import functools

import jax
import jax.numpy as jnp
from jax import lax
from jax.experimental import pallas as pl
from jax.experimental.pallas import tpu as pltpu
from jax.sharding import Mesh
from jax.sharding import PartitionSpec as P

H = 128
ATOMS = 32
EPM = 256
MB = 4
NODES = MB * ATOMS
PAIRS = ATOMS * ATOMS
OWN = H // MB
GAP = 129
ROWS = 144
SMALL = 8
GROUP = 32
CLASS = 8
AXES = 3
W_PARTS = 1
BF = jnp.bfloat16
F32 = jnp.float32


def spot_of(dp):
    return dp % 4, dp // 4 % 4, dp // 16


def slot_of(dp):
    x, y, z = spot_of(dp)
    return ((x + z) % 2 * 2 + (y + z) % 2) * CLASS + z * 4 + y // 2 * 2 + x // 2


DP_AT = sorted(range(GROUP), key=slot_of)


def nn(left, right):
    return jnp.dot(left, right, preferred_element_type=F32)


def nt(left, right):
    return lax.dot_general(left, right, (((1,), (1,)), ((), ())), preferred_element_type=F32)


def tn(left, right):
    return lax.dot_general(left, right, (((0,), (0,)), ((), ())), preferred_element_type=F32)


def halves(value):
    high = value.astype(BF)
    return high, (value - high.astype(F32)).astype(BF)


def fine(dot, left, right):
    lh, ll = halves(left)
    rh, rl = halves(right)
    return dot(lh, rh) + (dot(lh, rl) + dot(ll, rh))


def fine_left(dot, left, right):
    lh, ll = halves(left)
    return dot(lh, right) + dot(ll, right)


def fine_right(dot, left, right):
    rh, rl = halves(right)
    return dot(left, rh) + dot(left, rl)


def sigmoid(value):
    return 0.5 * jnp.tanh(0.5 * value) + 0.5


def gate_forward(message, states, w_input, w_hidden, b_input, b_hidden):
    from_msg = nn(message, w_input) + b_input
    from_state = nn(states, w_hidden) + b_hidden
    reset = sigmoid(from_msg[:, :H] + from_state[:, :H])
    update = sigmoid(from_msg[:, H : 2 * H] + from_state[:, H : 2 * H])
    state_cand = from_state[:, 2 * H :]
    candidate = jnp.tanh(from_msg[:, 2 * H :] + reset * state_cand)
    renewed = (1.0 - update) * candidate + update * states.astype(F32)
    return reset, update, candidate, state_cand, renewed


def gate_backward(grad, states, parts, w_input, w_hidden):
    reset, update, candidate, state_cand = parts
    act = grad * (1.0 - update) * (1.0 - candidate * candidate)
    d_reset = act * state_cand * reset * (1.0 - reset)
    d_update = grad * (states.astype(F32) - candidate) * update * (1.0 - update)
    d_in = jnp.concatenate([d_reset, d_update, act], axis=1).astype(BF)
    d_hid = jnp.concatenate([d_reset, d_update, act * reset], axis=1).astype(BF)
    g_msg = nt(d_in, w_input).astype(BF)
    grad_states = grad * update + nt(d_hid, w_hidden)
    return d_in, d_hid, g_msg, grad_states


def edge_front(features, w_edge_in, b_edge_in):
    return tn(features, w_edge_in) + b_edge_in


def local_kernel(*refs):
    ins, refs = refs[:14], refs[14:]
    (send_ref, final_ref, base_ref, grad_t_ref, pairs_out_ref), refs = refs[:5], refs[5:]
    held, refs = refs[:14], refs[14:]
    u_one, u_two, d_all, d_own, pair_h, rows_scr, small_scr, q_scr, sems, w_sems = refs
    (
        source_ref,
        target_ref,
        live_ref,
        feat_ref,
        w_ein_ref,
        b_ein_ref,
        states_ref,
        b_mat_ref,
        w_in_ref,
        w_hid_ref,
        b_in_ref,
        b_hid_ref,
        cot_ref,
        w_ref,
    ) = held
    sect = section()
    chunk = H * H // W_PARTS
    copies = [
        pltpu.make_async_copy(ins[at], held[at], sems.at[at]) for at in range(13)
    ]

    def w_copy(at):
        cols = pl.ds(at * chunk, chunk)
        return pltpu.make_async_copy(ins[13].at[:, cols], w_ref.at[:, cols], w_sems.at[at])

    for copy in copies:
        copy.start()
    for at in range(W_PARTS):
        w_copy(at).start()
    for copy in copies:
        copy.wait()

    states0 = states_ref[...]
    w_ein = w_ein_ref[...]
    b_ein = b_ein_ref[...]
    b_mat = b_mat_ref[...]
    source = source_ref[...]
    target = target_ref[...]
    live = live_ref[...]
    pair = jnp.where(live > 0, source * ATOMS + target, -1)

    slot = lax.broadcasted_iota(jnp.int32, (PAIRS, H), 0)

    def hot_pairs(first, second):
        return jnp.concatenate(
            [jnp.where(slot == row, 1.0, 0.0).astype(BF) for row in (first, second)], axis=1
        )

    def pair_rows(mol):
        pre = edge_front(feat_ref[:, mol * EPM : (mol + 1) * EPM], w_ein, b_ein)
        hidden = (pre * sigmoid(pre)).astype(BF)
        hot = hot_pairs(pair[2 * mol : 2 * mol + 1, :], pair[2 * mol + 1 : 2 * mol + 2, :])
        pair_h[mol * PAIRS : (mol + 1) * PAIRS, :] = nn(hot, hidden).astype(BF)

    for mol in range(MB):
        pair_rows(mol)

    node = lax.broadcasted_iota(jnp.int32, (NODES, H), 0)
    hot_t, hot_s = [], []
    for row in range(8):
        shift = (row // 2) * ATOMS
        keep = live[row : row + 1, :] > 0
        t_at = jnp.where(keep, target[row : row + 1, :] + shift, -1)
        s_at = source[row : row + 1, :] + shift
        hot_t.append(jnp.where(node == t_at, 1.0, 0.0).astype(BF))
        hot_s.append(jnp.where(node == s_at, 1.0, 0.0).astype(BF))
    hot_t = jnp.concatenate(hot_t, axis=1)
    hot_s = jnp.concatenate(hot_s, axis=1)
    adj = nt(hot_t, hot_s).astype(BF)
    adj_t = nt(hot_s, hot_t).astype(BF)

    def spread(states, u_ref, wait):
        def step(at):
            base = pl.multiple_of(at * 4 * H, 4 * H)
            four = [w_ref[:, pl.ds(base + q * H, H)] for q in range(4)]
            out = nt(states, jnp.concatenate(four, axis=0))
            for q in range(4):
                u_ref[pl.ds(at * 4 + q, NODES, stride=GAP), :] = out[:, q * H : (q + 1) * H]

        if wait:
            for at in range(W_PARTS):
                w_copy(at).wait()
            for at in range(32):
                step(at)
        else:

            def body(at, carry):
                step(at)
                return carry

            lax.fori_loop(0, 32, body, 0, unroll=True)

    def u_rows(u_ref, at):
        return u_ref[pl.ds(at * GAP, H), :].astype(BF)

    def gather(states, u_ref):
        side = fine_right(nt, states, b_mat)
        extra = fine_right(nn, adj, side)
        parts = []
        for mol in range(MB):

            def body(at, total, mol=mol):
                first = mol * ATOMS + at * 4
                left = jnp.concatenate(
                    [
                        pair_h[pl.ds(pl.multiple_of((first + q) * ATOMS, ATOMS), ATOMS), :]
                        for q in range(4)
                    ],
                    axis=1,
                )
                right = jnp.concatenate(
                    [u_ref[pl.ds((first + q) * GAP, H), :] for q in range(4)], axis=1
                )
                return total + fine_right(nt, left, right)

            parts.append(lax.fori_loop(0, 8, body, jnp.zeros((ATOMS, H), F32), unroll=True))
        return (jnp.concatenate(parts, axis=0) + extra).astype(BF)

    w_in = w_in_ref[...]
    w_hid = w_hid_ref[...]
    b_in = jnp.concatenate([b_in_ref[part : part + 1, :] for part in range(3)], axis=1)
    b_hid = jnp.concatenate([b_hid_ref[part : part + 1, :] for part in range(3)], axis=1)

    spread(states0, u_one, True)
    msg_one = gather(states0, u_one)
    *parts_one, renewed = gate_forward(msg_one, states0, w_in, w_hid, b_in, b_hid)
    states1 = renewed.astype(BF)
    spread(states1, u_two, False)
    msg_two = gather(states1, u_two)
    *parts_two, final = gate_forward(msg_two, states1, w_in, w_hid, b_in, b_hid)
    own_rows = pl.ds(pl.multiple_of(sect * ATOMS, ATOMS), ATOMS)
    rows_scr[...] = final
    final_ref[...] = rows_scr[own_rows, :]

    d_in2, d_hid2, g_two, back_one = gate_backward(cot_ref[...], states1, parts_two, w_in, w_hid)
    g_two_t = g_two.astype(F32).T.astype(BF)

    for mol in range(MB):
        left = g_two_t[:, mol * ATOMS : (mol + 1) * ATOMS]

        def body(at, carry, mol=mol, left=left):
            first = mol * ATOMS + at * 4
            right = jnp.concatenate(
                [
                    pair_h[pl.ds(pl.multiple_of((first + q) * ATOMS, ATOMS), ATOMS), :]
                    for q in range(4)
                ],
                axis=1,
            )
            out = nn(left, right)
            for q in range(4):
                d_all[pl.ds(first + q, H, stride=GAP), :] = out[:, q * H : (q + 1) * H]
            return carry

        lax.fori_loop(0, 8, body, 0, unroll=True)

    def back_body(at, total):
        base = pl.multiple_of(at * 4 * H, 4 * H)
        left = jnp.concatenate(
            [d_all[pl.ds((at * 4 + q) * GAP, NODES), :].astype(BF) for q in range(4)], axis=1
        )
        right = jnp.concatenate([w_ref[:, pl.ds(base + q * H, H)] for q in range(4)], axis=0)
        return total + nn(left, right)

    back_msg = lax.fori_loop(0, 32, back_body, jnp.zeros((NODES, H), F32), unroll=True)
    share = nn(adj_t, g_two)
    grad_one = back_one + back_msg + fine(nn, share, b_mat)

    d_in1, d_hid1, g_one, back_zero = gate_backward(grad_one, states0, parts_one, w_in, w_hid)
    rows_scr[...] = g_one.astype(F32).T
    g_one_t = rows_scr[...].astype(BF)
    g_one_own = rows_scr[own_rows, :].astype(BF)

    for mol in range(MB):
        left = g_one_own[:, mol * ATOMS : (mol + 1) * ATOMS]

        def body(at, carry, mol=mol, left=left):
            first = mol * ATOMS + at * 4
            right = jnp.concatenate(
                [
                    pair_h[pl.ds(pl.multiple_of((first + q) * ATOMS, ATOMS), ATOMS), :]
                    for q in range(4)
                ],
                axis=1,
            )
            out = nn(left, right)
            for q in range(4):
                d_own[pl.ds(first + q, OWN, stride=GAP), :] = out[:, q * H : (q + 1) * H]
            return carry

        lax.fori_loop(0, 8, body, 0, unroll=True)

    both_t = jnp.concatenate([states0.astype(F32).T, states1.astype(F32).T], axis=1).astype(BF)

    for at in range(OWN // 2):
        right = jnp.concatenate(
            [
                jnp.concatenate(
                    [
                        d_own[pl.ds((at * 2 + q) * GAP, NODES), :].astype(BF),
                        d_all[pl.ds((sect * OWN + at * 2 + q) * GAP, NODES), :].astype(BF),
                    ],
                    axis=0,
                )
                for q in range(2)
            ],
            axis=1,
        )
        out = nn(both_t, right).astype(BF)
        for q in range(2):
            send_ref[DP_AT[at * 2 + q], 0:H, :] = out[:, q * H : (q + 1) * H]

    rows_scr[...] = g_one.astype(F32)
    g1 = rows_scr[own_rows, :].astype(BF)
    rows_scr[...] = g_two.astype(F32)
    g2 = rows_scr[own_rows, :].astype(BF)
    g_both = jnp.concatenate([g1, g2], axis=1)

    def q_body(at, carry):
        first = sect * ATOMS + at * 2
        right = jnp.concatenate(
            [
                jnp.concatenate([u_rows(u_one, first + q), u_rows(u_two, first + q)], axis=0)
                for q in range(2)
            ],
            axis=1,
        )
        out = nn(g_both, right).astype(BF)
        for q in range(2):
            q_scr[pl.ds(pl.multiple_of((at * 2 + q) * ATOMS, ATOMS), ATOMS), :] = out[
                :, q * H : (q + 1) * H
            ]
        return carry

    lax.fori_loop(0, 16, q_body, 0, unroll=True)
    own_cols = pl.ds(pl.multiple_of(sect * EPM, EPM), EPM)
    feat_own = feat_ref[:, own_cols]
    pre_own = edge_front(feat_own, w_ein, b_ein)
    sig = sigmoid(pre_own)
    slope = sig * (1.0 + pre_own * (1.0 - sig))
    rows_scr[0:8, :] = pair.astype(F32)
    pair_own = rows_scr[pl.ds(sect * 2, 2), :].astype(jnp.int32)
    hot = hot_pairs(pair_own[0:1, :], pair_own[1:2, :])
    g_pre = tn(hot, q_scr[...]) * slope

    g_share_t = nn(g_one_t, adj), nn(g_two_t, adj)
    grad_b_out = fine_left(nn, g_share_t[0], states0) + fine_left(nn, g_share_t[1], states1)
    rows_scr[...] = grad_b_out
    small_scr[0:32, :] = rows_scr[own_rows, :]
    both_rows = jnp.concatenate(
        [msg_one.astype(F32).T, msg_two.astype(F32).T], axis=1
    )
    d_in_both = jnp.concatenate([d_in1, d_in2], axis=0)
    d_hid_both = jnp.concatenate([d_hid1, d_hid2], axis=0)
    for at, (rows_t, d_both) in enumerate(
        ((both_rows, d_in_both), (both_t.astype(F32), d_hid_both))
    ):
        rows_scr[...] = rows_t[:, :H]
        first = rows_scr[own_rows, :]
        rows_scr[...] = rows_t[:, H:]
        left = jnp.concatenate([first, rows_scr[own_rows, :]], axis=1).astype(BF)
        out = nn(left, d_both)
        for part in range(3):
            row = 32 + at * 96 + part * 32
            small_scr[row : row + 32, :] = out[:, part * H : (part + 1) * H]
    small_scr[224:240, :] = fine_right(nn, feat_own, g_pre)
    small_scr[240:256, :] = jnp.zeros((16, H), F32)
    small_scr[240:241, :] = jnp.sum(g_pre, axis=0, keepdims=True)
    for at, pair_d in enumerate(((d_in1, d_in2), (d_hid1, d_hid2))):
        for part in range(3):
            cols = slice(part * H, (part + 1) * H)
            rows_scr[...] = pair_d[0][:, cols].astype(F32) + pair_d[1][:, cols].astype(F32)
            row = 241 + at * 3 + part
            small_scr[row : row + 1, :] = jnp.sum(rows_scr[own_rows, :], axis=0, keepdims=True)
    for at in range(GROUP):
        high, low = halves(small_scr[at * SMALL : (at + 1) * SMALL, :])
        both = jnp.concatenate([high.astype(F32), low.astype(F32)], axis=0)
        send_ref[DP_AT[at], H:ROWS, :] = both.astype(BF)

    rows_scr[...] = back_zero + fine(nn, nn(adj_t, g_one), b_mat)
    base_ref[...] = rows_scr[own_rows, :]
    grad_t_ref[...] = g_one_t
    pairs_out_ref[...] = pair_h[pl.ds(pl.multiple_of(sect * PAIRS, PAIRS), PAIRS), :]


def sum_kernel(got_ref, out_ref):
    def body(at, total):
        return total + got_ref[at].astype(F32)

    total = lax.fori_loop(1, GROUP, body, got_ref[0].astype(F32), unroll=True)
    high, low = halves(total[H : H + SMALL] + total[H + SMALL :])
    piece = jnp.concatenate([total[:H].T, high.astype(F32), low.astype(F32)], axis=0).astype(BF)

    for at in range(2 * CLASS):
        out_ref[at] = piece


def states_kernel(base_ref, grad_t_ref, pairs_ref, w_ref, out_ref, d_all, rows_scr):
    sect = section()
    rows_scr[...] = grad_t_ref[...].astype(F32).T
    own = rows_scr[pl.ds(pl.multiple_of(sect * ATOMS, ATOMS), ATOMS), :]
    left = own.T.astype(BF)
    gap = ATOMS + 1

    def body(at, carry):
        right = jnp.concatenate(
            [
                pairs_ref[pl.ds(pl.multiple_of((at * 4 + q) * ATOMS, ATOMS), ATOMS), :]
                for q in range(4)
            ],
            axis=1,
        )
        out = nn(left, right)
        for q in range(4):
            d_all[pl.ds(at * 4 + q, H, stride=gap), :] = out[:, q * H : (q + 1) * H]
        return carry

    lax.fori_loop(0, 8, body, 0, unroll=True)

    def back_body(at, total):
        base = pl.multiple_of(at * 4 * H, 4 * H)
        left = jnp.concatenate(
            [d_all[pl.ds((at * 4 + q) * gap, ATOMS), :].astype(BF) for q in range(4)], axis=1
        )
        right = jnp.concatenate([w_ref[:, pl.ds(base + q * H, H)] for q in range(4)], axis=0)
        return total + nn(left, right)

    out_ref[...] = lax.fori_loop(0, 32, back_body, base_ref[...], unroll=True)


def place_rows(parts, out_hbm, stage, sem):
    copies = []
    for part, (ref, other_core, change) in enumerate(parts):
        core, kind = place_of(other_core, change)
        for half in range(2):
            at_col = ((half * 2 + core) * GROUP + kind * CLASS) * H
            low = (part * 2 + half) * CLASS * H
            cols = pl.ds(low, CLASS * H)
            for dev in range(CLASS):
                for row in range(0, H, 16):
                    stage[row : row + 16, low + dev * H : low + (dev + 1) * H] = ref[
                        half * CLASS + dev, row : row + 16, :
                    ].astype(F32)
            copies.append(
                pltpu.make_async_copy(
                    stage.at[:, cols],
                    out_hbm.at[:, pl.ds(pl.multiple_of(at_col, CLASS * H), CLASS * H)],
                    sem.at[len(copies)],
                )
            )
            copies[-1].start()
    return copies


def place_of(other_core, change):
    core, dp = lax.axis_index("core"), lax.axis_index("dp")
    z = jnp.right_shift(dp, 4)
    kind = jnp.bitwise_and(dp + z, 1) * 2 + jnp.bitwise_and(jnp.right_shift(dp, 2) + z, 1)
    return (1 - core if other_core else core), jnp.bitwise_xor(kind, change)


def section():
    return lax.axis_index("zh") * 2 + lax.axis_index("core")


CHANGES = (2, 1, 3)


OWN_PARTS = ((False, 0), (True, 0))
REST = tuple((False, change) for change in CHANGES)
FAR_REST = tuple((True, change) for change in CHANGES)


def place_some(kinds, first, *refs):
    count = len(kinds)
    out_hbm, stage, sems = refs[count + (0 if first else 1) :]
    parts = [(ref,) + kind for ref, kind in zip(refs, kinds)]
    for copy in place_rows(parts, out_hbm, stage, sems):
        copy.wait()


def place_last(*refs):
    blocks, refs = refs[:8], refs[9:]
    out_hbm, *ends = refs[:8]
    stage, sems, small, gb, gi, gh, ge, be, bi, bh, end_sems = refs[8:]
    blocks = [(ref,) + kind for ref, kind in zip(blocks, OWN_PARTS + REST + FAR_REST)]
    copies = place_rows(blocks[6:], out_hbm, stage, sems)
    for ref, other_core, change in blocks:
        core, kind = place_of(other_core, change)
        for at in range(2 * CLASS):
            block = ((at // CLASS) * 2 + core) * GROUP + kind * CLASS + at % CLASS
            row = pl.multiple_of(block * SMALL, SMALL)
            both = ref[at, H:ROWS, :].astype(F32)
            small[pl.ds(row, SMALL), :] = both[:SMALL] + both[SMALL:]
    misc = jnp.zeros((32, H), F32)
    for sect in range(MB):
        base = sect * GROUP * SMALL
        rows = slice(sect * 32, (sect + 1) * 32)
        gb[rows, :] = small[base : base + 32, :]
        for part in range(3):
            cols = slice(part * H, (part + 1) * H)
            row = base + 32 + part * 32
            gi[rows, cols] = small[row : row + 32, :]
            gh[rows, cols] = small[row + 96 : row + 128, :]
        misc = misc + small[base + 224 : base + 256, :]
    ge[...] = misc[0:16]
    be[...] = misc[16:17]
    bi[...] = misc[17:20]
    bh[...] = misc[20:23]
    end_copies = [
        pltpu.make_async_copy(here, there, end_sems.at[at])
        for at, (here, there) in enumerate(zip((gb, gi, gh, ge, be, bi, bh), ends))
    ]
    for copy in end_copies:
        copy.start()
    for copy in copies + end_copies:
        copy.wait()


VMEM_SPEC = pl.BlockSpec(memory_space=pltpu.VMEM)
ANY_SPEC = pl.BlockSpec(memory_space=pl.ANY)
BIG = 60 * 2**20
LOW = 8 * 2**20
shape = jax.ShapeDtypeStruct


def run_layers(operands):
    return pl.pallas_call(
        local_kernel,
        out_shape=(
            shape((GROUP, ROWS, H), BF),
            shape((ATOMS, H), F32),
            shape((ATOMS, H), F32),
            shape((H, NODES), BF),
            shape((PAIRS, H), BF),
        ),
        in_specs=[ANY_SPEC] * 14,
        out_specs=(VMEM_SPEC,) * 5,
        scratch_shapes=[pltpu.VMEM(v.shape, v.dtype) for v in operands]
        + [
            pltpu.VMEM(((NODES + 1) * GAP, H), F32),
            pltpu.VMEM(((NODES + 1) * GAP, H), F32),
            pltpu.VMEM(((H + 1) * GAP, H), F32),
            pltpu.VMEM(((OWN + 1) * GAP, H), F32),
            pltpu.VMEM((MB * PAIRS, H), BF),
            pltpu.VMEM((NODES, H), F32),
            pltpu.VMEM((GROUP * SMALL, H), F32),
            pltpu.VMEM((PAIRS, H), BF),
            pltpu.SemaphoreType.DMA((13,)),
            pltpu.SemaphoreType.DMA((W_PARTS,)),
        ],
        compiler_params=pltpu.CompilerParams(vmem_limit_bytes=BIG),
        name="layers",
    )(*operands)


def neighbours(axis):
    pairs = []
    for zh in range(2):
        for core in range(2):
            for dp in range(GROUP):
                x, y, z = spot_of(dp)
                spot = [x, y, zh * 2 + z]
                spot[axis] = (spot[axis] + (-1 if core else 1)) % 4
                x, y, z = spot
                pairs.append(
                    (
                        z // 2 * 64 + core * GROUP + z % 2 * 16 + y * 4 + x,
                        zh * 64 + core * GROUP + dp,
                    )
                )
    return pairs


def local(
    node_states,
    edge_features,
    edge_source,
    edge_target,
    edge_live,
    w_edge_in,
    b_edge_in,
    w_edge_out,
    b_edge_out,
    w_input,
    w_hidden,
    b_input,
    b_hidden,
    cotangent,
):
    operands = [v.reshape(8, 128) for v in (edge_source, edge_target, edge_live)] + [
        edge_features,
        w_edge_in,
        b_edge_in.reshape(1, H),
        node_states,
        b_edge_out.reshape(H, H),
        w_input,
        w_hidden,
        b_input.reshape(3, H),
        b_hidden.reshape(3, H),
        cotangent,
        w_edge_out,
    ]

    send, final, base, grad_t, pairs = run_layers(operands)
    grad_states = pl.pallas_call(
        states_kernel,
        out_shape=shape((ATOMS, H), F32),
        in_specs=[VMEM_SPEC] * 4,
        out_specs=VMEM_SPEC,
        scratch_shapes=[pltpu.VMEM(((H + 1) * (ATOMS + 1), H), F32), pltpu.VMEM((NODES, H), F32)],
        compiler_params=pltpu.CompilerParams(vmem_limit_bytes=LOW),
        cost_estimate=pl.CostEstimate(
            flops=2 * ATOMS * H * H * H, bytes_accessed=2 * H * H * H, transcendentals=0
        ),
        name="states_back",
    )(base, grad_t, pairs, w_edge_out)
    got = lax.all_to_all(send, "dp", split_axis=0, concat_axis=0)
    got, grad_states = lax.optimization_barrier((got, grad_states))
    piece = pl.pallas_call(
        sum_kernel,
        out_shape=shape((2 * CLASS, ROWS, H), BF),
        in_specs=[VMEM_SPEC],
        out_specs=VMEM_SPEC,
        compiler_params=pltpu.CompilerParams(vmem_limit_bytes=LOW),
        name="sum_parts",
    )(got)
    classes = [
        [zh * 64 + c * GROUP + DP_AT[kind * CLASS + at] for zh in range(2) for at in range(CLASS)]
        for c in range(2)
        for kind in range(4)
    ]
    near = lax.all_to_all(
        piece, ("zh", "core", "dp"), split_axis=0, concat_axis=0, axis_index_groups=classes
    )
    swap = [(0, 1), (1, 0)]
    far = lax.ppermute(near, "core", swap)
    rest = [lax.ppermute(near, ("zh", "core", "dp"), neighbours(axis)) for axis in range(AXES)]

    params = pltpu.CompilerParams(vmem_limit_bytes=LOW)
    cost = pl.CostEstimate(flops=0, bytes_accessed=6 * 2**20, transcendentals=0)

    def stage(parts):
        return [pltpu.VMEM((H, parts * 2 * CLASS * H), F32), pltpu.SemaphoreType.DMA((2 * parts,))]

    whole = shape((H, H * H), F32)

    def place_blocks(kinds, blocks, out, name):
        count = len(kinds)
        first = out is None
        return pl.pallas_call(
            functools.partial(place_some, kinds, first),
            out_shape=whole,
            in_specs=[VMEM_SPEC] * count + ([] if first else [ANY_SPEC]),
            out_specs=ANY_SPEC,
            scratch_shapes=stage(count),
            input_output_aliases={} if first else {count: 0},
            compiler_params=params,
            cost_estimate=cost,
            name=name,
        )(*blocks, *([] if first else [out]))

    out = place_blocks(OWN_PARTS, (near, far), None, "place_own")
    rest[0], out = lax.optimization_barrier((rest[0], out))
    far_rest = [lax.ppermute(rest[0], "core", swap)]
    out = place_blocks(REST[:1], rest[:1], out, "place_x")
    for axis in (1, 2):
        rest[axis], out = lax.optimization_barrier((rest[axis], out))
        far_rest.append(lax.ppermute(rest[axis], "core", swap))
    out = place_blocks(
        REST[1:] + FAR_REST[:1], (rest[1], rest[2], far_rest[0]), out, "place_y_z_far_x"
    )
    ends = [
        shape((H, H), F32),
        shape((H, 3 * H), F32),
        shape((H, 3 * H), F32),
        shape((16, H), F32),
        shape((1, H), F32),
        shape((3, H), F32),
        shape((3, H), F32),
    ]
    grad_w_out, grad_b_out, grad_w_in, grad_w_hid, grad_ein, grad_bein, grad_bin, grad_bhid = (
        pl.pallas_call(
            place_last,
            out_shape=[whole] + ends,
            in_specs=[VMEM_SPEC] * (2 * AXES + 2) + [ANY_SPEC],
            out_specs=[ANY_SPEC] * 8,
            scratch_shapes=stage(2)
            + [pltpu.VMEM((MB * GROUP * SMALL, H), F32)]
            + [pltpu.VMEM(v.shape, v.dtype) for v in ends]
            + [pltpu.SemaphoreType.DMA((7,))],
            input_output_aliases={2 * AXES + 2: 0},
            compiler_params=params,
            cost_estimate=cost,
            name="place_last",
        )(near, far, *rest, *far_rest, out)
    )
    return (
        final,
        grad_states,
        grad_ein,
        grad_bein.reshape(H),
        grad_w_out,
        grad_b_out.reshape(H * H),
        grad_w_in,
        grad_w_hid,
        grad_bin.reshape(3 * H),
        grad_bhid.reshape(3 * H),
    )


def solution(mesh):
    wide = Mesh(mesh.devices.reshape(2, 2, GROUP), ("zh", "core", "dp"))
    split = P(("dp", "zh", "core"), None)
    in_specs = (
        P("dp", None),
        P(None, "dp"),
        P("dp"),
        P("dp"),
        P("dp"),
        P(),
        P(),
        P(),
        P(),
        P(),
        P(),
        P(),
        P(),
        P("dp", None),
    )
    out_specs = (split, split, P(), P(), P(), P(), P(), P(), P(), P())
    return jax.shard_map(local, mesh=wide, in_specs=in_specs, out_specs=out_specs, check_vma=False)
```

```python
import functools

import jax
import jax.numpy as jnp
from jax import lax
from jax.experimental import pallas as pl
from jax.experimental.pallas import tpu as pltpu
from jax.sharding import Mesh
from jax.sharding import PartitionSpec as P

H = 128
ATOMS = 32
EPM = 256
MB = 4
NODES = MB * ATOMS
PAIRS = ATOMS * ATOMS
OWN = H // MB
GAP = 129
ROWS = 136
SMALL = 8
GROUP = 32
CLASS = 8
AXES = 3
BF = jnp.bfloat16
F32 = jnp.float32


def spot_of(dp):
    return dp % 4, dp // 4 % 4, dp // 16


def slot_of(dp):
    x, y, z = spot_of(dp)
    return ((x + z) % 2 * 2 + (y + z) % 2) * CLASS + z * 4 + y // 2 * 2 + x // 2


DP_AT = sorted(range(GROUP), key=slot_of)


def nn(left, right):
    return jnp.dot(left, right, preferred_element_type=F32)


def nt(left, right):
    return lax.dot_general(left, right, (((1,), (1,)), ((), ())), preferred_element_type=F32)


def tn(left, right):
    return lax.dot_general(left, right, (((0,), (0,)), ((), ())), preferred_element_type=F32)


def halves(value):
    high = value.astype(BF)
    return high, (value - high.astype(F32)).astype(BF)


def fine(dot, left, right):
    lh, ll = halves(left)
    rh, rl = halves(right)
    return dot(lh, rh) + (dot(lh, rl) + dot(ll, rh))


def fine_left(dot, left, right):
    lh, ll = halves(left)
    return dot(lh, right) + dot(ll, right)


def fine_right(dot, left, right):
    rh, rl = halves(right)
    return dot(left, rh) + dot(left, rl)


def sigmoid(value):
    return 0.5 * jnp.tanh(0.5 * value) + 0.5


def gate_forward(message, states, w_input, w_hidden, b_input, b_hidden):
    both = jnp.concatenate([message, states], axis=1)
    w_both = jnp.concatenate([w_input[:, : 2 * H], w_hidden[:, : 2 * H]], axis=0)
    gates = sigmoid(nn(both, w_both) + (b_input + b_hidden)[:, : 2 * H])
    reset, update = gates[:, :H], gates[:, H:]
    state_cand = nn(states, w_hidden[:, 2 * H :]) + b_hidden[:, 2 * H :]
    candidate = jnp.tanh(nn(message, w_input[:, 2 * H :]) + b_input[:, 2 * H :] + reset * state_cand)
    renewed = (1.0 - update) * candidate + update * states.astype(F32)
    return reset, update, candidate, state_cand, renewed


def gate_backward(grad, states, parts, w_input, w_hidden):
    reset, update, candidate, state_cand = parts
    act = grad * (1.0 - update) * (1.0 - candidate * candidate)
    d_reset = act * state_cand * reset * (1.0 - reset)
    d_update = grad * (states.astype(F32) - candidate) * update * (1.0 - update)
    d_in = jnp.concatenate([d_reset, d_update, act], axis=1).astype(BF)
    d_hid = jnp.concatenate([d_reset, d_update, act * reset], axis=1).astype(BF)
    g_msg = nt(d_in, w_input).astype(BF)
    grad_states = grad * update + nt(d_hid, w_hidden)
    return d_in, d_hid, g_msg, grad_states


def edge_front(features, w_edge_in, b_edge_in):
    return tn(features, w_edge_in) + b_edge_in


def local_kernel(*refs):
    ins, refs = refs[:14], refs[14:]
    (send_ref, final_ref, base_ref, grad_t_ref, pairs_out_ref), refs = refs[:5], refs[5:]
    held, refs = refs[:14], refs[14:]
    u_one, u_two, d_all, d_own, pair_h, rows_scr, small_scr, q_scr, sems, w_sem = refs
    (
        source_ref,
        target_ref,
        live_ref,
        feat_ref,
        w_ein_ref,
        b_ein_ref,
        states_ref,
        b_mat_ref,
        w_in_ref,
        w_hid_ref,
        b_in_ref,
        b_hid_ref,
        cot_ref,
        w_ref,
    ) = held
    sect = section()
    copies = [
        pltpu.make_async_copy(ins[at], held[at], sems.at[at]) for at in range(13)
    ]

    for copy in copies[:7]:
        copy.start()
    w_copy = pltpu.make_async_copy(ins[13], w_ref, w_sem)
    w_copy.start()
    for copy in copies[7:]:
        copy.start()
    for copy in copies[:7]:
        copy.wait()

    states0 = states_ref[...]
    w_ein = w_ein_ref[...]
    b_ein = b_ein_ref[...]
    source = source_ref[...]
    target = target_ref[...]
    live = live_ref[...]
    pair = jnp.where(live > 0, source * ATOMS + target, -1)

    slot = lax.broadcasted_iota(jnp.int32, (PAIRS, H), 0)

    def hot_pairs(first, second):
        return jnp.concatenate(
            [jnp.where(slot == row, 1.0, 0.0).astype(BF) for row in (first, second)], axis=1
        )

    def pair_rows(mol):
        pre = edge_front(feat_ref[:, mol * EPM : (mol + 1) * EPM], w_ein, b_ein)
        hidden = (pre * sigmoid(pre)).astype(BF)
        hot = hot_pairs(pair[2 * mol : 2 * mol + 1, :], pair[2 * mol + 1 : 2 * mol + 2, :])
        pair_h[mol * PAIRS : (mol + 1) * PAIRS, :] = nn(hot, hidden).astype(BF)

    for mol in range(MB):
        pair_rows(mol)

    node = lax.broadcasted_iota(jnp.int32, (NODES, H), 0)
    hot_t, hot_s = [], []
    for row in range(8):
        shift = (row // 2) * ATOMS
        keep = live[row : row + 1, :] > 0
        t_at = jnp.where(keep, target[row : row + 1, :] + shift, -1)
        s_at = source[row : row + 1, :] + shift
        hot_t.append(jnp.where(node == t_at, 1.0, 0.0).astype(BF))
        hot_s.append(jnp.where(node == s_at, 1.0, 0.0).astype(BF))
    hot_t = jnp.concatenate(hot_t, axis=1)
    hot_s = jnp.concatenate(hot_s, axis=1)
    adj = nt(hot_t, hot_s).astype(BF)
    adj_t = nt(hot_s, hot_t).astype(BF)

    def spread(states, u_ref, wait):
        def step(at):
            base = pl.multiple_of(at * 4 * H, 4 * H)
            four = [w_ref[:, pl.ds(base + q * H, H)] for q in range(4)]
            out = nt(states, jnp.concatenate(four, axis=0))
            for q in range(4):
                u_ref[pl.ds(at * 4 + q, NODES, stride=GAP), :] = out[:, q * H : (q + 1) * H]

        if wait:
            w_copy.wait()
            for at in range(32):
                step(at)
        else:

            def body(at, carry):
                step(at)
                return carry

            lax.fori_loop(0, 32, body, 0, unroll=True)

    def u_rows(u_ref, at):
        return u_ref[pl.ds(at * GAP, H), :].astype(BF)

    def gather(states, u_ref):
        side = fine_right(nt, states, b_mat)
        extra = fine_right(nn, adj, side)
        parts = []
        for mol in range(MB):

            def body(at, total, mol=mol):
                first = mol * ATOMS + at * 4
                left = jnp.concatenate(
                    [
                        pair_h[pl.ds(pl.multiple_of((first + q) * ATOMS, ATOMS), ATOMS), :]
                        for q in range(4)
                    ],
                    axis=1,
                )
                right = jnp.concatenate([u_rows(u_ref, first + q) for q in range(4)], axis=1)
                return total + nt(left, right)

            parts.append(lax.fori_loop(0, 8, body, jnp.zeros((ATOMS, H), F32), unroll=True))
        return (jnp.concatenate(parts, axis=0) + extra).astype(BF)

    spread(states0, u_one, True)
    for copy in copies[7:]:
        copy.wait()
    b_mat = b_mat_ref[...]
    w_in = w_in_ref[...]
    w_hid = w_hid_ref[...]
    b_in = jnp.concatenate([b_in_ref[part : part + 1, :] for part in range(3)], axis=1)
    b_hid = jnp.concatenate([b_hid_ref[part : part + 1, :] for part in range(3)], axis=1)

    msg_one = gather(states0, u_one)
    *parts_one, renewed = gate_forward(msg_one, states0, w_in, w_hid, b_in, b_hid)
    states1 = renewed.astype(BF)
    spread(states1, u_two, False)
    msg_two = gather(states1, u_two)
    *parts_two, final = gate_forward(msg_two, states1, w_in, w_hid, b_in, b_hid)
    own_rows = pl.ds(pl.multiple_of(sect * ATOMS, ATOMS), ATOMS)
    rows_scr[...] = final
    final_ref[...] = rows_scr[own_rows, :]

    d_in2, d_hid2, g_two, back_one = gate_backward(cot_ref[...], states1, parts_two, w_in, w_hid)
    g_two_t = g_two.astype(F32).T.astype(BF)

    for mol in range(MB):
        left = g_two_t[:, mol * ATOMS : (mol + 1) * ATOMS]

        def body(at, carry, mol=mol, left=left):
            first = mol * ATOMS + at * 4
            right = jnp.concatenate(
                [
                    pair_h[pl.ds(pl.multiple_of((first + q) * ATOMS, ATOMS), ATOMS), :]
                    for q in range(4)
                ],
                axis=1,
            )
            out = nn(left, right)
            for q in range(4):
                d_all[pl.ds(first + q, H, stride=GAP), :] = out[:, q * H : (q + 1) * H]
            return carry

        lax.fori_loop(0, 8, body, 0, unroll=True)

    def back_body(at, total):
        base = pl.multiple_of(at * 4 * H, 4 * H)
        left = jnp.concatenate(
            [d_all[pl.ds((at * 4 + q) * GAP, NODES), :].astype(BF) for q in range(4)], axis=1
        )
        right = jnp.concatenate([w_ref[:, pl.ds(base + q * H, H)] for q in range(4)], axis=0)
        return total + nn(left, right)

    back_msg = lax.fori_loop(0, 32, back_body, jnp.zeros((NODES, H), F32), unroll=True)
    share = nn(adj_t, g_two)
    grad_one = back_one + back_msg + fine(nn, share, b_mat)

    d_in1, d_hid1, g_one, back_zero = gate_backward(grad_one, states0, parts_one, w_in, w_hid)
    rows_scr[...] = g_one.astype(F32).T
    g_one_t = rows_scr[...].astype(BF)
    g_one_own = rows_scr[own_rows, :].astype(BF)

    for mol in range(MB):
        left = g_one_own[:, mol * ATOMS : (mol + 1) * ATOMS]

        def body(at, carry, mol=mol, left=left):
            first = mol * ATOMS + at * 4
            right = jnp.concatenate(
                [
                    pair_h[pl.ds(pl.multiple_of((first + q) * ATOMS, ATOMS), ATOMS), :]
                    for q in range(4)
                ],
                axis=1,
            )
            out = nn(left, right)
            for q in range(4):
                d_own[pl.ds(first + q, OWN, stride=GAP), :] = out[:, q * H : (q + 1) * H]
            return carry

        lax.fori_loop(0, 8, body, 0, unroll=True)

    both_t = jnp.concatenate([states0.astype(F32).T, states1.astype(F32).T], axis=1).astype(BF)

    for at in range(OWN // 2):
        right = jnp.concatenate(
            [
                jnp.concatenate(
                    [
                        d_own[pl.ds((at * 2 + q) * GAP, NODES), :].astype(BF),
                        d_all[pl.ds((sect * OWN + at * 2 + q) * GAP, NODES), :].astype(BF),
                    ],
                    axis=0,
                )
                for q in range(2)
            ],
            axis=1,
        )
        out = nn(both_t, right).astype(BF)
        for q in range(2):
            send_ref[DP_AT[at * 2 + q], 0:H, :] = out[:, q * H : (q + 1) * H]

    rows_scr[...] = g_one.astype(F32)
    g1 = rows_scr[own_rows, :].astype(BF)
    rows_scr[...] = g_two.astype(F32)
    g2 = rows_scr[own_rows, :].astype(BF)
    g_both = jnp.concatenate([g1, g2], axis=1)

    def q_body(at, carry):
        first = sect * ATOMS + at * 2
        right = jnp.concatenate(
            [
                jnp.concatenate([u_rows(u_one, first + q), u_rows(u_two, first + q)], axis=0)
                for q in range(2)
            ],
            axis=1,
        )
        out = nn(g_both, right).astype(BF)
        for q in range(2):
            q_scr[pl.ds(pl.multiple_of((at * 2 + q) * ATOMS, ATOMS), ATOMS), :] = out[
                :, q * H : (q + 1) * H
            ]
        return carry

    lax.fori_loop(0, 16, q_body, 0, unroll=True)
    own_cols = pl.ds(pl.multiple_of(sect * EPM, EPM), EPM)
    feat_own = feat_ref[:, own_cols]
    pre_own = edge_front(feat_own, w_ein, b_ein)
    sig = sigmoid(pre_own)
    slope = sig * (1.0 + pre_own * (1.0 - sig))
    rows_scr[0:8, :] = pair.astype(F32)
    pair_own = rows_scr[pl.ds(sect * 2, 2), :].astype(jnp.int32)
    hot = hot_pairs(pair_own[0:1, :], pair_own[1:2, :])
    g_pre = tn(hot, q_scr[...]) * slope

    g_share_t = nn(g_one_t, adj), nn(g_two_t, adj)
    grad_b_out = fine_left(nn, g_share_t[0], states0) + fine_left(nn, g_share_t[1], states1)
    rows_scr[...] = grad_b_out
    small_scr[0:32, :] = rows_scr[own_rows, :]
    both_rows = jnp.concatenate(
        [msg_one.astype(F32).T, msg_two.astype(F32).T], axis=1
    )
    d_in_both = jnp.concatenate([d_in1, d_in2], axis=0)
    d_hid_both = jnp.concatenate([d_hid1, d_hid2], axis=0)
    for at, (rows_t, d_both) in enumerate(
        ((both_rows, d_in_both), (both_t.astype(F32), d_hid_both))
    ):
        rows_scr[...] = rows_t[:, :H]
        first = rows_scr[own_rows, :]
        rows_scr[...] = rows_t[:, H:]
        left = jnp.concatenate([first, rows_scr[own_rows, :]], axis=1).astype(BF)
        out = nn(left, d_both)
        for part in range(3):
            row = 32 + at * 96 + part * 32
            small_scr[row : row + 32, :] = out[:, part * H : (part + 1) * H]
    small_scr[224:240, :] = fine_right(nn, feat_own, g_pre)
    small_scr[240:256, :] = jnp.zeros((16, H), F32)
    small_scr[240:241, :] = jnp.sum(g_pre, axis=0, keepdims=True)
    for at, pair_d in enumerate(((d_in1, d_in2), (d_hid1, d_hid2))):
        for part in range(3):
            cols = slice(part * H, (part + 1) * H)
            rows_scr[...] = pair_d[0][:, cols].astype(F32) + pair_d[1][:, cols].astype(F32)
            row = 241 + at * 3 + part
            small_scr[row : row + 1, :] = jnp.sum(rows_scr[own_rows, :], axis=0, keepdims=True)
    for at in range(GROUP):
        send_ref[DP_AT[at], H:ROWS, :] = small_scr[at * SMALL : (at + 1) * SMALL, :].astype(BF)

    rows_scr[...] = back_zero + fine(nn, nn(adj_t, g_one), b_mat)
    base_ref[...] = rows_scr[own_rows, :]
    grad_t_ref[...] = g_one_t
    pairs_out_ref[...] = pair_h[pl.ds(pl.multiple_of(sect * PAIRS, PAIRS), PAIRS), :]


def sum_kernel(got_ref, out_ref):
    def body(at, total):
        return total + got_ref[at].astype(F32)

    total = lax.fori_loop(1, GROUP, body, got_ref[0].astype(F32), unroll=True)
    piece = jnp.concatenate([total[:H].T, total[H:]], axis=0).astype(BF)

    for at in range(2 * CLASS):
        out_ref[at] = piece


def states_kernel(base_ref, grad_t_ref, pairs_ref, w_ref, out_ref, d_all, rows_scr):
    sect = section()
    rows_scr[...] = grad_t_ref[...].astype(F32).T
    own = rows_scr[pl.ds(pl.multiple_of(sect * ATOMS, ATOMS), ATOMS), :]
    left = own.T.astype(BF)
    gap = ATOMS + 1

    def body(at, carry):
        right = jnp.concatenate(
            [
                pairs_ref[pl.ds(pl.multiple_of((at * 4 + q) * ATOMS, ATOMS), ATOMS), :]
                for q in range(4)
            ],
            axis=1,
        )
        out = nn(left, right)
        for q in range(4):
            d_all[pl.ds(at * 4 + q, H, stride=gap), :] = out[:, q * H : (q + 1) * H]
        return carry

    lax.fori_loop(0, 8, body, 0, unroll=True)

    def back_body(at, total):
        base = pl.multiple_of(at * 4 * H, 4 * H)
        left = jnp.concatenate(
            [d_all[pl.ds((at * 4 + q) * gap, ATOMS), :].astype(BF) for q in range(4)], axis=1
        )
        right = jnp.concatenate([w_ref[:, pl.ds(base + q * H, H)] for q in range(4)], axis=0)
        return total + nn(left, right)

    out_ref[...] = lax.fori_loop(0, 32, back_body, base_ref[...], unroll=True)


def place_rows(parts, out_hbm, stage, sem):
    copies = []
    for part, (ref, other_core, change) in enumerate(parts):
        core, kind = place_of(other_core, change)
        for half in range(2):
            at_col = ((half * 2 + core) * GROUP + kind * CLASS) * H
            low = (part * 2 + half) * CLASS * H
            cols = pl.ds(low, CLASS * H)
            for dev in range(CLASS):
                for row in range(0, H, 16):
                    stage[row : row + 16, low + dev * H : low + (dev + 1) * H] = ref[
                        half * CLASS + dev, row : row + 16, :
                    ].astype(F32)
            copies.append(
                pltpu.make_async_copy(
                    stage.at[:, cols],
                    out_hbm.at[:, pl.ds(pl.multiple_of(at_col, CLASS * H), CLASS * H)],
                    sem.at[len(copies)],
                )
            )
            copies[-1].start()
    return copies


def place_of(other_core, change):
    core, dp = lax.axis_index("core"), lax.axis_index("dp")
    z = jnp.right_shift(dp, 4)
    kind = jnp.bitwise_and(dp + z, 1) * 2 + jnp.bitwise_and(jnp.right_shift(dp, 2) + z, 1)
    return (1 - core if other_core else core), jnp.bitwise_xor(kind, change)


def section():
    return lax.axis_index("zh") * 2 + lax.axis_index("core")


CHANGES = (2, 1, 3)


OWN_PARTS = ((False, 0), (True, 0))
REST = tuple((False, change) for change in CHANGES)
FAR_REST = tuple((True, change) for change in CHANGES)


def place_some(kinds, first, *refs):
    count = len(kinds)
    out_hbm, stage, sems = refs[count + (0 if first else 1) :]
    parts = [(ref,) + kind for ref, kind in zip(refs, kinds)]
    for copy in place_rows(parts, out_hbm, stage, sems):
        copy.wait()


def place_last(*refs):
    blocks, refs = refs[:8], refs[9:]
    out_hbm, *ends = refs[:8]
    stage, sems, small, gb, gi, gh, ge, be, bi, bh, end_sems = refs[8:]
    blocks = [(ref,) + kind for ref, kind in zip(blocks, OWN_PARTS + REST + FAR_REST)]
    copies = place_rows(blocks[6:], out_hbm, stage, sems)
    for ref, other_core, change in blocks:
        core, kind = place_of(other_core, change)
        for at in range(2 * CLASS):
            block = ((at // CLASS) * 2 + core) * GROUP + kind * CLASS + at % CLASS
            row = pl.multiple_of(block * SMALL, SMALL)
            small[pl.ds(row, SMALL), :] = ref[at, H:ROWS, :].astype(F32)
    misc = jnp.zeros((32, H), F32)
    for sect in range(MB):
        base = sect * GROUP * SMALL
        rows = slice(sect * 32, (sect + 1) * 32)
        gb[rows, :] = small[base : base + 32, :]
        for part in range(3):
            cols = slice(part * H, (part + 1) * H)
            row = base + 32 + part * 32
            gi[rows, cols] = small[row : row + 32, :]
            gh[rows, cols] = small[row + 96 : row + 128, :]
        misc = misc + small[base + 224 : base + 256, :]
    ge[...] = misc[0:16]
    be[...] = misc[16:17]
    bi[...] = misc[17:20]
    bh[...] = misc[20:23]
    end_copies = [
        pltpu.make_async_copy(here, there, end_sems.at[at])
        for at, (here, there) in enumerate(zip((gb, gi, gh, ge, be, bi, bh), ends))
    ]
    for copy in end_copies:
        copy.start()
    for copy in copies + end_copies:
        copy.wait()


VMEM_SPEC = pl.BlockSpec(memory_space=pltpu.VMEM)
ANY_SPEC = pl.BlockSpec(memory_space=pl.ANY)
BIG = 60 * 2**20
LOW = 8 * 2**20
shape = jax.ShapeDtypeStruct


def run_layers(operands):
    return pl.pallas_call(
        local_kernel,
        out_shape=(
            shape((GROUP, ROWS, H), BF),
            shape((ATOMS, H), F32),
            shape((ATOMS, H), F32),
            shape((H, NODES), BF),
            shape((PAIRS, H), BF),
        ),
        in_specs=[ANY_SPEC] * 14,
        out_specs=(VMEM_SPEC,) * 5,
        scratch_shapes=[pltpu.VMEM(v.shape, v.dtype) for v in operands]
        + [
            pltpu.VMEM(((NODES + 1) * GAP, H), F32),
            pltpu.VMEM(((NODES + 1) * GAP, H), F32),
            pltpu.VMEM(((H + 1) * GAP, H), F32),
            pltpu.VMEM(((OWN + 1) * GAP, H), F32),
            pltpu.VMEM((MB * PAIRS, H), BF),
            pltpu.VMEM((NODES, H), F32),
            pltpu.VMEM((GROUP * SMALL, H), F32),
            pltpu.VMEM((PAIRS, H), BF),
            pltpu.SemaphoreType.DMA((13,)),
            pltpu.SemaphoreType.DMA,
        ],
        compiler_params=pltpu.CompilerParams(vmem_limit_bytes=BIG),
        name="layers",
    )(*operands)


def neighbours(axis):
    pairs = []
    for zh in range(2):
        for core in range(2):
            for dp in range(GROUP):
                x, y, z = spot_of(dp)
                spot = [x, y, zh * 2 + z]
                spot[axis] = (spot[axis] + (-1 if core else 1)) % 4
                x, y, z = spot
                pairs.append(
                    (
                        z // 2 * 64 + core * GROUP + z % 2 * 16 + y * 4 + x,
                        zh * 64 + core * GROUP + dp,
                    )
                )
    return pairs


def local(
    node_states,
    edge_features,
    edge_source,
    edge_target,
    edge_live,
    w_edge_in,
    b_edge_in,
    w_edge_out,
    b_edge_out,
    w_input,
    w_hidden,
    b_input,
    b_hidden,
    cotangent,
):
    operands = [v.reshape(8, 128) for v in (edge_source, edge_target, edge_live)] + [
        edge_features,
        w_edge_in,
        b_edge_in.reshape(1, H),
        node_states,
        b_edge_out.reshape(H, H),
        w_input,
        w_hidden,
        b_input.reshape(3, H),
        b_hidden.reshape(3, H),
        cotangent,
        w_edge_out,
    ]

    send, final, base, grad_t, pairs = run_layers(operands)
    grad_states = pl.pallas_call(
        states_kernel,
        out_shape=shape((ATOMS, H), F32),
        in_specs=[VMEM_SPEC] * 4,
        out_specs=VMEM_SPEC,
        scratch_shapes=[pltpu.VMEM(((H + 1) * (ATOMS + 1), H), F32), pltpu.VMEM((NODES, H), F32)],
        compiler_params=pltpu.CompilerParams(vmem_limit_bytes=LOW),
        cost_estimate=pl.CostEstimate(
            flops=2 * ATOMS * H * H * H, bytes_accessed=2 * H * H * H, transcendentals=0
        ),
        name="states_back",
    )(base, grad_t, pairs, w_edge_out)
    got = lax.all_to_all(send, "dp", split_axis=0, concat_axis=0)
    got, grad_states = lax.optimization_barrier((got, grad_states))
    piece = pl.pallas_call(
        sum_kernel,
        out_shape=shape((2 * CLASS, ROWS, H), BF),
        in_specs=[VMEM_SPEC],
        out_specs=VMEM_SPEC,
        compiler_params=pltpu.CompilerParams(vmem_limit_bytes=LOW),
        name="sum_parts",
    )(got)
    classes = [
        [zh * 64 + c * GROUP + DP_AT[kind * CLASS + at] for zh in range(2) for at in range(CLASS)]
        for c in range(2)
        for kind in range(4)
    ]
    near = lax.all_to_all(
        piece, ("zh", "core", "dp"), split_axis=0, concat_axis=0, axis_index_groups=classes
    )
    swap = [(0, 1), (1, 0)]
    far = lax.ppermute(near, "core", swap)
    rest = [lax.ppermute(near, ("zh", "core", "dp"), neighbours(axis)) for axis in range(AXES)]

    params = pltpu.CompilerParams(vmem_limit_bytes=LOW)
    cost = pl.CostEstimate(flops=0, bytes_accessed=6 * 2**20, transcendentals=0)

    def stage(parts):
        return [pltpu.VMEM((H, parts * 2 * CLASS * H), F32), pltpu.SemaphoreType.DMA((2 * parts,))]

    whole = shape((H, H * H), F32)

    def place_blocks(kinds, blocks, out, name):
        count = len(kinds)
        first = out is None
        return pl.pallas_call(
            functools.partial(place_some, kinds, first),
            out_shape=whole,
            in_specs=[VMEM_SPEC] * count + ([] if first else [ANY_SPEC]),
            out_specs=ANY_SPEC,
            scratch_shapes=stage(count),
            input_output_aliases={} if first else {count: 0},
            compiler_params=params,
            cost_estimate=cost,
            name=name,
        )(*blocks, *([] if first else [out]))

    out = place_blocks(OWN_PARTS, (near, far), None, "place_own")
    rest[0], out = lax.optimization_barrier((rest[0], out))
    far_rest = [lax.ppermute(rest[0], "core", swap)]
    out = place_blocks(REST[:1], rest[:1], out, "place_x")
    for axis in (1, 2):
        rest[axis], out = lax.optimization_barrier((rest[axis], out))
        far_rest.append(lax.ppermute(rest[axis], "core", swap))
    out = place_blocks(
        REST[1:] + FAR_REST[:1], (rest[1], rest[2], far_rest[0]), out, "place_y_z_far_x"
    )
    ends = [
        shape((H, H), F32),
        shape((H, 3 * H), F32),
        shape((H, 3 * H), F32),
        shape((16, H), F32),
        shape((1, H), F32),
        shape((3, H), F32),
        shape((3, H), F32),
    ]
    grad_w_out, grad_b_out, grad_w_in, grad_w_hid, grad_ein, grad_bein, grad_bin, grad_bhid = (
        pl.pallas_call(
            place_last,
            out_shape=[whole] + ends,
            in_specs=[VMEM_SPEC] * (2 * AXES + 2) + [ANY_SPEC],
            out_specs=[ANY_SPEC] * 8,
            scratch_shapes=stage(2)
            + [pltpu.VMEM((MB * GROUP * SMALL, H), F32)]
            + [pltpu.VMEM(v.shape, v.dtype) for v in ends]
            + [pltpu.SemaphoreType.DMA((7,))],
            input_output_aliases={2 * AXES + 2: 0},
            compiler_params=params,
            cost_estimate=cost,
            name="place_last",
        )(near, far, *rest, *far_rest, out)
    )
    return (
        final,
        grad_states,
        grad_ein,
        grad_bein.reshape(H),
        grad_w_out,
        grad_b_out.reshape(H * H),
        grad_w_in,
        grad_w_hid,
        grad_bin.reshape(3 * H),
        grad_bhid.reshape(3 * H),
    )


def solution(mesh):
    wide = Mesh(mesh.devices.reshape(2, 2, GROUP), ("zh", "core", "dp"))
    split = P(("dp", "zh", "core"), None)
    in_specs = (
        P("dp", None),
        P(None, "dp"),
        P("dp"),
        P("dp"),
        P("dp"),
        P(),
        P(),
        P(),
        P(),
        P(),
        P(),
        P(),
        P(),
        P("dp", None),
    )
    out_specs = (split, split, P(), P(), P(), P(), P(), P(), P(), P())
    return jax.shard_map(local, mesh=wide, in_specs=in_specs, out_specs=out_specs, check_vma=False)
```
